128 devices in a mesh: lat: 4 (over y), patch: 32 (over x, z, core).
Axes of the slice: x: 4, y: 4, z: 4, core: 2. Of those that a mesh axis runs over, the one named last changes fastest.
Arguments:
- coarse: bfloat16 [8192, 64, 128], P(('lat', 'patch')), may hold values from -6 to 6
- slot_owner: int32 [128, 112, 1], replicated, may hold values from 0 to 127; in each aligned block of 112 rows (0 to 111, 112 to 223, ..., all dimensions but the last counted through in order) at most 2 rows name the same one
- slot_block: int32 [128, 112], replicated, may hold values from 0 to 63
- interp: bfloat16 [128, 56], replicated, may hold values from -0.5 to 0.5
- lift: bfloat16 [128, 64], replicated, may hold values from -0.75 to 0.75
- conv_weights: bfloat16 [4, 9, 128, 128], replicated, may hold values from -0.1875 to 0.1875
- gains: float32 [4, 128], replicated, may hold values from 0.1 to 1.9
- fine_noisy: bfloat16 [32, 128, 56, 448], P('patch', None, 'lat'), may hold values from -20 to 20
- out_grad: float32 [32, 128, 56, 448], P('patch', None, 'lat'), may hold values from -6 to 6
Outputs:
- denoised: float32 [32, 128, 56, 448], P('patch', None, 'lat')
- coarse_grad: float32 [8192, 64, 128], P(('lat', 'patch'))
- interp_grad: float32 [128, 56], replicated
- lift_grad: float32 [128, 64], replicated
- conv_grads: float32 [4, 9, 128, 128], replicated
- gain_grads: float32 [4, 128], replicated
The draws below stay inside these ranges and needn't reach their ends.
Inputs may be any that keep to these rules, and one draw needn't show every extreme that they name: `slot_owner`: among the 112 slots of one tile no owner is named more than 2 times, and in every draw some tile names some owner exactly 2 times; every owner is named somewhere.
All inputs are finite; a program needn't handle non-finite values.
Results may differ from the reference program's by a relative error of at most 0.012.
Values may be sent and summed in bfloat16 or wider, within the bound.
No kernel may reach another device: no remote copies, remote signals or barrier semaphores. Data moves between devices by JAX's collectives and lax.ppermute only.
A program may use at most 192 MiB of HBM per device.

```python
import math
import jax
import jax.numpy as jnp
import numpy as np
from jax import lax

CH = 128
CC = 64
GROUPS = 32
BLK_CELLS = 128
KMAX = 112
PC = 448
FR = 14
BLK_DEV = 64
CAP = 2
REGION = 56
NR = 56
PATCHES = 32
BLOCKS = 8192
N_LAT = 4
DEVICES = 128


def draw_fine_noisy(key, part):
    key = jax.random.fold_in(key, 11)
    base_key, rough_key = jax.random.split(key)
    col_place = jnp.arange(PC, dtype=jnp.float32) / (PC - 1)
    row_place = jnp.arange(NR, dtype=jnp.float32) / (NR - 1)
    rough = jax.random.uniform(rough_key, (PATCHES, CH, NR, PC), jnp.float32, 0.5, 1.5)
    base = jnp.clip(jax.random.normal(base_key, (PATCHES, CH, NR, PC), jnp.float32), -4.0, 4.0)
    ramp = jnp.exp(1.3 * (row_place - 0.5))[:, None] * jnp.exp(0.5 * (col_place - 0.5))[None, :]
    return (base * rough * ramp[None, None, :, :]).astype(jnp.bfloat16)


def plant(entries, stream_key, smallest, largest):
    longest = entries.shape.index(max(entries.shape))
    spots = []
    for shift in (0, 1):
        where = [jax.random.randint(jax.random.fold_in(stream_key, axis), (), 0, length) for axis, length in enumerate(entries.shape)]
        where[longest] = (where[longest] + shift) % entries.shape[longest]
        spots.append(tuple(where))
    return entries.at[spots[0]].set(smallest).at[spots[1]].set(largest)


def levels(own_key, extent, shards, least, high):
    loudness, own = 1.0, jax.random.fold_in(own_key, 6)
    for dim, shards_of in shards:
        heights = jnp.exp(jax.random.uniform(jax.random.fold_in(own, dim), (shards_of,), jnp.float32, least / len(shards), high / len(shards)))
        loudness = loudness * jnp.repeat(heights, extent[dim] // shards_of).reshape([-1 if axis == dim else 1 for axis in range(len(extent))])
    return loudness


def assign_block(rng, own, number, rows, count, top, limit, slope):
    sequence = jax.random.permutation(rng, count)
    packed, common = load_shares(count, rows * top, limit, slope, True), load_shares(count, rows * top, limit, slope, False)
    places = jnp.arange(count)

    def named(sizes, turn):
        used = int((sizes > 0).sum())
        fixed = max(1, used // 4)
        moved = fixed + (places - fixed + turn * (used - fixed)) % max(1, count - fixed)
        return jnp.zeros((count,), jnp.int32).at[sequence[jnp.where(places < fixed, places, moved)]].set(jnp.asarray(sizes, jnp.int32))

    sizes = jnp.where(number % 4 == 0, named(packed, number // 4), named(common, number - number // 4 - 1))
    mixed = jax.random.permutation(jax.random.fold_in(own, 3), count)
    giver, sink = mixed[0:count // 2 * 2:2], mixed[1:count // 2 * 2:2]
    slack = jnp.minimum(sizes[giver] - 1, limit - sizes[sink]) // 2
    slack = jnp.where((giver == sequence[0]) | (sink == sequence[0]) | (sizes[sink] == 0), 0, jnp.maximum(slack, 0))
    moved = jax.random.randint(jax.random.fold_in(own, 4), (count // 2,), 0, 1 << 20) % (slack + 1)
    sizes = sizes.at[giver].add(-moved).at[sink].add(moved)
    labels = jnp.searchsorted(jnp.cumsum(sizes), jnp.arange(rows * top), side="right").astype(jnp.int32)
    table = labels.reshape(top, rows).T
    table = table[jax.random.permutation(jax.random.fold_in(own, 1), rows)]
    turn = jax.random.randint(jax.random.fold_in(own, 2), (rows, 1), 0, top)
    return jnp.take_along_axis(table, (jnp.arange(top)[None, :] + turn) % top, axis=1)


def load_shares(amount, total, limit, lean, full):
    portions = [(1 << 20) // math.isqrt(rank ** lean) + 1 for rank in range(1, amount + 1)]
    largest = limit if full else min(limit, max(-(-total // amount), total * portions[0] // sum(portions)))
    least = 1 if total - largest >= amount - 1 else 0
    given, surplus = [largest] + [least] * (amount - 1), total - largest - least * (amount - 1)
    while surplus > 0:
        free = [i for i in range(1, amount) if given[i] < largest] or [i for i in range(1, amount) if given[i] < limit]
        whole, budget = sum([portions[i] for i in free]), surplus
        for i in free:
            more = min(limit - given[i], max(1, budget * portions[i] // whole), surplus)
            given[i] = given[i] + more
            surplus = surplus - more
    return np.array(given)


def centred(stream_key, dims, deviation, limit, cuts=(), kind=jnp.bfloat16):
    drawn = deviation * jax.random.normal(stream_key, dims, jnp.float32)
    if cuts:
        drawn = drawn * levels(stream_key, dims, cuts, -0.22, 0.18)
    return jnp.clip(drawn, -limit, limit).astype(kind)


def setup_inputs(seed: int = 0) -> dict:
    streams_of = jax.random.split(jax.random.key(seed), 10)
    coarse = centred(streams_of[0], (BLOCKS, CC, BLK_CELLS), 1.0, 6.0, ((0, 128),))
    slot_owner_keys = jax.random.split(jax.random.fold_in(streams_of[1], 1), DEVICES * KMAX // KMAX)
    slot_owner_turns = jax.random.permutation(jax.random.fold_in(streams_of[1], 3), DEVICES * KMAX // KMAX)
    slot_owner = jax.vmap(lambda own, number: assign_block(jax.random.fold_in(streams_of[1], 2), own, number, KMAX, DEVICES, 1, CAP, 2))(slot_owner_keys, slot_owner_turns).reshape((DEVICES, KMAX, 1))
    slot_block = plant(jax.random.randint(streams_of[2], (DEVICES, KMAX), 0, BLK_DEV), jax.random.fold_in(streams_of[2], 1), 0, BLK_DEV - 1).astype(jnp.int32)
    interp = centred(streams_of[3], (BLK_CELLS, REGION), BLK_CELLS ** -0.5, 0.5)
    lift = centred(streams_of[4], (CH, CC), CC ** -0.5, 0.75)
    conv_weights = centred(streams_of[5], (4, 9, CH, CH), (9 * CH) ** -0.5, 0.1875)
    gains = jnp.clip(1.0 + 0.18 * jax.random.normal(streams_of[6], (4, CH), jnp.float32), 0.1, 1.9)
    fine_noisy = draw_fine_noisy(jax.random.fold_in(streams_of[9], 71), 0)
    out_grad = centred(streams_of[8], (PATCHES, CH, NR, PC), 1.0, 6.0, ((0, 32), (2, 4)), jnp.float32)
    return {"coarse": coarse, "slot_owner": slot_owner, "slot_block": slot_block, "interp": interp, "lift": lift, "conv_weights": conv_weights, "gains": gains, "fine_noisy": fine_noisy, "out_grad": out_grad}


EPSILON = 1e-05

def conv_apply(padded, weights):
    out_rows = padded.shape[1] - 2
    out_cols = padded.shape[2] - 2
    summed = jnp.zeros((weights.shape[1], out_rows, out_cols), jnp.float32)
    for offset in range(9):
        row_shift = offset // 3
        col_shift = offset % 3
        window = padded[:, row_shift:row_shift + out_rows, col_shift:col_shift + out_cols]
        summed = summed + jnp.einsum('oc,crw->orw', weights[offset].astype(jnp.float32), window.astype(jnp.float32))
    return summed

def conv_transpose(padded_grad, weights):
    out_rows = padded_grad.shape[1] - 2
    out_cols = padded_grad.shape[2] - 2
    summed = jnp.zeros((weights.shape[2], out_rows, out_cols), jnp.float32)
    for offset in range(9):
        row_shift = 2 - offset // 3
        col_shift = 2 - offset % 3
        window = padded_grad[:, row_shift:row_shift + out_rows, col_shift:col_shift + out_cols]
        summed = summed + jnp.einsum('oc,orw->crw', weights[offset].astype(jnp.float32), window.astype(jnp.float32))
    return summed

def kernel_grad(gradient, padded):
    out_rows = gradient.shape[1]
    out_cols = gradient.shape[2]
    terms = []
    for offset in range(9):
        row_shift = offset // 3
        col_shift = offset % 3
        window = padded[:, row_shift:row_shift + out_rows, col_shift:col_shift + out_cols]
        terms.append(jnp.einsum('orw,crw->oc', gradient.astype(jnp.float32), window.astype(jnp.float32)))
    return jnp.stack(terms)

def zero_border(values):
    return jnp.pad(values, ((0, 0), (1, 1), (1, 1)))

def norm_act(values, gain_row, cell_count):
    grouped = values.reshape(GROUPS, -1)
    group_mean = lax.optimization_barrier(jnp.sum(grouped, 1)) / cell_count
    inv_spread = lax.rsqrt(lax.optimization_barrier(jnp.sum(grouped * grouped, 1)) / cell_count - group_mean * group_mean + EPSILON)
    per_group = values.shape[0] // GROUPS
    mean_col = jnp.repeat(group_mean, per_group)[:, None, None]
    spread_col = jnp.repeat(inv_spread, per_group)[:, None, None]
    normed = (values - mean_col) * spread_col
    scaled = normed * gain_row[:, None, None]
    return (normed, spread_col, scaled, (scaled * jax.nn.sigmoid(scaled)).astype(jnp.bfloat16))

def norm_back(grad_act, normed, spread_col, scaled, gain_row, cell_count):
    sigmoid_y = jax.nn.sigmoid(scaled)
    grad_scaled = grad_act * sigmoid_y * (1.0 + scaled * (1.0 - sigmoid_y))
    gain_term = lax.optimization_barrier(jnp.sum(grad_scaled * normed, axis=(1, 2)))
    grad_normed = grad_scaled * gain_row[:, None, None]
    first_sum = lax.optimization_barrier(jnp.sum(grad_normed.reshape(GROUPS, -1), 1))
    second_sum = lax.optimization_barrier(jnp.sum((grad_normed * normed).reshape(GROUPS, -1), 1))
    per_group = grad_normed.shape[0] // GROUPS
    first_col = jnp.repeat(first_sum / cell_count, per_group)[:, None, None]
    second_col = jnp.repeat(second_sum / cell_count, per_group)[:, None, None]
    return (spread_col * (grad_normed - first_col - normed * second_col), gain_term)

def block_forward(values, conv_weights, gains, first_index, cell_count):
    normed_a, spread_a, scaled_a, act_a = norm_act(values, gains[first_index], cell_count)
    padded_a = zero_border(act_a)
    conv_a = conv_apply(padded_a, conv_weights[first_index])
    normed_b, spread_b, scaled_b, act_b = norm_act(conv_a, gains[first_index + 1], cell_count)
    padded_b = zero_border(act_b)
    conv_b = conv_apply(padded_b, conv_weights[first_index + 1])
    saved = (normed_a, spread_a, scaled_a, padded_a, normed_b, spread_b, scaled_b, padded_b)
    return (values + conv_b, saved)

def block_back(grad_out, saved, conv_weights, gains, first_index, cell_count):
    normed_a, spread_a, scaled_a, padded_a, normed_b, spread_b, scaled_b, padded_b = saved
    grad_b = grad_out.astype(jnp.bfloat16)
    kernel_b = kernel_grad(grad_b, padded_b)
    grad_act_b = conv_transpose(zero_border(grad_b), conv_weights[first_index + 1])
    grad_conv, gain_b = norm_back(grad_act_b, normed_b, spread_b, scaled_b, gains[first_index + 1], cell_count)
    grad_a = grad_conv.astype(jnp.bfloat16)
    kernel_a = kernel_grad(grad_a, padded_a)
    grad_act_a = conv_transpose(zero_border(grad_a), conv_weights[first_index])
    grad_input, gain_a = norm_back(grad_act_a, normed_a, spread_a, scaled_a, gains[first_index], cell_count)
    return (grad_out + grad_input, (kernel_a, kernel_b), (gain_a, gain_b))

def pool_mean(values):
    chans, height, breadth = values.shape
    return values.reshape(chans, height // 2, 2, breadth // 2, 2).mean(axis=(2, 4))

def pool_sum(values):
    chans, height, breadth = values.shape
    return values.reshape(chans, height // 2, 2, breadth // 2, 2).sum(axis=(2, 4))

def widen(values):
    return jnp.repeat(jnp.repeat(values, 2, axis=1), 2, axis=2)

def reference(coarse, slot_owner, slot_block, interp, lift, conv_weights, gains, fine_noisy, out_grad):
    owners = slot_owner[:, :, 0]
    global_ids = (owners * BLK_DEV + slot_block).reshape(-1).astype(jnp.int32)
    chosen = jnp.take(coarse, global_ids, axis=0)
    pieces = jnp.einsum('kcb,bq->kcq', chosen.astype(jnp.float32), interp.astype(jnp.float32)).astype(jnp.bfloat16)
    per_row = KMAX // FR
    cond = pieces.reshape(N_LAT, PATCHES, FR, per_row, CC, REGION).transpose(1, 4, 0, 2, 3, 5).reshape(PATCHES, CC, NR, PC)
    full_count = CH // GROUPS * NR * PC
    half_count = full_count // 4

    def one_patch(inputs):
        noisy, cond_patch, grad_patch = inputs
        hidden = noisy.astype(jnp.float32) + jnp.einsum('oc,crw->orw', lift.astype(jnp.float32), cond_patch.astype(jnp.float32))
        level_one, saved_one = block_forward(hidden, conv_weights, gains, 0, full_count)
        pooled = pool_mean(level_one)
        level_two, saved_two = block_forward(pooled, conv_weights, gains, 2, half_count)
        denoised_patch = level_one + widen(level_two)
        grad_pooled, kernels_two, gains_two = block_back(pool_sum(grad_patch), saved_two, conv_weights, gains, 2, half_count)
        grad_level = grad_patch + 0.25 * widen(grad_pooled)
        grad_hidden, kernels_one, gains_one = block_back(grad_level, saved_one, conv_weights, gains, 0, full_count)
        hidden_grad = grad_hidden.astype(jnp.bfloat16)
        lift_term = jnp.einsum('orw,crw->oc', hidden_grad.astype(jnp.float32), cond_patch.astype(jnp.float32))
        grad_cond = jnp.einsum('oc,orw->crw', lift.astype(jnp.float32), hidden_grad.astype(jnp.float32)).astype(jnp.bfloat16)
        conv_terms = jnp.stack([kernels_one[0], kernels_one[1], kernels_two[0], kernels_two[1]])
        gain_terms = jnp.stack([gains_one[0], gains_one[1], gains_two[0], gains_two[1]])
        return (denoised_patch, grad_cond, lift_term, conv_terms, gain_terms)
    denoised, grad_cond, lift_terms, conv_terms, gain_terms = lax.map(one_patch, (fine_noisy, cond, out_grad))
    grad_pieces = grad_cond.reshape(PATCHES, CC, N_LAT, FR, per_row, REGION).transpose(2, 0, 3, 4, 1, 5).reshape(DEVICES * KMAX, CC, REGION)
    interp_grad = jnp.einsum('kcb,kcq->bq', chosen.astype(jnp.float32), grad_pieces.astype(jnp.float32))
    summed = jax.ops.segment_sum(grad_pieces.astype(jnp.float32).reshape(DEVICES * KMAX, CC * REGION), global_ids, num_segments=BLOCKS)
    coarse_grad = jnp.einsum('ncq,bq->ncb', summed.reshape(BLOCKS, CC, REGION), interp.astype(jnp.float32), precision=lax.Precision.HIGHEST)
    grad_scale = 1.0 / math.sqrt(PATCHES * NR * PC)
    lift_grad = lax.optimization_barrier(jnp.sum(lift_terms, 0)) * grad_scale
    conv_grads = lax.optimization_barrier(jnp.sum(conv_terms, 0)) * grad_scale
    gain_grads = lax.optimization_barrier(jnp.sum(gain_terms, 0)) * grad_scale
    return (denoised, coarse_grad, interp_grad * grad_scale, lift_grad, conv_grads, gain_grads)
```

```python
import math

import jax
import jax.numpy as jnp
from jax import lax
from jax.experimental import pallas as pl
from jax.experimental.pallas import tpu as pltpu
from jax.sharding import PartitionSpec as P

GROUPS = 32
EPSILON = 1e-05
BF = jnp.bfloat16
F32 = jnp.float32
BOTH = ("lat", "patch")
VMEM_BYTES = 56 * 1024 * 1024
STAT_ROWS = 16
SPAN = 4


def call(kernel, outs, scratch, scalars, args, name):
    smem = pl.BlockSpec(memory_space=pltpu.SMEM)
    vmem = pl.BlockSpec(memory_space=pltpu.VMEM)
    return pl.pallas_call(
        kernel,
        out_shape=[jax.ShapeDtypeStruct(s, d) for s, d in outs],
        in_specs=[smem] * len(scalars) + [vmem] * len(args),
        out_specs=[vmem] * len(outs),
        scratch_shapes=[pltpu.VMEM(s, d) for s, d in scratch],
        compiler_params=pltpu.CompilerParams(vmem_limit_bytes=VMEM_BYTES),
        name=name,
    )(*scalars, *args)


def fold8(x):
    return jnp.sum(x.reshape(x.shape[0] // 8, 8, x.shape[1]), axis=0)


def group_sum(v):
    lane = lax.broadcasted_iota(jnp.int32, v.shape, 1)
    n = v.shape[1]
    v = v + jnp.where(lane % 2 == 0, pltpu.roll(v, n - 1, 1), pltpu.roll(v, 1, 1))
    return v + jnp.where(lane % 4 < 2, pltpu.roll(v, n - 2, 1), pltpu.roll(v, 2, 1))


def split3(v):
    hi = v.astype(BF).astype(F32)
    mid = (v - hi).astype(BF).astype(F32)
    return hi, mid, v - hi - mid


def stat_block(first, second):
    row = lax.broadcasted_iota(jnp.int32, (STAT_ROWS, first.shape[1]), 0)
    block = jnp.zeros(row.shape, F32)
    for i, part in enumerate(split3(first) + split3(second)):
        block = jnp.where(row == i, part, block)
    return block.astype(BF)


def stat_pair(block):
    f = block.astype(F32)
    return f[0:1] + f[1:2] + f[2:3], f[3:4] + f[4:5] + f[5:6]


def total_pair(blocks):
    pairs = [stat_pair(b) for b in blocks]
    return sum(p[0] for p in pairs), sum(p[1] for p in pairs)


def put_row(dst, index, value):
    width, chans = value.shape
    cell = lax.broadcasted_iota(jnp.int32, value.shape, 0)
    left = jnp.where(cell == 0, 0.0, pltpu.roll(value, 1, 0))
    right = jnp.where(cell == width - 1, 0.0, pltpu.roll(value, width - 1, 0))
    dst[index, :, 0:chans] = left.astype(BF)
    dst[index, :, chans : 2 * chans] = value.astype(BF)
    dst[index, :, 2 * chans : 3 * chans] = right.astype(BF)


def conv_pairs(rows3, weights, height, emit, carry):
    chans = weights.shape[1] // 2
    table = weights[...]

    def step(j, carry):
        lhs = jnp.concatenate([rows3[2 * j + s] for s in range(SPAN)], axis=1)
        out = jnp.dot(lhs, table, preferred_element_type=F32)
        carry = emit(2 * j, out[:, :chans], carry)
        return emit(2 * j + 1, out[:, chans:], carry)

    carry = lax.fori_loop(0, height // 2, step, carry)
    if height % 2:
        lhs = jnp.concatenate([rows3[height - 1 + s] for s in range(3)], axis=1)
        out = jnp.dot(lhs, weights[0 : lhs.shape[1], 0:chans], preferred_element_type=F32)
        carry = emit(height - 1, out, carry)
    return carry


def sigm(y):
    return 0.5 * jnp.tanh(0.5 * y) + 0.5


def act_of(x, vec):
    y = x * vec[2:3] + vec[3:4]
    return y * sigm(y)


def act_grad(grad, x, vec):
    y = x * vec[2:3] + vec[3:4]
    sg = sigm(y)
    return grad * sg * (1.0 + y * (1.0 - sg)), (x - vec[0:1]) * vec[1:2]


def norm_vectors(up, down, opposite, own, gain, width, height, count):
    up_stats, down_stats = up[width : width + STAT_ROWS], down[width : width + STAT_ROWS]
    first, second = total_pair([own[...], up_stats, down_stats, opposite[...]])
    first = group_sum(jnp.broadcast_to(first, (8, first.shape[1])))
    second = group_sum(jnp.broadcast_to(second, first.shape))
    mean = first / count
    inv = lax.rsqrt(second / count - mean * mean + EPSILON)
    gain8 = jnp.broadcast_to(gain[...], mean.shape)
    scale = inv * gain8
    row = lax.broadcasted_iota(jnp.int32, mean.shape, 0)
    local = 1.0 / (width * height)
    up_mean = stat_pair(up_stats)[0] * local
    down_mean = stat_pair(down_stats)[0] * local
    vec = jnp.where(row == 0, mean, inv)
    for i, part in enumerate([scale, -mean * scale, gain8, up_mean, down_mean]):
        vec = jnp.where(row == i + 2, part, vec)
    return vec


def back_vectors(up, down, opposite, own, vec, width, count):
    stats = [own[...], opposite[...]]
    stats += [up[width : width + STAT_ROWS], down[width : width + STAT_ROWS]]
    first, second = total_pair(stats)
    first = group_sum(jnp.broadcast_to(first * vec[4:5], (8, first.shape[1])))
    second = group_sum(jnp.broadcast_to(second * vec[4:5], first.shape))
    return first[0:1] / count, second[0:1] / count


def norm_grad(grad, x, vec, first, second):
    gs, normed = act_grad(grad, x, vec)
    return vec[1:2] * (gs * vec[4:5] - first - normed * second)


def send_raw(to_up, to_down, block, top, bottom, sums, width, height):
    first = jnp.sum(sums[0], axis=0, keepdims=True)
    second = jnp.sum(sums[1], axis=0, keepdims=True)
    stats = stat_block(first, second)
    mean = stat_pair(stats)[0] * (1.0 / (width * height))
    to_up[0:width] = (top - mean).astype(BF)
    to_down[0:width] = (bottom - mean).astype(BF)
    to_up[width : width + STAT_ROWS] = stats
    to_down[width : width + STAT_ROWS] = stats
    block[...] = stats


def send_grad(to_up, to_down, block, top, bottom, sums, width):
    stats = stat_block(
        jnp.sum(sums[0], axis=0, keepdims=True), jnp.sum(sums[1], axis=0, keepdims=True)
    )
    to_up[0:width] = top.astype(BF)
    to_down[0:width] = bottom.astype(BF)
    to_up[width : width + STAT_ROWS] = stats
    to_down[width : width + STAT_ROWS] = stats
    block[...] = stats


def halo_raw(up, down, vec, width):
    above = up[0:width].astype(F32) + vec[5:6]
    below = down[0:width].astype(F32) + vec[6:7]
    return above, below


def zeros2(chans):
    return jnp.zeros((8, chans), F32), jnp.zeros((8, chans), F32)


def add_sums(sums, x):
    return sums[0] + fold8(x), sums[1] + fold8(x * x)


def route_kernel(me_ref, owners_ref, blocks_ref, out_ref):
    me = me_ref[0]
    slots, tiles = owners_ref.shape
    owners = owners_ref[...]
    mine = owners == me
    k = lax.broadcasted_iota(jnp.int32, (slots, slots), 0)
    j = lax.broadcasted_iota(jnp.int32, (slots, slots), 1)
    earlier = jnp.where(j < k, 1.0, 0.0).astype(BF)
    flags = jnp.where(mine, 1.0, 0.0)
    before = jnp.dot(earlier, flags.astype(BF), preferred_element_type=F32)
    blocks = blocks_ref[...].astype(F32)
    first = jnp.sum(jnp.where(mine & (before < 0.5), blocks, 0.0), axis=0, keepdims=True)
    second = jnp.sum(jnp.where(mine & (before > 0.5), blocks, 0.0), axis=0, keepdims=True)
    count = jnp.sum(flags, axis=0, keepdims=True)
    lane = lax.broadcasted_iota(jnp.int32, (slots, tiles), 1)
    slot = lax.broadcasted_iota(jnp.int32, (slots, tiles), 0)
    column = jnp.sum(jnp.where(lane == me, owners, 0).astype(F32), axis=1, keepdims=True)
    as_row = jnp.sum(jnp.where(lane == slot, column, 0.0), axis=0, keepdims=True)
    same = (column == as_row) & (slot < lane) & (lane < slots)
    position = jnp.sum(jnp.where(same, 1.0, 0.0), axis=0, keepdims=True)
    row = lax.broadcasted_iota(jnp.int32, (8, tiles), 0)
    out = jnp.where(row == 0, first, 0.0)
    for i, part in enumerate([second, count, as_row, position]):
        out = jnp.where(row == i + 1, part, out)
    out_ref[...] = out.astype(jnp.int32)


def send_kernel(route_ref, coarse_ref, interp_ref, out_ref):
    table = interp_ref[...]

    def step(d, _):
        pair = jnp.concatenate([coarse_ref[route_ref[0, d]], coarse_ref[route_ref[1, d]]], axis=0)
        piece = lax.dot_general(table, pair, (((1,), (1,)), ((), ())), preferred_element_type=F32)
        out_ref[d] = piece.astype(BF)
        return 0

    lax.fori_loop(0, out_ref.shape[0], step, 0, unroll=8)


def pool_kernel(grad_ref, pooled_ref, up_ref, down_ref, rows_ref):
    height, width, chans = grad_ref.shape
    half = width // 2

    def step(r, _):
        rows_ref[...] = grad_ref[2 * r] + grad_ref[2 * r + 1]
        pooled_ref[r] = rows_ref[pl.ds(0, half, stride=2)] + rows_ref[pl.ds(1, half, stride=2)]
        return 0

    lax.fori_loop(0, height // 2, step, 0)
    up_ref[0:width] = grad_ref[0].astype(BF)
    up_ref[width : width + half] = pooled_ref[0].astype(BF)
    down_ref[0:width] = grad_ref[height - 1].astype(BF)
    down_ref[width : width + half] = pooled_ref[height // 2 - 1].astype(BF)


def head_back_kernel(pooled_ref, up_ref, down_ref, edge_ref, weights_ref, grad_ref, rows3):
    height, width, chans = pooled_ref.shape
    start = up_ref.shape[0] - width
    put_row(rows3, 0, up_ref[start:].astype(F32) * edge_ref[0:1])
    put_row(rows3, height + 1, down_ref[start:].astype(F32) * edge_ref[1:2])

    def fill(r, _):
        put_row(rows3, r + 1, pooled_ref[r])
        return 0

    lax.fori_loop(0, height, fill, 0)

    def emit(r, value, carry):
        grad_ref[r] = value
        return carry

    conv_pairs(rows3, weights_ref, height, emit, 0)


def hidden_kernel(route_ref, arrived_ref, noisy_ref, lift_ref, hid_ref, cond_ref, up_ref, down_ref,
                  block_ref, line_ref):
    height, width, chans = noisy_ref.shape
    region = arrived_ref.shape[1]
    per_row = width // region
    upper = lax.broadcasted_iota(jnp.int32, (region, chans), 1) >= chans // 2
    table = lift_ref[...]

    def step(r, sums):
        for i in range(per_row):
            k = r * per_row + i
            piece = arrived_ref[route_ref[3, k]].astype(F32)
            keep = upper == (route_ref[4, k] > 0)
            line_ref[i * region : (i + 1) * region] = jnp.where(keep, piece, 0.0)
        cond = line_ref[...].astype(BF)
        cond_ref[r] = cond
        hidden = noisy_ref[r].astype(F32) + jnp.dot(cond, table, preferred_element_type=F32)
        hid_ref[r] = hidden
        return add_sums(sums, hidden)

    sums = lax.fori_loop(0, height, step, zeros2(chans))
    send_raw(up_ref, down_ref, block_ref, hid_ref[0], hid_ref[height - 1], sums, width, height)


def norm_rows(x_ref, vec, up_ref, down_ref, edge_ref, rows3, act_ref):
    height, width, chans = x_ref.shape
    above, below = halo_raw(up_ref, down_ref, vec, width)
    above = act_of(above, vec) * edge_ref[0:1]
    below = act_of(below, vec) * edge_ref[1:2]
    put_row(rows3, 0, above)
    put_row(rows3, height + 1, below)
    act_ref[0] = above.astype(BF)
    act_ref[height + 1] = below.astype(BF)

    def fill(r, _):
        value = act_of(x_ref[r], vec)
        put_row(rows3, r + 1, value)
        act_ref[r + 1] = value.astype(BF)
        return 0

    lax.fori_loop(0, height, fill, 0)


def make_first(count):
    def kernel(x_ref, up_ref, down_ref, opp_ref, own_ref, edge_ref, gain_ref, weights_ref,
               y_ref, act_ref, vec_ref, to_up, to_down, block_ref, rows3):
        height, width, chans = x_ref.shape
        vec = norm_vectors(up_ref, down_ref, opp_ref, own_ref, gain_ref, width, height, count)
        vec_ref[...] = vec
        norm_rows(x_ref, vec, up_ref, down_ref, edge_ref, rows3, act_ref)

        def emit(r, value, sums):
            y_ref[r] = value
            return add_sums(sums, value)

        sums = conv_pairs(rows3, weights_ref, height, emit, zeros2(chans))
        send_raw(to_up, to_down, block_ref, y_ref[0], y_ref[height - 1], sums, width, height)

    return kernel


def make_second(count):
    def kernel(y_ref, up_ref, down_ref, opp_ref, own_ref, edge_ref, gain_ref, weights_ref, hid_ref,
               level_ref, pooled_ref, act_ref, vec_ref, to_up, to_down, block_ref, rows3, line_ref):
        height, width, chans = y_ref.shape
        half = width // 2
        vec = norm_vectors(up_ref, down_ref, opp_ref, own_ref, gain_ref, width, height, count)
        vec_ref[...] = vec
        norm_rows(y_ref, vec, up_ref, down_ref, edge_ref, rows3, act_ref)
        table = weights_ref[...]

        def step(j, sums):
            lhs = jnp.concatenate([rows3[2 * j + s] for s in range(SPAN)], axis=1)
            out = jnp.dot(lhs, table, preferred_element_type=F32)
            one = hid_ref[2 * j] + out[:, :chans]
            two = hid_ref[2 * j + 1] + out[:, chans:]
            level_ref[2 * j] = one
            level_ref[2 * j + 1] = two
            line_ref[...] = one + two
            pooled = 0.25 * (line_ref[pl.ds(0, half, stride=2)] + line_ref[pl.ds(1, half, stride=2)])
            pooled_ref[j] = pooled
            return add_sums(sums, pooled)

        sums = lax.fori_loop(0, height // 2, step, zeros2(chans))
        last = height // 2 - 1
        send_raw(to_up, to_down, block_ref, pooled_ref[0], pooled_ref[last], sums, half, height // 2)

    return kernel


def make_turn(count):
    def kernel(y_ref, up_ref, down_ref, opp_ref, own_ref, edge_ref, gain_ref, grad_ref,
               act_ref, vec_ref, to_up, to_down, block_ref):
        height, width, chans = y_ref.shape
        vec = norm_vectors(up_ref, down_ref, opp_ref, own_ref, gain_ref, width, height, count)
        vec_ref[...] = vec
        above, below = halo_raw(up_ref, down_ref, vec, width)
        act_ref[0] = (act_of(above, vec) * edge_ref[0:1]).astype(BF)
        act_ref[height + 1] = (act_of(below, vec) * edge_ref[1:2]).astype(BF)

        def fill(r, sums):
            x = y_ref[r]
            y = x * vec[2:3] + vec[3:4]
            sg = sigm(y)
            act_ref[r + 1] = (y * sg).astype(BF)
            gs = grad_ref[r] * sg * (1.0 + y * (1.0 - sg))
            return sums[0] + fold8(gs), sums[1] + fold8(gs * (x - vec[0:1]) * vec[1:2])

        sums = lax.fori_loop(0, height, fill, zeros2(chans))
        send_grad(to_up, to_down, block_ref, grad_ref[0], grad_ref[height - 1], sums, width)

    return kernel


def tail_kernel(act_ref, weights_ref, pooled_ref, level_ref, out_ref, rows3, line_ref):
    height, width, chans = pooled_ref.shape

    def fill(r, _):
        put_row(rows3, r, act_ref[r].astype(F32))
        return 0

    lax.fori_loop(0, height + 2, fill, 0)

    def emit(r, value, carry):
        two = pooled_ref[r] + value
        line_ref[pl.ds(0, width, stride=2)] = two
        line_ref[pl.ds(1, width, stride=2)] = two
        wide = line_ref[...]
        out_ref[2 * r] = level_ref[2 * r] + wide
        out_ref[2 * r + 1] = level_ref[2 * r + 1] + wide
        return carry

    conv_pairs(rows3, weights_ref, height, emit, 0)


def back_conv(rows3, weights_ref, x_ref, vec, grad_ref, to_up, to_down, block_ref):
    height, width, chans = x_ref.shape

    def emit(r, value, sums):
        grad_ref[r] = value
        gs, normed = act_grad(value, x_ref[r], vec)
        return sums[0] + fold8(gs), sums[1] + fold8(gs * normed)

    sums = conv_pairs(rows3, weights_ref, height, emit, zeros2(chans))
    send_grad(to_up, to_down, block_ref, grad_ref[0], grad_ref[height - 1], sums, width)


def make_back_mid(count):
    def kernel(ga_ref, y_ref, yup_ref, ydown_ref, vec_ref, gup_ref, gdown_ref, opp_ref, own_ref,
               edge_ref, weights_ref, x_ref, xvec_ref,
               g_ref, out_ref, to_up, to_down, block_ref, rows3):
        height, width, chans = y_ref.shape
        vec = vec_ref[...]
        first, second = back_vectors(gup_ref, gdown_ref, opp_ref, own_ref, vec, width, count)
        above, below = halo_raw(yup_ref, ydown_ref, vec, width)
        g_above = norm_grad(gup_ref[0:width].astype(F32), above, vec, first, second)
        g_below = norm_grad(gdown_ref[0:width].astype(F32), below, vec, first, second)
        put_row(rows3, 0, g_above * edge_ref[0:1])
        put_row(rows3, height + 1, g_below * edge_ref[1:2])

        def fill(r, _):
            value = norm_grad(ga_ref[r], y_ref[r], vec, first, second)
            put_row(rows3, r + 1, value)
            g_ref[r] = value.astype(BF)
            return 0

        lax.fori_loop(0, height, fill, 0)
        back_conv(rows3, weights_ref, x_ref, xvec_ref[...], out_ref, to_up, to_down, block_ref)

    return kernel


def make_back_join(count):
    def kernel(ga_ref, p_ref, pup_ref, pdown_ref, pvec_ref, gup_ref, gdown_ref, opp_ref, own_ref,
               edge_ref, pg_ref, og_ref, oup_ref, odown_ref, weights_ref, x_ref, xvec_ref,
               level_ref, g_ref, out_ref, to_up, to_down, block_ref, rows3, line_ref):
        half_height, half, chans = p_ref.shape
        height, width, _ = og_ref.shape
        vec = pvec_ref[...]
        first, second = back_vectors(gup_ref, gdown_ref, opp_ref, own_ref, vec, half, count)

        def widened(value):
            line_ref[pl.ds(0, half, stride=2)] = value
            line_ref[pl.ds(1, half, stride=2)] = value
            return 0.25 * line_ref[...]

        above, below = halo_raw(pup_ref, pdown_ref, vec, half)
        g_above = norm_grad(gup_ref[0:half].astype(F32), above, vec, first, second)
        g_below = norm_grad(gdown_ref[0:half].astype(F32), below, vec, first, second)
        wide = widened(g_above + oup_ref[width : width + half].astype(F32))
        put_row(rows3, 0, (oup_ref[0:width].astype(F32) + wide) * edge_ref[0:1])
        wide = widened(g_below + odown_ref[width : width + half].astype(F32))
        put_row(rows3, height + 1, (odown_ref[0:width].astype(F32) + wide) * edge_ref[1:2])

        def fill(r, _):
            value = pg_ref[r] + norm_grad(ga_ref[r], p_ref[r], vec, first, second)
            wide = widened(value)
            for i in range(2):
                grad = og_ref[2 * r + i] + wide
                level_ref[2 * r + i] = grad
                put_row(rows3, 2 * r + i + 1, grad)
                g_ref[2 * r + i] = grad.astype(BF)
            return 0

        lax.fori_loop(0, half_height, fill, 0)
        back_conv(rows3, weights_ref, x_ref, xvec_ref[...], out_ref, to_up, to_down, block_ref)

    return kernel


def kernel_grad_kernel(g_ref, act_ref, out_ref, rows3, acc_ref):
    height, width, chans = g_ref.shape

    def fill(r, _):
        put_row(rows3, r, act_ref[r].astype(F32))
        return 0

    lax.fori_loop(0, height + 2, fill, 0)
    acc_ref[...] = jnp.zeros(acc_ref.shape, F32)

    def step(r, _):
        rhs = jnp.concatenate([rows3[r + s] for s in range(3)], axis=1)
        acc_ref[...] += lax.dot_general(
            g_ref[r], rhs, (((0,), (0,)), ((), ())), preferred_element_type=F32
        )
        return 0

    lax.fori_loop(0, height, step, 0)
    for tap in range(9):
        out_ref[tap] = acc_ref[:, tap * chans : (tap + 1) * chans].astype(out_ref.dtype)


def make_last(count):
    def kernel(route_ref, ga_ref, x_ref, vec_ref, gup_ref, gdown_ref, opp_ref, own_ref, level_ref,
               lift_ref, cond_ref, out_ref, lift_out, line_ref):
        height, width, chans = x_ref.shape
        region = out_ref.shape[1]
        per_row = width // region
        vec = vec_ref[...]
        first, second = back_vectors(gup_ref, gdown_ref, opp_ref, own_ref, vec, 0, count)
        upper = lax.broadcasted_iota(jnp.int32, (region, chans), 1) >= chans // 2
        table = lift_ref[...]
        lift_out[...] = jnp.zeros(lift_out.shape, F32)

        def clear(d, _):
            out_ref[d] = jnp.zeros((region, chans), BF)
            return 0

        lax.fori_loop(0, out_ref.shape[0], clear, 0, unroll=8)

        def step(r, _):
            grad = level_ref[r] + norm_grad(ga_ref[r], x_ref[r], vec, first, second)
            grad = grad.astype(BF)
            lift_out[...] += lax.dot_general(
                grad, cond_ref[r], (((0,), (0,)), ((), ())), preferred_element_type=F32
            )
            line_ref[...] = jnp.dot(grad, table, preferred_element_type=F32)
            for i in range(per_row):
                k = r * per_row + i
                d = route_ref[3, k]
                piece = line_ref[i * region : (i + 1) * region]
                keep = upper == (route_ref[4, k] > 0)
                out_ref[d] = jnp.where(keep, piece, out_ref[d].astype(F32)).astype(BF)
            return 0

        lax.fori_loop(0, height, step, 0)

    return kernel


def owner_kernel(route_ref, arrived_ref, coarse_ref, interp_ref, grad_ref, interp_out, sums_ref):
    tiles, region, lanes = arrived_ref.shape
    half = lanes // 2
    blocks = coarse_ref.shape[0]
    upper = lax.broadcasted_iota(jnp.int32, (region, lanes), 1) >= half

    def clear(b, _):
        sums_ref[b] = jnp.zeros((region, lanes), F32)
        return 0

    lax.fori_loop(0, blocks, clear, 0, unroll=8)

    def gather(d, _):
        piece = arrived_ref[d].astype(F32)
        count = route_ref[2, d]
        first, second = route_ref[0, d], route_ref[1, d]
        keep = jnp.logical_not(upper) & (count > 0)
        sums_ref[first] += jnp.where(keep, piece, 0.0)
        keep = upper & (count > 1)
        sums_ref[second] += jnp.where(keep, piece, 0.0)
        return 0

    lax.fori_loop(0, tiles, gather, 0, unroll=4)
    table = interp_ref[...]
    interp_out[...] = jnp.zeros(interp_out.shape, F32)

    def finish(b, _):
        total = sums_ref[b].astype(BF)
        wide = lax.dot_general(total, table, (((0,), (0,)), ((), ())), preferred_element_type=F32)
        grad_ref[b] = wide[:half] + wide[half:]
        pair = jnp.concatenate([coarse_ref[b], coarse_ref[b]], axis=0)
        interp_out[...] += jnp.dot(total, pair, preferred_element_type=F32)
        return 0

    lax.fori_loop(0, blocks, finish, 0, unroll=4)


def ring(x, shift):
    count = lax.axis_size("lat")
    return lax.ppermute(x, "lat", [(i, (i + shift) % count) for i in range(count)])


def exchange(to_up, to_down, block):
    return ring(to_down, 1), ring(to_up, -1), ring(block, 2), block


def pair_weights(taps):
    inner, outer = taps.shape[1], taps.shape[2]
    rows = taps.reshape(3, 3 * inner, outer)
    none = jnp.zeros((3 * inner, outer), taps.dtype)
    one = jnp.concatenate([rows[0], rows[1], rows[2], none], axis=0)
    two = jnp.concatenate([none, rows[0], rows[1], rows[2]], axis=0)
    return jnp.concatenate([one, two], axis=1)


def body(coarse, slot_owner, slot_block, interp, lift, conv_weights, gains, fine_noisy, out_grad):
    devices = lax.axis_size(BOTH)
    lat_count = lax.axis_size("lat")
    lat = lax.axis_index("lat")
    me = lax.axis_index(BOTH).astype(jnp.int32).reshape(1)
    noisy = jnp.transpose(fine_noisy[0], (1, 2, 0))
    grad = jnp.transpose(out_grad[0], (1, 2, 0))
    height, width, chans = noisy.shape
    half_height, half = height // 2, width // 2
    slots = slot_owner.shape[1]
    blocks, coarse_chans, cells = coarse.shape
    region = interp.shape[1]
    full_count = float(chans // GROUPS * height * width * lat_count)
    half_count = full_count / 4

    edge = jnp.stack([lat > 0, lat < lat_count - 1]).astype(F32)
    edge = jnp.broadcast_to(edge[:, None], (2, chans))
    forward = [pair_weights(jnp.transpose(conv_weights[i], (0, 2, 1))) for i in range(4)]
    backward = [pair_weights(conv_weights[i][::-1]) for i in range(4)]
    lift_rows = jnp.concatenate([lift.T, lift.T], axis=0)
    lift_cols = jnp.concatenate([lift, lift], axis=1)
    gain_rows = [gains[i : i + 1] for i in range(4)]

    full = (height, width, chans)
    small = (half_height, half, chans)
    full3 = ((height + 2, width, 3 * chans), BF)
    small3 = ((half_height + 2, half, 3 * chans), BF)
    line = ((width, chans), F32)
    vec_shape = ((8, chans), F32)
    full_act = ((height + 2, width, chans), BF)
    small_act = ((half_height + 2, half, chans), BF)
    full_msg = [((width + STAT_ROWS, chans), BF)] * 2 + [((STAT_ROWS, chans), BF)]
    small_msg = [((half + STAT_ROWS, chans), BF)] * 2 + [((STAT_ROWS, chans), BF)]

    edge_msg = ((width + half, chans), BF)
    pooled_grad, edge_up, edge_down = call(
        pool_kernel, [(small, F32), edge_msg, edge_msg], [line], [], [grad], "pool_grad"
    )
    grad_above, grad_below = ring(edge_down, 1), ring(edge_up, -1)

    (route,) = call(
        route_kernel,
        [((8, devices), jnp.int32)],
        [],
        [me],
        [slot_owner[:, :, 0].T, slot_block.T],
        "route",
    )
    (outgoing,) = call(
        send_kernel, [((devices, region, 2 * coarse_chans), BF)], [], [route], [coarse, interp.T], "send"
    )
    outgoing, grad_above, grad_below = lax.optimization_barrier((outgoing, grad_above, grad_below))
    arrived = lax.all_to_all(outgoing, BOTH, split_axis=0, concat_axis=0, tiled=True)
    (act_grad_d,) = call(
        head_back_kernel, [(small, F32)], [small3], [],
        [pooled_grad, grad_above, grad_below, edge, backward[3]], "back_d",
    )

    hidden, cond, *msg = call(
        hidden_kernel, [(full, F32), (full, BF)] + full_msg, [line], [route],
        [arrived, noisy, lift_rows], "hidden",
    )
    msg_h = exchange(*msg)
    conv_a, act_a, vec_a, *msg = call(
        make_first(full_count), [(full, F32), full_act, vec_shape] + full_msg, [full3], [],
        [hidden, *msg_h, edge, gain_rows[0], forward[0]], "conv_a",
    )
    msg_a = exchange(*msg)
    level, pooled, act_b, vec_b, *msg = call(
        make_second(full_count), [(full, F32), (small, F32), full_act, vec_shape] + small_msg,
        [full3, line], [], [conv_a, *msg_a, edge, gain_rows[1], forward[1], hidden], "conv_b",
    )
    msg_p = exchange(*msg)
    conv_c, act_c, vec_c, *msg = call(
        make_first(half_count), [(small, F32), small_act, vec_shape] + small_msg, [small3], [],
        [pooled, *msg_p, edge, gain_rows[2], forward[2]], "conv_c",
    )
    msg_c = exchange(*msg)
    act_d, vec_d, *msg = call(
        make_turn(half_count), [small_act, vec_shape] + small_msg, [], [],
        [conv_c, *msg_c, edge, gain_rows[3], act_grad_d], "turn_d",
    )
    back_d = exchange(*msg)
    (denoised,) = call(
        tail_kernel, [(full, F32)], [small3, line], [], [act_d, forward[3], pooled, level], "conv_d"
    )

    def taps_grad(g, act, name):
        rows3 = full3 if g.shape[1] == width else small3
        acc = ((chans, 9 * chans), F32)
        return call(kernel_grad_kernel, [((9, chans, chans), BF)], [rows3, acc], [], [g, act], name)[0]

    taps_d = taps_grad(pooled_grad.astype(BF), act_d, "taps_d")
    g_c, act_grad_c, *msg = call(
        make_back_mid(half_count), [(small, BF), (small, F32)] + small_msg, [small3], [],
        [act_grad_d, conv_c, msg_c[0], msg_c[1], vec_d, *back_d, edge, backward[2], pooled, vec_c],
        "back_c",
    )
    back_c = exchange(*msg)
    taps_c = taps_grad(g_c, act_c, "taps_c")
    grad_level, g_b, act_grad_b, *msg = call(
        make_back_join(half_count), [(full, F32), (full, BF), (full, F32)] + full_msg,
        [full3, line], [],
        [act_grad_c, pooled, msg_p[0], msg_p[1], vec_c, *back_c, edge, pooled_grad, grad,
         grad_above, grad_below, backward[1], conv_a, vec_b],
        "back_b",
    )
    back_b = exchange(*msg)
    taps_b = taps_grad(g_b, act_b, "taps_b")
    g_a, act_grad_a, *msg = call(
        make_back_mid(full_count), [(full, BF), (full, F32)] + full_msg, [full3], [],
        [act_grad_b, conv_a, msg_a[0], msg_a[1], vec_b, *back_b, edge, backward[0], hidden, vec_a],
        "back_a",
    )
    block = msg[2]
    back_a = (ring(block, 1), ring(block, -1), ring(block, 2), block)
    taps_a = taps_grad(g_a, act_a, "taps_a")
    placed, lift_term = call(
        make_last(full_count),
        [((devices, region, 2 * coarse_chans), BF), ((chans, 2 * coarse_chans), F32)], [line],
        [route],
        [act_grad_a, hidden, vec_a, *back_a, grad_level, lift_cols, cond], "grad_pieces",
    )

    gain_terms = jnp.concatenate(
        [sum(stat_pair(m[3])[1:]) for m in (back_a, back_b, back_c, back_d)], axis=0
    )
    lift_sum = lift_term[:, :coarse_chans] + lift_term[:, coarse_chans:]
    param_rows = chans * chans * 36 // (devices * chans)
    taps = jnp.concatenate(
        [t.reshape(-1, chans) for t in (taps_a, taps_b, taps_c, taps_d)]
    ).reshape(devices, param_rows, chans)
    extra = jnp.concatenate(
        [lift_sum.reshape(-1, chans), gain_terms,
         jnp.zeros((devices - lift_sum.size // chans - 4, chans), F32)]
    ).astype(BF).reshape(devices, 1, chans)
    params = jnp.concatenate([taps, extra], axis=1)
    returned = lax.all_to_all(placed, BOTH, split_axis=0, concat_axis=0, tiled=True)
    params = lax.all_to_all(params, BOTH, split_axis=0, concat_axis=0, tiled=True)
    coarse_grad, interp_term = call(
        owner_kernel, [((blocks, coarse_chans, cells), F32), ((region, cells), F32)],
        [((blocks, region, 2 * coarse_chans), F32)], [route], [returned, coarse, interp.T], "owner",
    )
    param_sum = jnp.sum(params.astype(F32), axis=0)
    interp_rows = jnp.concatenate([interp_term, jnp.zeros((devices - region, cells), F32)])
    interp_parts = lax.all_to_all(
        interp_rows.astype(BF).reshape(devices, 1, cells), BOTH, split_axis=0, concat_axis=0, tiled=True
    )
    interp_sum = jnp.sum(interp_parts.astype(F32), axis=0)
    scale = 1.0 / math.sqrt(height * width * devices)
    chunk = jnp.concatenate([param_sum, interp_sum], axis=0) * scale
    everything = lax.all_gather(chunk.astype(BF), BOTH).astype(F32)
    conv_total = everything[:, :param_rows].reshape(4, 9, chans, chans)
    extra_total = everything[:, param_rows]
    lift_count = lift_sum.size // chans
    lift_total = extra_total[:lift_count].reshape(lift_sum.shape)
    gain_total = extra_total[lift_count : lift_count + 4]
    interp_total = everything[:region, param_rows + 1].T
    return (
        jnp.transpose(denoised, (2, 0, 1))[None],
        coarse_grad,
        interp_total,
        lift_total,
        conv_total,
        gain_total,
    )


def solution(mesh):
    placed = (
        P(BOTH, None, None),
        P(),
        P(),
        P(),
        P(),
        P(),
        P(),
        P("patch", None, "lat", None),
        P("patch", None, "lat", None),
    )
    return jax.shard_map(
        body,
        mesh=mesh,
        in_specs=placed,
        out_specs=(
            P("patch", None, "lat", None),
            P(BOTH, None, None),
            P(),
            P(),
            P(),
            P(),
        ),
        check_vma=False,
    )
```

```python
import math

import jax
import jax.numpy as jnp
from jax import lax
from jax.experimental import pallas as pl
from jax.experimental.pallas import tpu as pltpu
from jax.sharding import PartitionSpec as P

GROUPS = 32
EPSILON = 1e-05
BF = jnp.bfloat16
F32 = jnp.float32
BOTH = ("lat", "patch")
VMEM_BYTES = 30 * 1024 * 1024
STAT_ROWS = 16
SPAN = 4


def call(kernel, outs, scratch, scalars, args, name):
    smem = pl.BlockSpec(memory_space=pltpu.SMEM)
    vmem = pl.BlockSpec(memory_space=pltpu.VMEM)
    return pl.pallas_call(
        kernel,
        out_shape=[jax.ShapeDtypeStruct(s, d) for s, d in outs],
        in_specs=[smem] * len(scalars) + [vmem] * len(args),
        out_specs=[vmem] * len(outs),
        scratch_shapes=[pltpu.VMEM(s, d) for s, d in scratch],
        compiler_params=pltpu.CompilerParams(vmem_limit_bytes=VMEM_BYTES),
        name=name,
    )(*scalars, *args)


def fold8(x):
    return jnp.sum(x.reshape(x.shape[0] // 8, 8, x.shape[1]), axis=0)


def group_sum(v):
    lane = lax.broadcasted_iota(jnp.int32, v.shape, 1)
    n = v.shape[1]
    v = v + jnp.where(lane % 2 == 0, pltpu.roll(v, n - 1, 1), pltpu.roll(v, 1, 1))
    return v + jnp.where(lane % 4 < 2, pltpu.roll(v, n - 2, 1), pltpu.roll(v, 2, 1))


def split3(v):
    hi = v.astype(BF).astype(F32)
    mid = (v - hi).astype(BF).astype(F32)
    return hi, mid, v - hi - mid


def stat_block(first, second):
    row = lax.broadcasted_iota(jnp.int32, (STAT_ROWS, first.shape[1]), 0)
    block = jnp.zeros(row.shape, F32)
    for i, part in enumerate(split3(first) + split3(second)):
        block = jnp.where(row == i, part, block)
    return block.astype(BF)


def stat_pair(block):
    f = block.astype(F32)
    return f[0:1] + f[1:2] + f[2:3], f[3:4] + f[4:5] + f[5:6]


def total_pair(blocks):
    pairs = [stat_pair(b) for b in blocks]
    return sum(p[0] for p in pairs), sum(p[1] for p in pairs)


def put_row(dst, index, value):
    width, chans = value.shape
    cell = lax.broadcasted_iota(jnp.int32, value.shape, 0)
    left = jnp.where(cell == 0, 0.0, pltpu.roll(value, 1, 0))
    right = jnp.where(cell == width - 1, 0.0, pltpu.roll(value, width - 1, 0))
    dst[index, :, 0:chans] = left.astype(BF)
    dst[index, :, chans : 2 * chans] = value.astype(BF)
    dst[index, :, 2 * chans : 3 * chans] = right.astype(BF)


def build_table(table, weights, flipped):
    chans = weights.shape[2]
    span = 3 * chans
    blank = jnp.zeros((span, chans), BF)
    table[0:span, chans : 2 * chans] = blank
    table[3 * span : 4 * span, 0:chans] = blank
    for tap in range(9):
        value = weights[8 - tap if flipped else tap]
        table[tap * chans : (tap + 1) * chans, 0:chans] = value
        table[span + tap * chans : span + (tap + 1) * chans, chans : 2 * chans] = value


def conv_pairs(rows3, table, height, fill, emit, carry):
    chans = table.shape[1] // 2

    def pair(j):
        lhs = jnp.concatenate([rows3[2 * j + s] for s in range(SPAN)], axis=1)
        return jnp.dot(lhs, table[...], preferred_element_type=F32)

    def both(j, out, carry):
        carry = emit(2 * j, out[:, :chans], carry)
        return emit(2 * j + 1, out[:, chans:], carry)

    mixed = (height - 3) // 2
    for r in range(1, 4):
        fill(r)
    for r in range(4 + 2 * mixed, height + 1):
        fill(r)

    def step(j, carry):
        out = pair(j)
        fill(2 * j + 4)
        fill(2 * j + 5)
        return both(j, out, carry)

    carry = lax.fori_loop(0, mixed, step, carry)
    carry = lax.fori_loop(mixed, height // 2, lambda j, c: both(j, pair(j), c), carry)
    if height % 2:
        lhs = jnp.concatenate([rows3[height - 1 + s] for s in range(3)], axis=1)
        out = jnp.dot(lhs, table[0 : lhs.shape[1], 0:chans], preferred_element_type=F32)
        carry = emit(height - 1, out, carry)
    return carry


def sigm(y):
    return 0.5 * jnp.tanh(0.5 * y) + 0.5


def act_of(x, vec):
    y = x * vec[2:3] + vec[3:4]
    return y * sigm(y)


def act_grad(grad, x, vec):
    y = x * vec[2:3] + vec[3:4]
    sg = sigm(y)
    return grad * sg * (1.0 + y * (1.0 - sg)), (x - vec[0:1]) * vec[1:2]


def norm_vectors(up, down, opposite, own, gain, width, height, count):
    up_stats, down_stats = up[width : width + STAT_ROWS], down[width : width + STAT_ROWS]
    first, second = total_pair([own[...], up_stats, down_stats, opposite[...]])
    first = group_sum(jnp.broadcast_to(first, (8, first.shape[1])))
    second = group_sum(jnp.broadcast_to(second, first.shape))
    mean = first / count
    inv = lax.rsqrt(second / count - mean * mean + EPSILON)
    gain8 = jnp.broadcast_to(gain[...], mean.shape)
    scale = inv * gain8
    row = lax.broadcasted_iota(jnp.int32, mean.shape, 0)
    local = 1.0 / (width * height)
    up_mean = stat_pair(up_stats)[0] * local
    down_mean = stat_pair(down_stats)[0] * local
    vec = jnp.where(row == 0, mean, inv)
    for i, part in enumerate([scale, -mean * scale, gain8, up_mean, down_mean]):
        vec = jnp.where(row == i + 2, part, vec)
    return vec


def back_vectors(up, down, opposite, own, vec, width, count):
    stats = [own[...], opposite[...]]
    stats += [up[width : width + STAT_ROWS], down[width : width + STAT_ROWS]]
    first, second = total_pair(stats)
    first = group_sum(jnp.broadcast_to(first * vec[4:5], (8, first.shape[1])))
    second = group_sum(jnp.broadcast_to(second * vec[4:5], first.shape))
    return first[0:1] / count, second[0:1] / count


def norm_grad(grad, x, vec, first, second):
    gs, normed = act_grad(grad, x, vec)
    return vec[1:2] * (gs * vec[4:5] - first - normed * second)


def send_raw(to_up, to_down, block, top, bottom, sums, width, height):
    first = jnp.sum(sums[0], axis=0, keepdims=True)
    second = jnp.sum(sums[1], axis=0, keepdims=True)
    stats = stat_block(first, second)
    mean = stat_pair(stats)[0] * (1.0 / (width * height))
    to_up[0:width] = (top - mean).astype(BF)
    to_down[0:width] = (bottom - mean).astype(BF)
    to_up[width : width + STAT_ROWS] = stats
    to_down[width : width + STAT_ROWS] = stats
    block[...] = stats


def send_grad(to_up, to_down, block, top, bottom, sums, width):
    stats = stat_block(
        jnp.sum(sums[0], axis=0, keepdims=True), jnp.sum(sums[1], axis=0, keepdims=True)
    )
    to_up[0:width] = top.astype(BF)
    to_down[0:width] = bottom.astype(BF)
    to_up[width : width + STAT_ROWS] = stats
    to_down[width : width + STAT_ROWS] = stats
    block[...] = stats


def halo_raw(up, down, vec, width):
    above = up[0:width].astype(F32) + vec[5:6]
    below = down[0:width].astype(F32) + vec[6:7]
    return above, below


def zeros2(chans):
    return jnp.zeros((8, chans), F32), jnp.zeros((8, chans), F32)


def add_sums(sums, x):
    return sums[0] + fold8(x), sums[1] + fold8(x * x)


def route_kernel(me_ref, owners_ref, blocks_ref, out_ref):
    me = me_ref[0]
    slots, tiles = owners_ref.shape
    owners = owners_ref[...]
    mine = owners == me
    k = lax.broadcasted_iota(jnp.int32, (slots, slots), 0)
    j = lax.broadcasted_iota(jnp.int32, (slots, slots), 1)
    earlier = jnp.where(j < k, 1.0, 0.0).astype(BF)
    flags = jnp.where(mine, 1.0, 0.0)
    before = jnp.dot(earlier, flags.astype(BF), preferred_element_type=F32)
    blocks = blocks_ref[...].astype(F32)
    first = jnp.sum(jnp.where(mine & (before < 0.5), blocks, 0.0), axis=0, keepdims=True)
    second = jnp.sum(jnp.where(mine & (before > 0.5), blocks, 0.0), axis=0, keepdims=True)
    count = jnp.sum(flags, axis=0, keepdims=True)
    lane = lax.broadcasted_iota(jnp.int32, (slots, tiles), 1)
    slot = lax.broadcasted_iota(jnp.int32, (slots, tiles), 0)
    column = jnp.sum(jnp.where(lane == me, owners, 0).astype(F32), axis=1, keepdims=True)
    as_row = jnp.sum(jnp.where(lane == slot, column, 0.0), axis=0, keepdims=True)
    same = (column == as_row) & (slot < lane) & (lane < slots)
    position = jnp.sum(jnp.where(same, 1.0, 0.0), axis=0, keepdims=True)
    row = lax.broadcasted_iota(jnp.int32, (8, tiles), 0)
    out = jnp.where(row == 0, first, 0.0)
    for i, part in enumerate([second, count, as_row, position]):
        out = jnp.where(row == i + 1, part, out)
    out_ref[...] = out.astype(jnp.int32)


def send_kernel(route_ref, coarse_ref, interp_ref, out_ref, low_ref, high_ref):
    table = interp_ref[...]
    region = table.shape[0]
    blocks, chans, _ = coarse_ref.shape
    upper = lax.broadcasted_iota(jnp.int32, (region, 2 * chans), 1) >= chans

    def pieces(b, _):
        pair = coarse_ref[pl.ds(2 * b, 2)].reshape(2 * chans, coarse_ref.shape[2])
        piece = lax.dot_general(table, pair, (((1,), (1,)), ((), ())), preferred_element_type=F32)
        turned = pltpu.roll(piece, chans, 1)
        low_ref[2 * b] = piece
        high_ref[2 * b] = turned
        low_ref[2 * b + 1] = turned
        high_ref[2 * b + 1] = piece
        return 0

    lax.fori_loop(0, blocks // 2, pieces, 0, unroll=4)

    def step(d, _):
        first, second = low_ref[route_ref[0, d]], high_ref[route_ref[1, d]]
        out_ref[d] = jnp.where(upper, second, first).astype(BF)
        return 0

    lax.fori_loop(0, out_ref.shape[0], step, 0, unroll=8)


def pool_kernel(grad_ref, pooled_ref, up_ref, down_ref, rows_ref):
    height, width, chans = grad_ref.shape
    half = width // 2

    def step(r, _):
        rows_ref[...] = grad_ref[2 * r] + grad_ref[2 * r + 1]
        pooled_ref[r] = rows_ref[pl.ds(0, half, stride=2)] + rows_ref[pl.ds(1, half, stride=2)]
        return 0

    lax.fori_loop(0, height // 2, step, 0)
    up_ref[0:width] = grad_ref[0].astype(BF)
    up_ref[width : width + half] = pooled_ref[0].astype(BF)
    down_ref[0:width] = grad_ref[height - 1].astype(BF)
    down_ref[width : width + half] = pooled_ref[height // 2 - 1].astype(BF)


def head_back_kernel(pooled_ref, up_ref, down_ref, edge_ref, weights_ref, grad_ref, rows3, table):
    height, width, chans = pooled_ref.shape
    start = up_ref.shape[0] - width
    build_table(table, weights_ref, True)
    put_row(rows3, 0, up_ref[start:].astype(F32) * edge_ref[0:1])
    put_row(rows3, height + 1, down_ref[start:].astype(F32) * edge_ref[1:2])

    def emit(r, value, carry):
        grad_ref[r] = value
        return carry

    conv_pairs(rows3, table, height, lambda r: put_row(rows3, r, pooled_ref[r - 1]), emit, 0)


def hidden_kernel(route_ref, arrived_ref, noisy_ref, lift_ref, hid_ref, cond_ref, up_ref, down_ref,
                  block_ref, line_ref):
    height, width, chans = noisy_ref.shape
    region = arrived_ref.shape[1]
    per_row = width // region
    upper = lax.broadcasted_iota(jnp.int32, (region, chans), 1) >= chans // 2
    table = lift_ref[...]

    def step(r, sums):
        for i in range(per_row):
            k = r * per_row + i
            piece = arrived_ref[route_ref[3, k]].astype(F32)
            keep = upper == (route_ref[4, k] > 0)
            line_ref[i * region : (i + 1) * region] = jnp.where(keep, piece, 0.0)
        cond = line_ref[...].astype(BF)
        cond_ref[r] = cond
        hidden = noisy_ref[r].astype(F32) + jnp.dot(cond, table, preferred_element_type=F32)
        hid_ref[r] = hidden
        return add_sums(sums, hidden)

    sums = lax.fori_loop(0, height, step, zeros2(chans))
    send_raw(up_ref, down_ref, block_ref, hid_ref[0], hid_ref[height - 1], sums, width, height)


def norm_rows(x_ref, vec, up_ref, down_ref, edge_ref, rows3, act_ref):
    height, width, chans = x_ref.shape
    above, below = halo_raw(up_ref, down_ref, vec, width)
    above = act_of(above, vec) * edge_ref[0:1]
    below = act_of(below, vec) * edge_ref[1:2]
    put_row(rows3, 0, above)
    put_row(rows3, height + 1, below)
    act_ref[0] = above.astype(BF)
    act_ref[height + 1] = below.astype(BF)

    def fill(r):
        value = act_of(x_ref[r - 1], vec)
        put_row(rows3, r, value)
        act_ref[r] = value.astype(BF)

    return fill


def make_first(count):
    def kernel(x_ref, up_ref, down_ref, opp_ref, own_ref, edge_ref, gain_ref, weights_ref,
               y_ref, act_ref, vec_ref, to_up, to_down, block_ref, rows3, table):
        height, width, chans = x_ref.shape
        vec = norm_vectors(up_ref, down_ref, opp_ref, own_ref, gain_ref, width, height, count)
        vec_ref[...] = vec
        build_table(table, weights_ref, False)
        fill = norm_rows(x_ref, vec, up_ref, down_ref, edge_ref, rows3, act_ref)

        def emit(r, value, sums):
            y_ref[r] = value
            return add_sums(sums, value)

        sums = conv_pairs(rows3, table, height, fill, emit, zeros2(chans))
        send_raw(to_up, to_down, block_ref, y_ref[0], y_ref[height - 1], sums, width, height)

    return kernel


def make_second(count):
    def kernel(y_ref, up_ref, down_ref, opp_ref, own_ref, edge_ref, gain_ref, weights_ref, hid_ref,
               level_ref, pooled_ref, act_ref, vec_ref, to_up, to_down, block_ref, rows3, table,
               line_ref):
        height, width, chans = y_ref.shape
        half = width // 2
        vec = norm_vectors(up_ref, down_ref, opp_ref, own_ref, gain_ref, width, height, count)
        vec_ref[...] = vec
        build_table(table, weights_ref, False)
        fill = norm_rows(y_ref, vec, up_ref, down_ref, edge_ref, rows3, act_ref)

        def emit(r, value, carry):
            one = hid_ref[r] + value
            level_ref[r] = one
            if carry[0] is None:
                return one, carry[1]
            line_ref[...] = carry[0] + one
            pooled = 0.25 * (line_ref[pl.ds(0, half, stride=2)] + line_ref[pl.ds(1, half, stride=2)])
            pooled_ref[r // 2] = pooled
            return None, add_sums(carry[1], pooled)

        sums = conv_pairs(rows3, table, height, fill, emit, (None, zeros2(chans)))[1]
        last = height // 2 - 1
        send_raw(to_up, to_down, block_ref, pooled_ref[0], pooled_ref[last], sums, half, height // 2)

    return kernel


def make_turn(count):
    def kernel(y_ref, up_ref, down_ref, opp_ref, own_ref, edge_ref, gain_ref, grad_ref,
               act_ref, vec_ref, to_up, to_down, block_ref):
        height, width, chans = y_ref.shape
        vec = norm_vectors(up_ref, down_ref, opp_ref, own_ref, gain_ref, width, height, count)
        vec_ref[...] = vec
        above, below = halo_raw(up_ref, down_ref, vec, width)
        act_ref[0] = (act_of(above, vec) * edge_ref[0:1]).astype(BF)
        act_ref[height + 1] = (act_of(below, vec) * edge_ref[1:2]).astype(BF)

        def fill(r, sums):
            x = y_ref[r]
            y = x * vec[2:3] + vec[3:4]
            sg = sigm(y)
            act_ref[r + 1] = (y * sg).astype(BF)
            gs = grad_ref[r] * sg * (1.0 + y * (1.0 - sg))
            return sums[0] + fold8(gs), sums[1] + fold8(gs * (x - vec[0:1]) * vec[1:2])

        sums = lax.fori_loop(0, height, fill, zeros2(chans))
        send_grad(to_up, to_down, block_ref, grad_ref[0], grad_ref[height - 1], sums, width)

    return kernel


def tail_kernel(act_ref, weights_ref, pooled_ref, level_ref, out_ref, rows3, table, line_ref):
    height, width, chans = pooled_ref.shape
    build_table(table, weights_ref, False)
    put_row(rows3, 0, act_ref[0].astype(F32))
    put_row(rows3, height + 1, act_ref[height + 1].astype(F32))

    def emit(r, value, carry):
        two = pooled_ref[r] + value
        line_ref[pl.ds(0, width, stride=2)] = two
        line_ref[pl.ds(1, width, stride=2)] = two
        wide = line_ref[...]
        out_ref[2 * r] = level_ref[2 * r] + wide
        out_ref[2 * r + 1] = level_ref[2 * r + 1] + wide
        return carry

    conv_pairs(rows3, table, height, lambda r: put_row(rows3, r, act_ref[r].astype(F32)), emit, 0)


def back_conv(rows3, table, fill, x_ref, vec, grad_ref, to_up, to_down, block_ref):
    height, width, chans = x_ref.shape

    def emit(r, value, sums):
        grad_ref[r] = value
        gs, normed = act_grad(value, x_ref[r], vec)
        return sums[0] + fold8(gs), sums[1] + fold8(gs * normed)

    sums = conv_pairs(rows3, table, height, fill, emit, zeros2(chans))
    send_grad(to_up, to_down, block_ref, grad_ref[0], grad_ref[height - 1], sums, width)


def make_back_mid(count):
    def kernel(ga_ref, y_ref, yup_ref, ydown_ref, vec_ref, gup_ref, gdown_ref, opp_ref, own_ref,
               edge_ref, weights_ref, x_ref, xvec_ref,
               g_ref, out_ref, to_up, to_down, block_ref, rows3, table):
        height, width, chans = y_ref.shape
        vec = vec_ref[...]
        first, second = back_vectors(gup_ref, gdown_ref, opp_ref, own_ref, vec, width, count)
        above, below = halo_raw(yup_ref, ydown_ref, vec, width)
        g_above = norm_grad(gup_ref[0:width].astype(F32), above, vec, first, second)
        g_below = norm_grad(gdown_ref[0:width].astype(F32), below, vec, first, second)
        put_row(rows3, 0, g_above * edge_ref[0:1])
        put_row(rows3, height + 1, g_below * edge_ref[1:2])

        def fill(r):
            value = norm_grad(ga_ref[r - 1], y_ref[r - 1], vec, first, second)
            put_row(rows3, r, value)
            g_ref[r - 1] = value.astype(BF)

        build_table(table, weights_ref, True)
        back_conv(rows3, table, fill, x_ref, xvec_ref[...], out_ref, to_up, to_down, block_ref)

    return kernel


def make_back_join(count):
    def kernel(ga_ref, p_ref, pup_ref, pdown_ref, pvec_ref, gup_ref, gdown_ref, opp_ref, own_ref,
               edge_ref, pg_ref, og_ref, oup_ref, odown_ref, weights_ref, x_ref, xvec_ref,
               level_ref, g_ref, out_ref, to_up, to_down, block_ref, rows3, table, line_ref):
        half_height, half, chans = p_ref.shape
        height, width, _ = og_ref.shape
        vec = pvec_ref[...]
        first, second = back_vectors(gup_ref, gdown_ref, opp_ref, own_ref, vec, half, count)

        def widened(value):
            line_ref[pl.ds(0, half, stride=2)] = value
            line_ref[pl.ds(1, half, stride=2)] = value
            return 0.25 * line_ref[...]

        above, below = halo_raw(pup_ref, pdown_ref, vec, half)
        g_above = norm_grad(gup_ref[0:half].astype(F32), above, vec, first, second)
        g_below = norm_grad(gdown_ref[0:half].astype(F32), below, vec, first, second)
        wide = widened(g_above + oup_ref[width : width + half].astype(F32))
        put_row(rows3, 0, (oup_ref[0:width].astype(F32) + wide) * edge_ref[0:1])
        wide = widened(g_below + odown_ref[width : width + half].astype(F32))
        put_row(rows3, height + 1, (odown_ref[0:width].astype(F32) + wide) * edge_ref[1:2])

        def widen_row(r, _):
            value = pg_ref[r] + norm_grad(ga_ref[r], p_ref[r], vec, first, second)
            wide = widened(value)
            for i in range(2):
                grad = og_ref[2 * r + i] + wide
                level_ref[2 * r + i] = grad
            return 0

        def fill(r):
            grad = level_ref[r - 1]
            put_row(rows3, r, grad)
            g_ref[r - 1] = grad.astype(BF)

        build_table(table, weights_ref, True)
        lax.fori_loop(0, half_height, widen_row, 0)
        back_conv(rows3, table, fill, x_ref, xvec_ref[...], out_ref, to_up, to_down, block_ref)

    return kernel


def kernel_grad_kernel(g_ref, act_ref, out_ref, rows3, acc_ref):
    height, width, chans = g_ref.shape

    def fill(r, _):
        put_row(rows3, r, act_ref[r].astype(F32))
        return 0

    lax.fori_loop(0, height + 2, fill, 0)
    acc_ref[...] = jnp.zeros(acc_ref.shape, F32)

    def step(r, _):
        rhs = jnp.concatenate([rows3[r + s] for s in range(3)], axis=1)
        acc_ref[...] += lax.dot_general(
            g_ref[r], rhs, (((0,), (0,)), ((), ())), preferred_element_type=F32
        )
        return 0

    lax.fori_loop(0, height, step, 0)
    for tap in range(9):
        out_ref[tap] = acc_ref[:, tap * chans : (tap + 1) * chans].astype(out_ref.dtype)


def make_last(count):
    def kernel(route_ref, ga_ref, x_ref, vec_ref, gup_ref, gdown_ref, opp_ref, own_ref, level_ref,
               lift_ref, cond_ref, out_ref, lift_out, line_ref):
        height, width, chans = x_ref.shape
        region = out_ref.shape[1]
        per_row = width // region
        vec = vec_ref[...]
        first, second = back_vectors(gup_ref, gdown_ref, opp_ref, own_ref, vec, 0, count)
        upper = lax.broadcasted_iota(jnp.int32, (region, chans), 1) >= chans // 2
        table = lift_ref[...]
        lift_out[...] = jnp.zeros(lift_out.shape, F32)

        def clear(d, _):
            out_ref[d] = jnp.zeros((region, chans), BF)
            return 0

        lax.fori_loop(0, out_ref.shape[0], clear, 0, unroll=8)

        def step(r, _):
            grad = level_ref[r] + norm_grad(ga_ref[r], x_ref[r], vec, first, second)
            grad = grad.astype(BF)
            lift_out[...] += lax.dot_general(
                grad, cond_ref[r], (((0,), (0,)), ((), ())), preferred_element_type=F32
            )
            line_ref[...] = jnp.dot(grad, table, preferred_element_type=F32)
            for i in range(per_row):
                k = r * per_row + i
                d = route_ref[3, k]
                piece = line_ref[i * region : (i + 1) * region]
                keep = upper == (route_ref[4, k] > 0)
                out_ref[d] = jnp.where(keep, piece, out_ref[d].astype(F32)).astype(BF)
            return 0

        lax.fori_loop(0, height, step, 0)

    return kernel


def owner_kernel(route_ref, arrived_ref, coarse_ref, interp_ref, grad_ref, interp_out, sums_ref):
    tiles, region, lanes = arrived_ref.shape
    half = lanes // 2
    blocks = coarse_ref.shape[0]
    upper = lax.broadcasted_iota(jnp.int32, (region, lanes), 1) >= half

    def clear(b, _):
        sums_ref[b] = jnp.zeros((region, lanes), F32)
        return 0

    lax.fori_loop(0, blocks, clear, 0, unroll=8)

    def gather(d, _):
        piece = arrived_ref[d].astype(F32)
        count = route_ref[2, d]
        first, second = route_ref[0, d], route_ref[1, d]
        keep = jnp.logical_not(upper) & (count > 0)
        sums_ref[first] += jnp.where(keep, piece, 0.0)
        keep = upper & (count > 1)
        sums_ref[second] += jnp.where(keep, piece, 0.0)
        return 0

    lax.fori_loop(0, tiles, gather, 0, unroll=4)
    table = interp_ref[...]
    interp_out[...] = jnp.zeros(interp_out.shape, F32)

    def finish(b, _):
        one, two = sums_ref[2 * b], sums_ref[2 * b + 1]
        one, two = one + pltpu.roll(one, half, 1), two + pltpu.roll(two, half, 1)
        total = jnp.where(upper, two, one).astype(BF)
        wide = lax.dot_general(total, table, (((0,), (0,)), ((), ())), preferred_element_type=F32)
        grad_ref[pl.ds(2 * b, 2)] = wide.reshape(2, half, wide.shape[1])
        pair = coarse_ref[pl.ds(2 * b, 2)].reshape(lanes, coarse_ref.shape[2])
        interp_out[...] += jnp.dot(total, pair, preferred_element_type=F32)
        return 0

    lax.fori_loop(0, blocks // 2, finish, 0, unroll=4)


def finish_kernel(sums_ref, conv_ref, extra_ref, interp_ref):
    devices, rows, lanes = sums_ref.shape
    taps = conv_ref.shape[0] // devices
    region = interp_ref.shape[0]
    for d in range(devices):
        part = sums_ref[d].astype(F32)
        conv_ref[d * taps : (d + 1) * taps] = part[0:taps]
        extra_ref[d : d + 1] = part[taps : taps + 1]
        if d < region:
            interp_ref[d : d + 1] = part[taps + 1 : taps + 2]


def ring(x, shift):
    count = lax.axis_size("lat")
    return lax.ppermute(x, "lat", [(i, (i + shift) % count) for i in range(count)])


def exchange(to_up, to_down, block):
    return ring(to_down, 1), ring(to_up, -1), ring(block, 2), block


def both(first, second):
    return lax.optimization_barrier((first, second))


def body(coarse, slot_owner, slot_block, interp, lift, conv_weights, gains, fine_noisy, out_grad):
    devices = lax.axis_size(BOTH)
    lat_count = lax.axis_size("lat")
    lat = lax.axis_index("lat")
    me = lax.axis_index(BOTH).astype(jnp.int32).reshape(1)
    noisy = jnp.transpose(fine_noisy[0], (1, 2, 0))
    grad = jnp.transpose(out_grad[0], (1, 2, 0))
    height, width, chans = noisy.shape
    half_height, half = height // 2, width // 2
    slots = slot_owner.shape[1]
    blocks, coarse_chans, cells = coarse.shape
    region = interp.shape[1]
    full_count = float(chans // GROUPS * height * width * lat_count)
    half_count = full_count / 4

    edge = jnp.stack([lat > 0, lat < lat_count - 1]).astype(F32)
    edge = jnp.broadcast_to(edge[:, None], (2, chans))
    turned = jnp.transpose(conv_weights, (0, 1, 3, 2))
    forward = [turned[i] for i in range(4)]
    backward = [conv_weights[i] for i in range(4)]
    lift_rows = jnp.concatenate([lift.T, lift.T], axis=0)
    lift_cols = jnp.concatenate([lift, lift], axis=1)
    gain_rows = [gains[i : i + 1] for i in range(4)]

    full = (height, width, chans)
    small = (half_height, half, chans)
    table = ((SPAN * 3 * chans, 2 * chans), BF)
    full3 = [((height + 2, width, 3 * chans), BF), table]
    small3 = [((half_height + 2, half, 3 * chans), BF), table]
    line = ((width, chans), F32)
    vec_shape = ((8, chans), F32)
    full_act = ((height + 2, width, chans), BF)
    small_act = ((half_height + 2, half, chans), BF)
    full_msg = [((width + STAT_ROWS, chans), BF)] * 2 + [((STAT_ROWS, chans), BF)]
    small_msg = [((half + STAT_ROWS, chans), BF)] * 2 + [((STAT_ROWS, chans), BF)]

    (route,) = call(
        route_kernel,
        [((8, devices), jnp.int32)],
        [],
        [me],
        [slot_owner[:, :, 0].T, slot_block.T],
        "route",
    )
    piece_shape = (region, 2 * coarse_chans)
    (outgoing,) = call(
        send_kernel, [((devices,) + piece_shape, BF)], [((blocks,) + piece_shape, F32)] * 2, [route],
        [coarse, interp.T], "send",
    )
    arrived = lax.all_to_all(outgoing, BOTH, split_axis=0, concat_axis=0, tiled=True)
    edge_msg = ((width + half, chans), BF)
    pooled_grad, edge_up, edge_down = call(
        pool_kernel, [(small, F32), edge_msg, edge_msg], [line], [], [grad], "pool_grad"
    )
    grad_above, grad_below = ring(edge_down, 1), ring(edge_up, -1)
    arrived, (pooled_grad, turned) = both(arrived, (pooled_grad, turned))

    hidden, cond, *msg = call(
        hidden_kernel, [(full, F32), (full, BF)] + full_msg, [line], [route],
        [arrived, noisy, lift_rows], "hidden",
    )
    msg_h = exchange(*msg)
    (act_grad_d,) = call(
        head_back_kernel, [(small, F32)], small3, [],
        [pooled_grad, grad_above, grad_below, edge, backward[3]], "back_d",
    )
    msg_h, act_grad_d = both(msg_h, act_grad_d)
    conv_a, act_a, vec_a, *msg = call(
        make_first(full_count), [(full, F32), full_act, vec_shape] + full_msg, full3, [],
        [hidden, *msg_h, edge, gain_rows[0], forward[0]], "conv_a",
    )
    msg_a = exchange(*msg)
    level, pooled, act_b, vec_b, *msg = call(
        make_second(full_count), [(full, F32), (small, F32), full_act, vec_shape] + small_msg,
        full3 + [line], [], [conv_a, *msg_a, edge, gain_rows[1], forward[1], hidden], "conv_b",
    )
    msg_p = exchange(*msg)
    conv_c, act_c, vec_c, *msg = call(
        make_first(half_count), [(small, F32), small_act, vec_shape] + small_msg, small3, [],
        [pooled, *msg_p, edge, gain_rows[2], forward[2]], "conv_c",
    )
    msg_c = exchange(*msg)
    act_d, vec_d, *msg = call(
        make_turn(half_count), [small_act, vec_shape] + small_msg, [], [],
        [conv_c, *msg_c, edge, gain_rows[3], act_grad_d], "turn_d",
    )
    back_d = exchange(*msg)

    def taps_grad(g, act, name):
        rows3 = full3[0] if g.shape[1] == width else small3[0]
        acc = ((chans, 9 * chans), F32)
        return call(kernel_grad_kernel, [((9, chans, chans), BF)], [rows3, acc], [], [g, act], name)[0]

    taps_d = taps_grad(pooled_grad.astype(BF), act_d, "taps_d")
    back_d, taps_d = both(back_d, taps_d)
    g_c, act_grad_c, *msg = call(
        make_back_mid(half_count), [(small, BF), (small, F32)] + small_msg, small3, [],
        [act_grad_d, conv_c, msg_c[0], msg_c[1], vec_d, *back_d, edge, backward[2], pooled, vec_c],
        "back_c",
    )
    back_c = exchange(*msg)
    taps_c = taps_grad(g_c, act_c, "taps_c")
    back_c, taps_c = both(back_c, taps_c)
    grad_level, g_b, act_grad_b, *msg = call(
        make_back_join(half_count), [(full, F32), (full, BF), (full, F32)] + full_msg,
        full3 + [line], [],
        [act_grad_c, pooled, msg_p[0], msg_p[1], vec_c, *back_c, edge, pooled_grad, grad,
         grad_above, grad_below, backward[1], conv_a, vec_b],
        "back_b",
    )
    back_b = exchange(*msg)
    g_a, act_grad_a, *msg = call(
        make_back_mid(full_count), [(full, BF), (full, F32)] + full_msg, full3, [],
        [act_grad_b, conv_a, msg_a[0], msg_a[1], vec_b, *back_b, edge, backward[0], hidden, vec_a],
        "back_a",
    )
    block = msg[2]
    back_a = (ring(block, 1), ring(block, -1), ring(block, 2), block)
    placed, lift_term = call(
        make_last(full_count),
        [((devices, region, 2 * coarse_chans), BF), ((chans, 2 * coarse_chans), F32)], [line],
        [route],
        [act_grad_a, hidden, vec_a, *back_a, grad_level, lift_cols, cond], "grad_pieces",
    )

    placed, (g_a, g_b, act_d) = both(placed, (g_a, g_b, act_d))
    returned = lax.all_to_all(placed, BOTH, split_axis=0, concat_axis=0, tiled=True)
    taps_b = taps_grad(g_b, act_b, "taps_b")
    taps_a = taps_grad(g_a, act_a, "taps_a")
    (denoised,) = call(
        tail_kernel, [(full, F32)], small3 + [line], [], [act_d, forward[3], pooled, level], "conv_d"
    )
    gain_terms = jnp.concatenate(
        [stat_pair(m[3])[1] for m in (back_a, back_b, back_c, back_d)], axis=0
    )
    lift_sum = lift_term[:, :coarse_chans] + lift_term[:, coarse_chans:]
    param_rows = 36
    lift_count = lift_sum.size // chans
    taps = jnp.concatenate(
        [t.reshape(-1, chans) for t in (taps_a, taps_b, taps_c, taps_d)]
    ).reshape(devices, param_rows, chans)
    extra = jnp.concatenate(
        [lift_sum.reshape(-1, chans), gain_terms, jnp.zeros((devices - lift_count - 4, chans), F32)]
    ).astype(BF).reshape(devices, 1, chans)
    params = jnp.concatenate([taps, extra, jnp.zeros((devices, 3, chans), BF)], axis=1)
    returned, (params, denoised) = both(returned, (params, denoised))
    params = lax.all_to_all(params, BOTH, split_axis=0, concat_axis=0, tiled=True)
    coarse_grad, interp_term = call(
        owner_kernel, [((blocks, coarse_chans, cells), F32), ((region, cells), F32)],
        [((blocks,) + piece_shape, F32)], [route], [returned, coarse, interp.T], "owner",
    )
    param_sum = jnp.sum(params.astype(F32), axis=0)
    interp_term, param_sum = both(interp_term, param_sum)
    interp_rows = jnp.concatenate([interp_term, jnp.zeros((devices - region, cells), F32)])
    interp_parts = lax.all_to_all(
        interp_rows.astype(BF).reshape(devices, 1, cells), BOTH, split_axis=0, concat_axis=0, tiled=True
    )
    scale = 1.0 / math.sqrt(height * width * devices)
    interp_sum = jnp.sum(interp_parts.astype(F32), axis=0)
    row = lax.broadcasted_iota(jnp.int32, param_sum.shape, 0)
    chunk = (jnp.where(row == param_rows + 1, interp_sum, param_sum) * scale).astype(BF)
    everything = lax.all_to_all(
        jnp.broadcast_to(chunk[None], (devices,) + chunk.shape), BOTH, split_axis=0, concat_axis=0,
        tiled=True,
    )
    conv_total, extra_total, interp_total = call(
        finish_kernel, [((devices * param_rows, chans), F32), ((devices, chans), F32),
                        ((region, cells), F32)],
        [], [], [everything], "finish",
    )
    conv_total = conv_total.reshape(4, 9, chans, chans)
    lift_total = extra_total[:lift_count].reshape(lift_sum.shape)
    gain_total = extra_total[lift_count : lift_count + 4]
    interp_total = interp_total.T
    return (
        jnp.transpose(denoised, (2, 0, 1))[None],
        coarse_grad,
        interp_total,
        lift_total,
        conv_total,
        gain_total,
    )


def solution(mesh):
    placed = (
        P(BOTH, None, None),
        P(),
        P(),
        P(),
        P(),
        P(),
        P(),
        P("patch", None, "lat", None),
        P("patch", None, "lat", None),
    )
    return jax.shard_map(
        body,
        mesh=mesh,
        in_specs=placed,
        out_specs=(
            P("patch", None, "lat", None),
            P(BOTH, None, None),
            P(),
            P(),
            P(),
            P(),
        ),
        check_vma=False,
    )
```

```python
import math

import jax
import jax.numpy as jnp
from jax import lax
from jax.experimental import pallas as pl
from jax.experimental.pallas import tpu as pltpu
from jax.sharding import PartitionSpec as P

GROUPS = 32
EPSILON = 1e-05
BF = jnp.bfloat16
F32 = jnp.float32
BOTH = ("lat", "patch")
VMEM_BYTES = 15 * 1024 * 1024
STAT_ROWS = 16
SPAN = 4


def call(kernel, outs, scratch, scalars, args, name, aliases={}, copies=0):
    smem = pl.BlockSpec(memory_space=pltpu.SMEM)
    vmem = pl.BlockSpec(memory_space=pltpu.VMEM)
    stay = pl.BlockSpec(memory_space=pl.ANY)
    taken = [i + len(scalars) in aliases for i in range(len(args))]
    return pl.pallas_call(
        kernel,
        out_shape=[jax.ShapeDtypeStruct(s, d) for s, d in outs],
        in_specs=[smem] * len(scalars) + [stay if t else vmem for t in taken],
        out_specs=[stay if i in aliases.values() else vmem for i in range(len(outs))],
        scratch_shapes=[pltpu.VMEM(s, d) for s, d in scratch]
        + [pltpu.SemaphoreType.DMA] * copies,
        compiler_params=pltpu.CompilerParams(vmem_limit_bytes=VMEM_BYTES),
        name=name,
        input_output_aliases=aliases,
    )(*scalars, *args)


def fold8(x):
    return jnp.sum(x.reshape(x.shape[0] // 8, 8, x.shape[1]), axis=0)


def group_sum(v):
    lane = lax.broadcasted_iota(jnp.int32, v.shape, 1)
    n = v.shape[1]
    v = v + jnp.where(lane % 2 == 0, pltpu.roll(v, n - 1, 1), pltpu.roll(v, 1, 1))
    return v + jnp.where(lane % 4 < 2, pltpu.roll(v, n - 2, 1), pltpu.roll(v, 2, 1))


def split3(v):
    hi = v.astype(BF).astype(F32)
    mid = (v - hi).astype(BF).astype(F32)
    return hi, mid, v - hi - mid


def stat_block(first, second):
    row = lax.broadcasted_iota(jnp.int32, (STAT_ROWS, first.shape[1]), 0)
    block = jnp.zeros(row.shape, F32)
    for i, part in enumerate(split3(first) + split3(second)):
        block = jnp.where(row == i, part, block)
    return block.astype(BF)


def stat_pair(block):
    f = block.astype(F32)
    return f[0:1] + f[1:2] + f[2:3], f[3:4] + f[4:5] + f[5:6]


def total_pair(blocks):
    pairs = [stat_pair(b) for b in blocks]
    return sum(p[0] for p in pairs), sum(p[1] for p in pairs)


def put_row(dst, index, value):
    width, chans = value.shape
    cell = lax.broadcasted_iota(jnp.int32, value.shape, 0)
    left = jnp.where(cell == 0, 0.0, pltpu.roll(value, 1, 0))
    right = jnp.where(cell == width - 1, 0.0, pltpu.roll(value, width - 1, 0))
    dst[index, :, 0:chans] = left.astype(BF)
    dst[index, :, chans : 2 * chans] = value.astype(BF)
    dst[index, :, 2 * chans : 3 * chans] = right.astype(BF)


def build_table(table, weights, flipped):
    chans = weights.shape[2]
    span = 3 * chans
    blank = jnp.zeros((span, chans), BF)
    table[0:span, chans : 2 * chans] = blank
    table[3 * span : 4 * span, 0:chans] = blank
    for tap in range(9):
        value = weights[8 - tap if flipped else tap]
        table[tap * chans : (tap + 1) * chans, 0:chans] = value
        table[span + tap * chans : span + (tap + 1) * chans, chans : 2 * chans] = value


def conv_pairs(rows3, table, height, fill, emit, carry):
    chans = table.shape[1] // 2

    def pair(j):
        lhs = jnp.concatenate([rows3[2 * j + s] for s in range(SPAN)], axis=1)
        return jnp.dot(lhs, table[...], preferred_element_type=F32)

    def both(j, out, carry):
        carry = emit(2 * j, out[:, :chans], carry)
        return emit(2 * j + 1, out[:, chans:], carry)

    mixed = (height - 3) // 2
    for r in range(1, 4):
        fill(r)
    for r in range(4 + 2 * mixed, height + 1):
        fill(r)

    def step(j, carry):
        out = pair(j)
        fill(2 * j + 4)
        fill(2 * j + 5)
        return both(j, out, carry)

    carry = lax.fori_loop(0, mixed, step, carry, unroll=True)
    for j in range(mixed, height // 2):
        carry = both(j, pair(j), carry)
    if height % 2:
        lhs = jnp.concatenate([rows3[height - 1 + s] for s in range(3)], axis=1)
        out = jnp.dot(lhs, table[0 : lhs.shape[1], 0:chans], preferred_element_type=F32)
        carry = emit(height - 1, out, carry)
    return carry


def sigm(y):
    return 0.5 * jnp.tanh(0.5 * y) + 0.5


def act_of(x, vec):
    y = x * vec[2:3] + vec[3:4]
    return y * sigm(y)


def act_grad(grad, x, vec):
    y = x * vec[2:3] + vec[3:4]
    sg = sigm(y)
    return grad * sg * (1.0 + y * (1.0 - sg)), (x - vec[0:1]) * vec[1:2]


def norm_vectors(up, down, opposite, own, gain, width, height, count):
    up_stats, down_stats = up[width : width + STAT_ROWS], down[width : width + STAT_ROWS]
    first, second = total_pair([own[...], up_stats, down_stats, opposite[...]])
    first = group_sum(jnp.broadcast_to(first, (8, first.shape[1])))
    second = group_sum(jnp.broadcast_to(second, first.shape))
    mean = first / count
    inv = lax.rsqrt(second / count - mean * mean + EPSILON)
    gain8 = jnp.broadcast_to(gain[...], mean.shape)
    scale = inv * gain8
    row = lax.broadcasted_iota(jnp.int32, mean.shape, 0)
    local = 1.0 / (width * height)
    up_mean = stat_pair(up_stats)[0] * local
    down_mean = stat_pair(down_stats)[0] * local
    vec = jnp.where(row == 0, mean, inv)
    for i, part in enumerate([scale, -mean * scale, gain8, up_mean, down_mean]):
        vec = jnp.where(row == i + 2, part, vec)
    return vec


def back_vectors(up, down, opposite, own, vec, width, count):
    stats = [own[...], opposite[...]]
    stats += [up[width : width + STAT_ROWS], down[width : width + STAT_ROWS]]
    first, second = total_pair(stats)
    first = group_sum(jnp.broadcast_to(first * vec[4:5], (8, first.shape[1])))
    second = group_sum(jnp.broadcast_to(second * vec[4:5], first.shape))
    return first[0:1] / count, second[0:1] / count


def norm_grad(grad, x, vec, first, second):
    gs, normed = act_grad(grad, x, vec)
    return vec[1:2] * (gs * vec[4:5] - first - normed * second)


def send_raw(to_up, to_down, block, top, bottom, sums, width, height):
    first = jnp.sum(sums[0], axis=0, keepdims=True)
    second = jnp.sum(sums[1], axis=0, keepdims=True)
    stats = stat_block(first, second)
    mean = stat_pair(stats)[0] * (1.0 / (width * height))
    to_up[0:width] = (top - mean).astype(BF)
    to_down[0:width] = (bottom - mean).astype(BF)
    to_up[width : width + STAT_ROWS] = stats
    to_down[width : width + STAT_ROWS] = stats
    block[...] = stats


def send_grad(to_up, to_down, block, top, bottom, sums, width):
    stats = stat_block(
        jnp.sum(sums[0], axis=0, keepdims=True), jnp.sum(sums[1], axis=0, keepdims=True)
    )
    to_up[0:width] = top.astype(BF)
    to_down[0:width] = bottom.astype(BF)
    to_up[width : width + STAT_ROWS] = stats
    to_down[width : width + STAT_ROWS] = stats
    block[...] = stats


def halo_raw(up, down, vec, width):
    above = up[0:width].astype(F32) + vec[5:6]
    below = down[0:width].astype(F32) + vec[6:7]
    return above, below


def zeros2(chans):
    return jnp.zeros((8, chans), F32), jnp.zeros((8, chans), F32)


def add_sums(sums, x):
    return sums[0] + fold8(x), sums[1] + fold8(x * x)


def route_kernel(me_ref, owners_ref, blocks_ref, out_ref):
    me = me_ref[0]
    slots, tiles = owners_ref.shape
    owners = owners_ref[...]
    mine = owners == me
    k = lax.broadcasted_iota(jnp.int32, (slots, slots), 0)
    j = lax.broadcasted_iota(jnp.int32, (slots, slots), 1)
    earlier = jnp.where(j < k, 1.0, 0.0).astype(BF)
    flags = jnp.where(mine, 1.0, 0.0)
    before = jnp.dot(earlier, flags.astype(BF), preferred_element_type=F32)
    blocks = blocks_ref[...].astype(F32)
    first = jnp.sum(jnp.where(mine & (before < 0.5), blocks, 0.0), axis=0, keepdims=True)
    second = jnp.sum(jnp.where(mine & (before > 0.5), blocks, 0.0), axis=0, keepdims=True)
    count = jnp.sum(flags, axis=0, keepdims=True)
    lane = lax.broadcasted_iota(jnp.int32, (slots, tiles), 1)
    slot = lax.broadcasted_iota(jnp.int32, (slots, tiles), 0)
    column = jnp.sum(jnp.where(lane == me, owners, 0).astype(F32), axis=1, keepdims=True)
    as_row = jnp.sum(jnp.where(lane == slot, column, 0.0), axis=0, keepdims=True)
    same = (column == as_row) & (slot < lane) & (lane < slots)
    position = jnp.sum(jnp.where(same, 1.0, 0.0), axis=0, keepdims=True)
    row = lax.broadcasted_iota(jnp.int32, (8, tiles), 0)
    out = jnp.where(row == 0, first, 0.0)
    for i, part in enumerate([second, count, as_row, position]):
        out = jnp.where(row == i + 1, part, out)
    out_ref[...] = out.astype(jnp.int32)


def send_kernel(route_ref, coarse_ref, interp_ref, out_ref, low_ref, high_ref):
    table = interp_ref[...]
    region = table.shape[0]
    blocks, chans, _ = coarse_ref.shape
    upper = lax.broadcasted_iota(jnp.int32, (region, 2 * chans), 1) >= chans

    def pieces(b, _):
        pair = coarse_ref[pl.ds(2 * b, 2)].reshape(2 * chans, coarse_ref.shape[2])
        piece = lax.dot_general(table, pair, (((1,), (1,)), ((), ())), preferred_element_type=F32)
        turned = pltpu.roll(piece, chans, 1)
        low_ref[2 * b] = piece
        high_ref[2 * b] = turned
        low_ref[2 * b + 1] = turned
        high_ref[2 * b + 1] = piece
        return 0

    lax.fori_loop(0, blocks // 2, pieces, 0, unroll=4)

    def step(d, _):
        first, second = low_ref[route_ref[0, d]], high_ref[route_ref[1, d]]
        out_ref[d] = jnp.where(upper, second, first).astype(BF)
        return 0

    lax.fori_loop(0, out_ref.shape[0], step, 0, unroll=8)


def pool_kernel(grad_ref, pooled_ref, up_ref, down_ref, rows_ref):
    height, width, chans = grad_ref.shape
    half = width // 2

    def step(r, _):
        rows_ref[...] = grad_ref[2 * r] + grad_ref[2 * r + 1]
        pooled_ref[r] = rows_ref[pl.ds(0, half, stride=2)] + rows_ref[pl.ds(1, half, stride=2)]
        return 0

    lax.fori_loop(0, height // 2, step, 0)
    up_ref[0:width] = grad_ref[0].astype(BF)
    up_ref[width : width + half] = pooled_ref[0].astype(BF)
    down_ref[0:width] = grad_ref[height - 1].astype(BF)
    down_ref[width : width + half] = pooled_ref[height // 2 - 1].astype(BF)


def head_back_kernel(pooled_ref, up_ref, down_ref, edge_ref, weights_ref, grad_ref, rows3, table):
    height, width, chans = pooled_ref.shape
    start = up_ref.shape[0] - width
    build_table(table, weights_ref, True)
    put_row(rows3, 0, up_ref[start:].astype(F32) * edge_ref[0:1])
    put_row(rows3, height + 1, down_ref[start:].astype(F32) * edge_ref[1:2])

    def emit(r, value, carry):
        grad_ref[r] = value
        return carry

    conv_pairs(rows3, table, height, lambda r: put_row(rows3, r, pooled_ref[r - 1]), emit, 0)


def hidden_kernel(route_ref, arrived_ref, noisy_ref, lift_ref, hid_ref, cond_ref, up_ref, down_ref,
                  block_ref, line_ref):
    height, width, chans = noisy_ref.shape
    region = arrived_ref.shape[1]
    per_row = width // region
    upper = lax.broadcasted_iota(jnp.int32, (region, chans), 1) >= chans // 2
    table = lift_ref[...]

    def step(r, sums):
        for i in range(per_row):
            k = r * per_row + i
            piece = arrived_ref[route_ref[3, k]].astype(F32)
            keep = upper == (route_ref[4, k] > 0)
            line_ref[i * region : (i + 1) * region] = jnp.where(keep, piece, 0.0)
        cond = line_ref[...].astype(BF)
        cond_ref[r] = cond
        hidden = noisy_ref[r].astype(F32) + jnp.dot(cond, table, preferred_element_type=F32)
        hid_ref[r] = hidden
        return add_sums(sums, hidden)

    sums = lax.fori_loop(0, height, step, zeros2(chans), unroll=2)
    send_raw(up_ref, down_ref, block_ref, hid_ref[0], hid_ref[height - 1], sums, width, height)


def norm_rows(x_ref, vec, up_ref, down_ref, edge_ref, rows3, act_ref):
    height, width, chans = x_ref.shape
    above, below = halo_raw(up_ref, down_ref, vec, width)
    above = act_of(above, vec) * edge_ref[0:1]
    below = act_of(below, vec) * edge_ref[1:2]
    put_row(rows3, 0, above)
    put_row(rows3, height + 1, below)
    if act_ref is not None:
        act_ref[0] = above.astype(BF)
        act_ref[height + 1] = below.astype(BF)

    def fill(r):
        value = act_of(x_ref[r - 1], vec)
        put_row(rows3, r, value)
        if act_ref is not None:
            act_ref[r] = value.astype(BF)

    return fill


def make_first(count, keep):
    def kernel(x_ref, up_ref, down_ref, opp_ref, own_ref, edge_ref, gain_ref, weights_ref,
               y_ref, *rest):
        act_ref = rest[0] if keep else None
        vec_ref, to_up, to_down, block_ref, rows3, table = rest[1:] if keep else rest
        height, width, chans = x_ref.shape
        vec = norm_vectors(up_ref, down_ref, opp_ref, own_ref, gain_ref, width, height, count)
        vec_ref[...] = vec
        build_table(table, weights_ref, False)
        fill = norm_rows(x_ref, vec, up_ref, down_ref, edge_ref, rows3, act_ref)

        def emit(r, value, sums):
            y_ref[r] = value
            return add_sums(sums, value)

        sums = conv_pairs(rows3, table, height, fill, emit, zeros2(chans))
        send_raw(to_up, to_down, block_ref, y_ref[0], y_ref[height - 1], sums, width, height)

    return kernel


def make_second(count):
    def kernel(y_ref, up_ref, down_ref, opp_ref, own_ref, edge_ref, gain_ref, weights_ref, hid_ref,
               level_ref, pooled_ref, vec_ref, to_up, to_down, block_ref, rows3, table,
               line_ref):
        height, width, chans = y_ref.shape
        half = width // 2
        vec = norm_vectors(up_ref, down_ref, opp_ref, own_ref, gain_ref, width, height, count)
        vec_ref[...] = vec
        build_table(table, weights_ref, False)
        fill = norm_rows(y_ref, vec, up_ref, down_ref, edge_ref, rows3, None)

        def emit(r, value, carry):
            one = hid_ref[r] + value
            level_ref[r] = one
            if carry[0] is None:
                return one, carry[1]
            line_ref[...] = carry[0] + one
            pooled = 0.25 * (line_ref[pl.ds(0, half, stride=2)] + line_ref[pl.ds(1, half, stride=2)])
            pooled_ref[r // 2] = pooled
            return None, add_sums(carry[1], pooled)

        sums = conv_pairs(rows3, table, height, fill, emit, (None, zeros2(chans)))[1]
        last = height // 2 - 1
        send_raw(to_up, to_down, block_ref, pooled_ref[0], pooled_ref[last], sums, half, height // 2)

    return kernel


def make_turn(count):
    def kernel(y_ref, up_ref, down_ref, opp_ref, own_ref, edge_ref, gain_ref, grad_ref,
               act_ref, vec_ref, to_up, to_down, block_ref):
        height, width, chans = y_ref.shape
        vec = norm_vectors(up_ref, down_ref, opp_ref, own_ref, gain_ref, width, height, count)
        vec_ref[...] = vec
        above, below = halo_raw(up_ref, down_ref, vec, width)
        act_ref[0] = (act_of(above, vec) * edge_ref[0:1]).astype(BF)
        act_ref[height + 1] = (act_of(below, vec) * edge_ref[1:2]).astype(BF)

        def fill(r, sums):
            x = y_ref[r]
            y = x * vec[2:3] + vec[3:4]
            sg = sigm(y)
            act_ref[r + 1] = (y * sg).astype(BF)
            gs = grad_ref[r] * sg * (1.0 + y * (1.0 - sg))
            return sums[0] + fold8(gs), sums[1] + fold8(gs * (x - vec[0:1]) * vec[1:2])

        sums = lax.fori_loop(0, height, fill, zeros2(chans))
        send_grad(to_up, to_down, block_ref, grad_ref[0], grad_ref[height - 1], sums, width)

    return kernel


def tail_kernel(act_ref, weights_ref, pooled_ref, level_ref, out_ref, rows3, table, line_ref):
    height, width, chans = pooled_ref.shape
    build_table(table, weights_ref, False)
    put_row(rows3, 0, act_ref[0].astype(F32))
    put_row(rows3, height + 1, act_ref[height + 1].astype(F32))

    def emit(r, value, carry):
        two = pooled_ref[r] + value
        line_ref[pl.ds(0, width, stride=2)] = two
        line_ref[pl.ds(1, width, stride=2)] = two
        wide = line_ref[...]
        out_ref[2 * r] = level_ref[2 * r] + wide
        out_ref[2 * r + 1] = level_ref[2 * r + 1] + wide
        return carry

    conv_pairs(rows3, table, height, lambda r: put_row(rows3, r, act_ref[r].astype(F32)), emit, 0)


def back_conv(rows3, table, fill, x_ref, vec, grad_ref, to_up, to_down, block_ref):
    height, width, chans = x_ref.shape

    def emit(r, value, sums):
        grad_ref[r] = value
        gs, normed = act_grad(value, x_ref[r], vec)
        return sums[0] + fold8(gs), sums[1] + fold8(gs * normed)

    sums = conv_pairs(rows3, table, height, fill, emit, zeros2(chans))
    send_grad(to_up, to_down, block_ref, grad_ref[0], grad_ref[height - 1], sums, width)


def make_back_mid(count):
    def kernel(ga_ref, y_ref, yup_ref, ydown_ref, vec_ref, gup_ref, gdown_ref, opp_ref, own_ref,
               edge_ref, weights_ref, x_ref, xvec_ref,
               g_ref, out_ref, to_up, to_down, block_ref, rows3, table):
        height, width, chans = y_ref.shape
        vec = vec_ref[...]
        first, second = back_vectors(gup_ref, gdown_ref, opp_ref, own_ref, vec, width, count)
        above, below = halo_raw(yup_ref, ydown_ref, vec, width)
        g_above = norm_grad(gup_ref[0:width].astype(F32), above, vec, first, second)
        g_below = norm_grad(gdown_ref[0:width].astype(F32), below, vec, first, second)
        put_row(rows3, 0, g_above * edge_ref[0:1])
        put_row(rows3, height + 1, g_below * edge_ref[1:2])

        def fill(r):
            value = norm_grad(ga_ref[r - 1], y_ref[r - 1], vec, first, second)
            put_row(rows3, r, value)
            g_ref[r - 1] = value.astype(BF)

        build_table(table, weights_ref, True)
        back_conv(rows3, table, fill, x_ref, xvec_ref[...], out_ref, to_up, to_down, block_ref)

    return kernel


def make_back_join(count):
    def kernel(ga_ref, p_ref, pup_ref, pdown_ref, pvec_ref, gup_ref, gdown_ref, opp_ref, own_ref,
               edge_ref, pg_ref, og_ref, oup_ref, odown_ref, weights_ref, x_ref, xvec_ref,
               g_ref, out_ref, to_up, to_down, block_ref, rows3, table, line_ref):
        half_height, half, chans = p_ref.shape
        height, width, _ = og_ref.shape
        vec = pvec_ref[...]
        first, second = back_vectors(gup_ref, gdown_ref, opp_ref, own_ref, vec, half, count)

        def widened(value):
            line_ref[pl.ds(0, half, stride=2)] = value
            line_ref[pl.ds(1, half, stride=2)] = value
            return 0.25 * line_ref[...]

        above, below = halo_raw(pup_ref, pdown_ref, vec, half)
        g_above = norm_grad(gup_ref[0:half].astype(F32), above, vec, first, second)
        g_below = norm_grad(gdown_ref[0:half].astype(F32), below, vec, first, second)
        wide = widened(g_above + oup_ref[width : width + half].astype(F32))
        put_row(rows3, 0, (oup_ref[0:width].astype(F32) + wide) * edge_ref[0:1])
        wide = widened(g_below + odown_ref[width : width + half].astype(F32))
        put_row(rows3, height + 1, (odown_ref[0:width].astype(F32) + wide) * edge_ref[1:2])

        def widen_row(r, _):
            value = pg_ref[r] + norm_grad(ga_ref[r], p_ref[r], vec, first, second)
            wide = widened(value)
            for i in range(2):
                g_ref[2 * r + i] = (og_ref[2 * r + i] + wide).astype(BF)
            return 0

        def fill(r):
            put_row(rows3, r, g_ref[r - 1].astype(F32))

        build_table(table, weights_ref, True)
        lax.fori_loop(0, half_height, widen_row, 0, unroll=True)
        back_conv(rows3, table, fill, x_ref, xvec_ref[...], out_ref, to_up, to_down, block_ref)

    return kernel


def taps_of(g_ref, rows3, acc_ref, out_ref):
    height, width, chans = g_ref.shape
    acc_ref[...] = jnp.zeros(acc_ref.shape, F32)

    def step(r, _):
        rhs = jnp.concatenate([rows3[r + s] for s in range(3)], axis=1)
        acc_ref[...] += lax.dot_general(
            g_ref[r], rhs, (((0,), (0,)), ((), ())), preferred_element_type=F32
        )
        return 0

    lax.fori_loop(0, height, step, 0, unroll=True)
    for tap in range(9):
        part = acc_ref[:, tap * chans : (tap + 1) * chans]
        out_ref[tap * chans : (tap + 1) * chans] = part.astype(out_ref.dtype)


def taps_act_kernel(g_ref, act_ref, out_ref, rows3, acc_ref):
    def fill(r, _):
        put_row(rows3, r, act_ref[r].astype(F32))
        return 0

    lax.fori_loop(0, g_ref.shape[0] + 2, fill, 0, unroll=True)
    taps_of(g_ref, rows3, acc_ref, out_ref)


def taps_raw_kernel(g_ref, x_ref, up_ref, down_ref, vec_ref, edge_ref, out_ref, rows3, acc_ref):
    fill = norm_rows(x_ref, vec_ref[...], up_ref, down_ref, edge_ref, rows3, None)

    def one(r, _):
        fill(r + 1)
        return 0

    lax.fori_loop(0, g_ref.shape[0], one, 0, unroll=True)
    taps_of(g_ref, rows3, acc_ref, out_ref)


def params_kernel(taps_a, taps_b, taps_c, taps_d, lift_ref, own_a, own_b, own_c, own_d, out_ref):
    start = 0
    for taps in (taps_a, taps_b, taps_c, taps_d):
        out_ref[start : start + taps.shape[0]] = taps[...]
        start += taps.shape[0]
    lift = lift_ref[...]
    chans, lanes = lift.shape
    lift = (lift + pltpu.roll(lift, lanes // 2, 1)).T[: lanes // 2]
    gains = [stat_pair(own[...])[1] for own in (own_a, own_b, own_c, own_d)]
    rows = jnp.concatenate([lift] + gains + [jnp.zeros((12, chans), F32)], axis=0)
    out_ref[start : start + rows.shape[0]] = rows.astype(BF)
    start += rows.shape[0]
    out_ref[start:] = jnp.zeros((out_ref.shape[0] - start, chans), BF)


def make_last(count):
    def kernel(route_ref, ga_ref, x_ref, vec_ref, gup_ref, gdown_ref, opp_ref, own_ref, level_ref,
               lift_ref, cond_ref, out_ref, lift_out, line_ref):
        height, width, chans = x_ref.shape
        region = out_ref.shape[1]
        per_row = width // region
        vec = vec_ref[...]
        first, second = back_vectors(gup_ref, gdown_ref, opp_ref, own_ref, vec, 0, count)
        upper = lax.broadcasted_iota(jnp.int32, (region, chans), 1) >= chans // 2
        table = lift_ref[...]
        lift_out[...] = jnp.zeros(lift_out.shape, F32)

        def clear(d, _):
            out_ref[d] = jnp.zeros((region, chans), BF)
            return 0

        lax.fori_loop(0, out_ref.shape[0], clear, 0, unroll=8)

        def step(r, _):
            grad = norm_grad(ga_ref[r], x_ref[r], vec, first, second)
            grad = (level_ref[r].astype(F32) + grad).astype(BF)
            lift_out[...] += lax.dot_general(
                grad, cond_ref[r], (((0,), (0,)), ((), ())), preferred_element_type=F32
            )
            line_ref[...] = jnp.dot(grad, table, preferred_element_type=F32)
            for i in range(per_row):
                k = r * per_row + i
                d = route_ref[3, k]
                piece = line_ref[i * region : (i + 1) * region]
                keep = upper == (route_ref[4, k] > 0)
                out_ref[d] = jnp.where(keep, piece, out_ref[d].astype(F32)).astype(BF)
            return 0

        lax.fori_loop(0, height, step, 0, unroll=2)

    return kernel


def make_owner(interp_at):
    def kernel(route_ref, arrived_ref, coarse_ref, interp_ref, known_ref, grad_ref, params_ref,
               sums_ref, interp_out, tail_ref, sem):
        owner_sums(route_ref, arrived_ref, coarse_ref, interp_ref, grad_ref, sums_ref, interp_out)
        rows = interp_out.shape[0]
        pad = jnp.zeros((8, interp_out.shape[1]), F32)
        tail_ref[...] = jnp.concatenate([interp_out[...], pad], axis=0).astype(BF)
        target = params_ref.at[pl.ds(interp_at, rows + 8)]
        copy = pltpu.make_async_copy(tail_ref, target, sem)
        copy.start()
        copy.wait()

    return kernel


def owner_sums(route_ref, arrived_ref, coarse_ref, interp_ref, grad_ref, sums_ref, interp_out):
    tiles, region, lanes = arrived_ref.shape
    half = lanes // 2
    blocks = coarse_ref.shape[0]
    upper = lax.broadcasted_iota(jnp.int32, (region, lanes), 1) >= half

    def clear(b, _):
        sums_ref[b] = jnp.zeros((region, lanes), F32)
        return 0

    lax.fori_loop(0, blocks, clear, 0, unroll=8)

    def gather(d, _):
        piece = arrived_ref[d].astype(F32)
        count = route_ref[2, d]
        first, second = route_ref[0, d], route_ref[1, d]
        keep = jnp.logical_not(upper) & (count > 0)
        sums_ref[first] += jnp.where(keep, piece, 0.0)
        keep = upper & (count > 1)
        sums_ref[second] += jnp.where(keep, piece, 0.0)
        return 0

    lax.fori_loop(0, tiles, gather, 0, unroll=8)
    table = interp_ref[...]
    interp_out[...] = jnp.zeros(interp_out.shape, F32)

    def finish(b, _):
        one, two = sums_ref[2 * b], sums_ref[2 * b + 1]
        one, two = one + pltpu.roll(one, half, 1), two + pltpu.roll(two, half, 1)
        total = jnp.where(upper, two, one).astype(BF)
        wide = lax.dot_general(total, table, (((0,), (0,)), ((), ())), preferred_element_type=F32)
        grad_ref[pl.ds(2 * b, 2)] = wide.reshape(2, half, wide.shape[1])
        pair = coarse_ref[pl.ds(2 * b, 2)].reshape(lanes, coarse_ref.shape[2])
        interp_out[...] += jnp.dot(total, pair, preferred_element_type=F32)
        return 0

    lax.fori_loop(0, blocks // 2, finish, 0, unroll=8)


def make_sum(scale):
    def kernel(parts_ref, out_ref):
        devices, rows, lanes = parts_ref.shape

        def add(d, total):
            return total + parts_ref[d].astype(F32)

        total = lax.fori_loop(0, devices, add, jnp.zeros((rows, lanes), F32), unroll=8)
        total = (total * scale).astype(BF)

        def put(d, _):
            out_ref[d] = total
            return 0

        lax.fori_loop(0, devices, put, 0, unroll=8)

    return kernel


def finish_kernel(rows_ref, *outs):
    start = 0
    for out in outs:
        count = out.shape[0]
        span = -(-count // 8) * 8
        step = 128 if count % 128 == 0 else span

        def move(i, _, start=start, out=out, step=step, count=count):
            part = rows_ref[pl.ds(pl.multiple_of(start + i * step, 8), step)].astype(F32)
            out[pl.ds(i * step, min(step, count))] = part[: min(step, count)]
            return 0

        lax.fori_loop(0, span // step, move, 0)
        start += span


def ring(x, shift):
    count = lax.axis_size("lat")
    return lax.ppermute(x, "lat", [(i, (i + shift) % count) for i in range(count)])


def exchange(to_up, to_down, block):
    return ring(to_down, 1), ring(to_up, -1), ring(block, 2), block


def both(first, second):
    return lax.optimization_barrier((first, second))


def body(coarse, slot_owner, slot_block, interp, lift, conv_weights, gains, fine_noisy, out_grad):
    devices = lax.axis_size(BOTH)
    lat_count = lax.axis_size("lat")
    lat = lax.axis_index("lat")
    me = lax.axis_index(BOTH).astype(jnp.int32).reshape(1)
    noisy = jnp.transpose(fine_noisy[0], (1, 2, 0))
    grad = jnp.transpose(out_grad[0], (1, 2, 0))
    height, width, chans = noisy.shape
    half_height, half = height // 2, width // 2
    slots = slot_owner.shape[1]
    blocks, coarse_chans, cells = coarse.shape
    region = interp.shape[1]
    full_count = float(chans // GROUPS * height * width * lat_count)
    half_count = full_count / 4

    edge = jnp.stack([lat > 0, lat < lat_count - 1]).astype(F32)
    edge = jnp.broadcast_to(edge[:, None], (2, chans))
    turned = jnp.transpose(conv_weights, (0, 1, 3, 2))
    forward = [turned[i] for i in range(4)]
    backward = [conv_weights[i] for i in range(4)]
    lift_rows = jnp.concatenate([lift.T, lift.T], axis=0)
    lift_cols = jnp.concatenate([lift, lift], axis=1)
    gain_rows = [gains[i : i + 1] for i in range(4)]

    full = (height, width, chans)
    small = (half_height, half, chans)
    table = ((SPAN * 3 * chans, 2 * chans), BF)
    full3 = [((height + 2, width, 3 * chans), BF), table]
    small3 = [((half_height + 2, half, 3 * chans), BF), table]
    line = ((width, chans), F32)
    vec_shape = ((8, chans), F32)
    small_act = ((half_height + 2, half, chans), BF)
    full_msg = [((width + STAT_ROWS, chans), BF)] * 2 + [((STAT_ROWS, chans), BF)]
    small_msg = [((half + STAT_ROWS, chans), BF)] * 2 + [((STAT_ROWS, chans), BF)]

    (route,) = call(
        route_kernel,
        [((8, devices), jnp.int32)],
        [],
        [me],
        [slot_owner[:, :, 0].T, slot_block.T],
        "route",
    )
    piece_shape = (region, 2 * coarse_chans)
    (outgoing,) = call(
        send_kernel, [((devices,) + piece_shape, BF)], [((blocks,) + piece_shape, F32)] * 2, [route],
        [coarse, interp.T], "send",
    )
    arrived = lax.all_to_all(outgoing, BOTH, split_axis=0, concat_axis=0, tiled=True)
    edge_msg = ((width + half, chans), BF)
    pooled_grad, edge_up, edge_down = call(
        pool_kernel, [(small, F32), edge_msg, edge_msg], [line], [], [grad], "pool_grad"
    )
    grad_above, grad_below = ring(edge_down, 1), ring(edge_up, -1)
    arrived, (pooled_grad, turned) = both(arrived, (pooled_grad, turned))

    hidden, cond, *msg = call(
        hidden_kernel, [(full, F32), (full, BF)] + full_msg, [line], [route],
        [arrived, noisy, lift_rows], "hidden",
    )
    msg_h = exchange(*msg)
    (act_grad_d,) = call(
        head_back_kernel, [(small, F32)], small3, [],
        [pooled_grad, grad_above, grad_below, edge, backward[3]], "back_d",
    )
    msg_h, act_grad_d = both(msg_h, act_grad_d)
    conv_a, vec_a, *msg = call(
        make_first(full_count, False), [(full, F32), vec_shape] + full_msg, full3, [],
        [hidden, *msg_h, edge, gain_rows[0], forward[0]], "conv_a",
    )
    msg_a = exchange(*msg)
    level, pooled, vec_b, *msg = call(
        make_second(full_count), [(full, F32), (small, F32), vec_shape] + small_msg,
        full3 + [line], [], [conv_a, *msg_a, edge, gain_rows[1], forward[1], hidden], "conv_b",
    )
    msg_p = exchange(*msg)
    conv_c, act_c, vec_c, *msg = call(
        make_first(half_count, True), [(small, F32), small_act, vec_shape] + small_msg, small3, [],
        [pooled, *msg_p, edge, gain_rows[2], forward[2]], "conv_c",
    )
    msg_c = exchange(*msg)
    act_d, vec_d, *msg = call(
        make_turn(half_count), [small_act, vec_shape] + small_msg, [], [],
        [conv_c, *msg_c, edge, gain_rows[3], act_grad_d], "turn_d",
    )
    back_d = exchange(*msg)

    acc = ((chans, 9 * chans), F32)
    taps_shape = [((9 * chans, chans), BF)]

    def taps_grad(g, act, name):
        return call(taps_act_kernel, taps_shape, [small3[0], acc], [], [g, act], name)[0]

    def taps_again(g, x, msg, vec, name):
        args = [g, x, msg[0], msg[1], vec, edge]
        return call(taps_raw_kernel, taps_shape, [full3[0], acc], [], args, name)[0]

    taps_d = taps_grad(pooled_grad.astype(BF), act_d, "taps_d")
    back_d, taps_d = both(back_d, taps_d)
    g_c, act_grad_c, *msg = call(
        make_back_mid(half_count), [(small, BF), (small, F32)] + small_msg, small3, [],
        [act_grad_d, conv_c, msg_c[0], msg_c[1], vec_d, *back_d, edge, backward[2], pooled, vec_c],
        "back_c",
    )
    back_c = exchange(*msg)
    taps_c = taps_grad(g_c, act_c, "taps_c")
    back_c, taps_c = both(back_c, taps_c)
    g_b, act_grad_b, *msg = call(
        make_back_join(half_count), [(full, BF), (full, F32)] + full_msg,
        full3 + [line], [],
        [act_grad_c, pooled, msg_p[0], msg_p[1], vec_c, *back_c, edge, pooled_grad, grad,
         grad_above, grad_below, backward[1], conv_a, vec_b],
        "back_b",
    )
    back_b = exchange(*msg)
    g_a, act_grad_a, *msg = call(
        make_back_mid(full_count), [(full, BF), (full, F32)] + full_msg, full3, [],
        [act_grad_b, conv_a, msg_a[0], msg_a[1], vec_b, *back_b, edge, backward[0], hidden, vec_a],
        "back_a",
    )
    block = msg[2]
    back_a = (ring(block, 1), ring(block, -1), ring(block, 2), block)
    placed, lift_term = call(
        make_last(full_count),
        [((devices, region, 2 * coarse_chans), BF), ((chans, 2 * coarse_chans), F32)], [line],
        [route],
        [act_grad_a, hidden, vec_a, *back_a, g_b, lift_cols, cond], "grad_pieces",
    )

    placed, (g_a, g_b, act_d) = both(placed, (g_a, g_b, act_d))
    returned = lax.all_to_all(placed, BOTH, split_axis=0, concat_axis=0, tiled=True)
    taps_b = taps_again(g_b, conv_a, msg_a, vec_b, "taps_b")
    taps_a = taps_again(g_a, hidden, msg_h, vec_a, "taps_a")
    chunk = 40
    conv_rows = 36 * chans
    interp_at = conv_rows + coarse_chans + 16
    params_shape = ((devices * chunk, chans), BF)
    (params,) = call(
        params_kernel, [params_shape], [], [],
        [taps_a, taps_b, taps_c, taps_d, lift_term, back_a[3], back_b[3], back_c[3], back_d[3]],
        "params",
    )
    returned, params = both(returned, params)
    coarse_grad, params = call(
        make_owner(interp_at), [((blocks, coarse_chans, cells), F32), params_shape],
        [((blocks,) + piece_shape, F32), ((region, cells), F32), ((region + 8, cells), BF)],
        [route], [returned, coarse, interp.T, params], "owner", {4: 1}, 1,
    )
    params, act_d = both(params, act_d)
    params = lax.all_to_all(
        params.reshape(devices, chunk, chans), BOTH, split_axis=0, concat_axis=0, tiled=True
    )
    (denoised,) = call(
        tail_kernel, [(full, F32)], small3 + [line], [], [act_d, forward[3], pooled, level], "conv_d"
    )
    params, denoised = both(params, denoised)
    scale = 1.0 / math.sqrt(height * width * devices)
    (copies,) = call(make_sum(scale), [((devices, chunk, chans), BF)], [], [], [params], "sums")
    everything = lax.all_to_all(copies, BOTH, split_axis=0, concat_axis=0, tiled=True)
    conv_total, lift_total, gain_total, interp_total = call(
        finish_kernel,
        [((conv_rows, chans), F32), ((coarse_chans, chans), F32), ((16, chans), F32),
         ((region, cells), F32)],
        [], [], [everything.reshape(devices * chunk, chans)], "finish",
    )
    conv_total = conv_total.reshape(4, 9, chans, chans)
    lift_total = lift_total.T
    gain_total = gain_total[:4]
    interp_total = interp_total.T
    return (
        jnp.transpose(denoised, (2, 0, 1))[None],
        coarse_grad,
        interp_total,
        lift_total,
        conv_total,
        gain_total,
    )


def solution(mesh):
    placed = (
        P(BOTH, None, None),
        P(),
        P(),
        P(),
        P(),
        P(),
        P(),
        P("patch", None, "lat", None),
        P("patch", None, "lat", None),
    )
    return jax.shard_map(
        body,
        mesh=mesh,
        in_specs=placed,
        out_specs=(
            P("patch", None, "lat", None),
            P(BOTH, None, None),
            P(),
            P(),
            P(),
            P(),
        ),
        check_vma=False,
    )
```

```python
import math

import jax
import jax.numpy as jnp
from jax import lax
from jax.experimental import pallas as pl
from jax.experimental.pallas import tpu as pltpu
from jax.sharding import PartitionSpec as P

GROUPS = 32
EPSILON = 1e-05
BF = jnp.bfloat16
F32 = jnp.float32
BOTH = ("lat", "patch")
VMEM_BYTES = 15 * 1024 * 1024
STAT_ROWS = 16
SPAN = 4


def call(kernel, outs, scratch, scalars, args, name, aliases={}, copies=0):
    smem = pl.BlockSpec(memory_space=pltpu.SMEM)
    vmem = pl.BlockSpec(memory_space=pltpu.VMEM)
    stay = pl.BlockSpec(memory_space=pl.ANY)
    taken = [i + len(scalars) in aliases for i in range(len(args))]
    return pl.pallas_call(
        kernel,
        out_shape=[jax.ShapeDtypeStruct(s, d) for s, d in outs],
        in_specs=[smem] * len(scalars) + [stay if t else vmem for t in taken],
        out_specs=[stay if i in aliases.values() else vmem for i in range(len(outs))],
        scratch_shapes=[pltpu.VMEM(s, d) for s, d in scratch]
        + [pltpu.SemaphoreType.DMA] * copies,
        compiler_params=pltpu.CompilerParams(vmem_limit_bytes=VMEM_BYTES),
        name=name,
        input_output_aliases=aliases,
    )(*scalars, *args)


def fold8(x):
    return jnp.sum(x.reshape(x.shape[0] // 8, 8, x.shape[1]), axis=0)


def group_sum(v):
    lane = lax.broadcasted_iota(jnp.int32, v.shape, 1)
    n = v.shape[1]
    v = v + jnp.where(lane % 2 == 0, pltpu.roll(v, n - 1, 1), pltpu.roll(v, 1, 1))
    return v + jnp.where(lane % 4 < 2, pltpu.roll(v, n - 2, 1), pltpu.roll(v, 2, 1))


def split3(v):
    hi = v.astype(BF).astype(F32)
    mid = (v - hi).astype(BF).astype(F32)
    return hi, mid, v - hi - mid


def stat_block(first, second):
    row = lax.broadcasted_iota(jnp.int32, (STAT_ROWS, first.shape[1]), 0)
    block = jnp.zeros(row.shape, F32)
    for i, part in enumerate(split3(first) + split3(second)):
        block = jnp.where(row == i, part, block)
    return block.astype(BF)


def stat_pair(block):
    f = block.astype(F32)
    return f[0:1] + f[1:2] + f[2:3], f[3:4] + f[4:5] + f[5:6]


def total_pair(blocks):
    pairs = [stat_pair(b) for b in blocks]
    return sum(p[0] for p in pairs), sum(p[1] for p in pairs)


def put_row(dst, index, value):
    width, chans = value.shape
    cell = lax.broadcasted_iota(jnp.int32, value.shape, 0)
    left = jnp.where(cell == 0, 0.0, pltpu.roll(value, 1, 0))
    right = jnp.where(cell == width - 1, 0.0, pltpu.roll(value, width - 1, 0))
    dst[index, :, 0:chans] = left.astype(BF)
    dst[index, :, chans : 2 * chans] = value.astype(BF)
    dst[index, :, 2 * chans : 3 * chans] = right.astype(BF)


def build_table(table, weights, flipped):
    chans = weights.shape[2]
    span = 3 * chans
    blank = jnp.zeros((span, chans), BF)
    table[0:span, chans : 2 * chans] = blank
    table[3 * span : 4 * span, 0:chans] = blank
    for tap in range(9):
        value = weights[8 - tap if flipped else tap]
        table[tap * chans : (tap + 1) * chans, 0:chans] = value
        table[span + tap * chans : span + (tap + 1) * chans, chans : 2 * chans] = value


def conv_pairs(rows3, table, height, fill, emit, carry):
    chans = table.shape[1] // 2

    def pair(j):
        lhs = jnp.concatenate([rows3[2 * j + s] for s in range(SPAN)], axis=1)
        return jnp.dot(lhs, table[...], preferred_element_type=F32)

    def both(j, out, carry):
        carry = emit(2 * j, out[:, :chans], carry)
        return emit(2 * j + 1, out[:, chans:], carry)

    mixed = (height - 3) // 2
    for r in range(1, 4):
        fill(r)
    for r in range(4 + 2 * mixed, height + 1):
        fill(r)

    def step(j, carry):
        out = pair(j)
        fill(2 * j + 4)
        fill(2 * j + 5)
        return both(j, out, carry)

    carry = lax.fori_loop(0, mixed, step, carry, unroll=True)
    for j in range(mixed, height // 2):
        carry = both(j, pair(j), carry)
    if height % 2:
        lhs = jnp.concatenate([rows3[height - 1 + s] for s in range(3)], axis=1)
        out = jnp.dot(lhs, table[0 : lhs.shape[1], 0:chans], preferred_element_type=F32)
        carry = emit(height - 1, out, carry)
    return carry


def sigm(y):
    return 0.5 * jnp.tanh(0.5 * y) + 0.5


def act_of(x, vec):
    y = x * vec[2:3] + vec[3:4]
    return y * sigm(y)


def act_grad(grad, x, vec):
    y = x * vec[2:3] + vec[3:4]
    sg = sigm(y)
    return grad * sg * (1.0 + y * (1.0 - sg)), (x - vec[0:1]) * vec[1:2]


def norm_vectors(up, down, opposite, own, gain, width, height, count):
    up_stats, down_stats = up[width : width + STAT_ROWS], down[width : width + STAT_ROWS]
    first, second = total_pair([own[...], up_stats, down_stats, opposite[...]])
    first = group_sum(jnp.broadcast_to(first, (8, first.shape[1])))
    second = group_sum(jnp.broadcast_to(second, first.shape))
    mean = first / count
    inv = lax.rsqrt(second / count - mean * mean + EPSILON)
    gain8 = jnp.broadcast_to(gain[...], mean.shape)
    scale = inv * gain8
    row = lax.broadcasted_iota(jnp.int32, mean.shape, 0)
    local = 1.0 / (width * height)
    up_mean = stat_pair(up_stats)[0] * local
    down_mean = stat_pair(down_stats)[0] * local
    vec = jnp.where(row == 0, mean, inv)
    for i, part in enumerate([scale, -mean * scale, gain8, up_mean, down_mean]):
        vec = jnp.where(row == i + 2, part, vec)
    return vec


def back_vectors(up, down, opposite, own, vec, width, count):
    stats = [own[...], opposite[...]]
    stats += [up[width : width + STAT_ROWS], down[width : width + STAT_ROWS]]
    first, second = total_pair(stats)
    first = group_sum(jnp.broadcast_to(first * vec[4:5], (8, first.shape[1])))
    second = group_sum(jnp.broadcast_to(second * vec[4:5], first.shape))
    inv = vec[1:2]
    slope = inv * inv * (second[0:1] / count)
    return inv * (first[0:1] / count) - vec[0:1] * slope, slope


def norm_grad(grad, x, vec, offset, slope):
    y = x * vec[2:3] + vec[3:4]
    sg = sigm(y)
    gs = grad * sg * (1.0 + y * (1.0 - sg))
    return gs * vec[2:3] - (x * slope + offset)


def send_raw(to_up, to_down, block, top, bottom, sums, width, height):
    first = jnp.sum(sums[0], axis=0, keepdims=True)
    second = jnp.sum(sums[1], axis=0, keepdims=True)
    stats = stat_block(first, second)
    mean = stat_pair(stats)[0] * (1.0 / (width * height))
    to_up[0:width] = (top - mean).astype(BF)
    to_down[0:width] = (bottom - mean).astype(BF)
    to_up[width : width + STAT_ROWS] = stats
    to_down[width : width + STAT_ROWS] = stats
    block[...] = stats


def send_grad(to_up, to_down, block, top, bottom, sums, width):
    stats = stat_block(
        jnp.sum(sums[0], axis=0, keepdims=True), jnp.sum(sums[1], axis=0, keepdims=True)
    )
    to_up[0:width] = top.astype(BF)
    to_down[0:width] = bottom.astype(BF)
    to_up[width : width + STAT_ROWS] = stats
    to_down[width : width + STAT_ROWS] = stats
    block[...] = stats


def halo_raw(up, down, vec, width):
    above = up[0:width].astype(F32) + vec[5:6]
    below = down[0:width].astype(F32) + vec[6:7]
    return above, below


def zeros2(chans):
    return jnp.zeros((8, chans), F32), jnp.zeros((8, chans), F32)


def add_sums(sums, x):
    return sums[0] + fold8(x), sums[1] + fold8(x * x)


def route_kernel(me_ref, owners_ref, blocks_ref, out_ref):
    me = me_ref[0]
    slots, tiles = owners_ref.shape
    owners = owners_ref[...]
    mine = owners == me
    k = lax.broadcasted_iota(jnp.int32, (slots, slots), 0)
    j = lax.broadcasted_iota(jnp.int32, (slots, slots), 1)
    earlier = jnp.where(j < k, 1.0, 0.0).astype(BF)
    flags = jnp.where(mine, 1.0, 0.0)
    before = jnp.dot(earlier, flags.astype(BF), preferred_element_type=F32)
    blocks = blocks_ref[...].astype(F32)
    first = jnp.sum(jnp.where(mine & (before < 0.5), blocks, 0.0), axis=0, keepdims=True)
    second = jnp.sum(jnp.where(mine & (before > 0.5), blocks, 0.0), axis=0, keepdims=True)
    count = jnp.sum(flags, axis=0, keepdims=True)
    lane = lax.broadcasted_iota(jnp.int32, (slots, tiles), 1)
    slot = lax.broadcasted_iota(jnp.int32, (slots, tiles), 0)
    column = jnp.sum(jnp.where(lane == me, owners, 0).astype(F32), axis=1, keepdims=True)
    as_row = jnp.sum(jnp.where(lane == slot, column, 0.0), axis=0, keepdims=True)
    same = (column == as_row) & (slot < lane) & (lane < slots)
    position = jnp.sum(jnp.where(same, 1.0, 0.0), axis=0, keepdims=True)
    row = lax.broadcasted_iota(jnp.int32, (8, tiles), 0)
    out = jnp.where(row == 0, first, 0.0)
    for i, part in enumerate([second, count, as_row, position]):
        out = jnp.where(row == i + 1, part, out)
    out_ref[...] = out.astype(jnp.int32)


def send_kernel(route_ref, coarse_ref, interp_ref, out_ref, low_ref, high_ref):
    table = interp_ref[...]
    region = table.shape[0]
    blocks, chans, _ = coarse_ref.shape
    upper = lax.broadcasted_iota(jnp.int32, (region, 2 * chans), 1) >= chans

    def pieces(b, _):
        pair = coarse_ref[pl.ds(2 * b, 2)].reshape(2 * chans, coarse_ref.shape[2])
        piece = lax.dot_general(table, pair, (((1,), (1,)), ((), ())), preferred_element_type=F32)
        turned = pltpu.roll(piece, chans, 1)
        low_ref[2 * b] = piece
        high_ref[2 * b] = turned
        low_ref[2 * b + 1] = turned
        high_ref[2 * b + 1] = piece
        return 0

    lax.fori_loop(0, blocks // 2, pieces, 0, unroll=8)

    def step(d, _):
        first, second = low_ref[route_ref[0, d]], high_ref[route_ref[1, d]]
        out_ref[d] = jnp.where(upper, second, first).astype(BF)
        return 0

    lax.fori_loop(0, out_ref.shape[0], step, 0, unroll=8)


def pool_kernel(grad_ref, pooled_ref, up_ref, down_ref, rows_ref):
    height, width, chans = grad_ref.shape
    half = width // 2

    def step(r, _):
        rows_ref[...] = grad_ref[2 * r] + grad_ref[2 * r + 1]
        pooled_ref[r] = rows_ref[pl.ds(0, half, stride=2)] + rows_ref[pl.ds(1, half, stride=2)]
        return 0

    lax.fori_loop(0, height // 2, step, 0)
    up_ref[0:width] = grad_ref[0].astype(BF)
    up_ref[width : width + half] = pooled_ref[0].astype(BF)
    down_ref[0:width] = grad_ref[height - 1].astype(BF)
    down_ref[width : width + half] = pooled_ref[height // 2 - 1].astype(BF)


def head_back_kernel(pooled_ref, up_ref, down_ref, edge_ref, weights_ref, grad_ref, rows3, table):
    height, width, chans = pooled_ref.shape
    start = up_ref.shape[0] - width
    build_table(table, weights_ref, True)
    put_row(rows3, 0, up_ref[start:].astype(F32) * edge_ref[0:1])
    put_row(rows3, height + 1, down_ref[start:].astype(F32) * edge_ref[1:2])

    def emit(r, value, carry):
        grad_ref[r] = value
        return carry

    conv_pairs(rows3, table, height, lambda r: put_row(rows3, r, pooled_ref[r - 1]), emit, 0)


def hidden_kernel(route_ref, arrived_ref, noisy_ref, lift_ref, hid_ref, cond_ref, up_ref, down_ref,
                  block_ref, line_ref):
    height, width, chans = noisy_ref.shape
    region = arrived_ref.shape[1]
    per_row = width // region
    upper = lax.broadcasted_iota(jnp.int32, (region, chans), 1) >= chans // 2
    table = lift_ref[...]

    def step(r, sums):
        for i in range(per_row):
            k = r * per_row + i
            piece = arrived_ref[route_ref[3, k]].astype(F32)
            keep = upper == (route_ref[4, k] > 0)
            line_ref[i * region : (i + 1) * region] = jnp.where(keep, piece, 0.0)
        cond = line_ref[...].astype(BF)
        cond_ref[r] = cond
        hidden = noisy_ref[r].astype(F32) + jnp.dot(cond, table, preferred_element_type=F32)
        hid_ref[r] = hidden
        return add_sums(sums, hidden)

    sums = lax.fori_loop(0, height, step, zeros2(chans), unroll=7)
    send_raw(up_ref, down_ref, block_ref, hid_ref[0], hid_ref[height - 1], sums, width, height)


def norm_rows(x_ref, vec, up_ref, down_ref, edge_ref, rows3, act_ref):
    height, width, chans = x_ref.shape
    above, below = halo_raw(up_ref, down_ref, vec, width)
    above = act_of(above, vec) * edge_ref[0:1]
    below = act_of(below, vec) * edge_ref[1:2]
    put_row(rows3, 0, above)
    put_row(rows3, height + 1, below)
    if act_ref is not None:
        act_ref[0] = above.astype(BF)
        act_ref[height + 1] = below.astype(BF)

    def fill(r):
        value = act_of(x_ref[r - 1], vec)
        put_row(rows3, r, value)
        if act_ref is not None:
            act_ref[r] = value.astype(BF)

    return fill


def make_first(count, keep):
    def kernel(x_ref, up_ref, down_ref, opp_ref, own_ref, edge_ref, gain_ref, weights_ref,
               y_ref, *rest):
        act_ref = rest[0] if keep else None
        vec_ref, to_up, to_down, block_ref, rows3, table = rest[1:] if keep else rest
        height, width, chans = x_ref.shape
        vec = norm_vectors(up_ref, down_ref, opp_ref, own_ref, gain_ref, width, height, count)
        vec_ref[...] = vec
        build_table(table, weights_ref, False)
        fill = norm_rows(x_ref, vec, up_ref, down_ref, edge_ref, rows3, act_ref)

        def emit(r, value, sums):
            y_ref[r] = value
            return add_sums(sums, value)

        sums = conv_pairs(rows3, table, height, fill, emit, zeros2(chans))
        send_raw(to_up, to_down, block_ref, y_ref[0], y_ref[height - 1], sums, width, height)

    return kernel


def make_second(count):
    def kernel(y_ref, up_ref, down_ref, opp_ref, own_ref, edge_ref, gain_ref, weights_ref, hid_ref,
               level_ref, pooled_ref, vec_ref, to_up, to_down, block_ref, rows3, table,
               line_ref):
        height, width, chans = y_ref.shape
        half = width // 2
        vec = norm_vectors(up_ref, down_ref, opp_ref, own_ref, gain_ref, width, height, count)
        vec_ref[...] = vec
        build_table(table, weights_ref, False)
        fill = norm_rows(y_ref, vec, up_ref, down_ref, edge_ref, rows3, None)

        def emit(r, value, carry):
            one = hid_ref[r] + value
            level_ref[r] = one
            if carry[0] is None:
                return one, carry[1]
            line_ref[...] = carry[0] + one
            pooled = 0.25 * (line_ref[pl.ds(0, half, stride=2)] + line_ref[pl.ds(1, half, stride=2)])
            pooled_ref[r // 2] = pooled
            return None, add_sums(carry[1], pooled)

        sums = conv_pairs(rows3, table, height, fill, emit, (None, zeros2(chans)))[1]
        last = height // 2 - 1
        send_raw(to_up, to_down, block_ref, pooled_ref[0], pooled_ref[last], sums, half, height // 2)

    return kernel


def make_turn(count):
    def kernel(y_ref, up_ref, down_ref, opp_ref, own_ref, edge_ref, gain_ref, grad_ref,
               act_ref, vec_ref, to_up, to_down, block_ref):
        height, width, chans = y_ref.shape
        vec = norm_vectors(up_ref, down_ref, opp_ref, own_ref, gain_ref, width, height, count)
        vec_ref[...] = vec
        above, below = halo_raw(up_ref, down_ref, vec, width)
        act_ref[0] = (act_of(above, vec) * edge_ref[0:1]).astype(BF)
        act_ref[height + 1] = (act_of(below, vec) * edge_ref[1:2]).astype(BF)

        def fill(r, sums):
            x = y_ref[r]
            y = x * vec[2:3] + vec[3:4]
            sg = sigm(y)
            act_ref[r + 1] = (y * sg).astype(BF)
            gs = grad_ref[r] * sg * (1.0 + y * (1.0 - sg))
            return sums[0] + fold8(gs), sums[1] + fold8(gs * (x - vec[0:1]) * vec[1:2])

        sums = lax.fori_loop(0, height, fill, zeros2(chans))
        send_grad(to_up, to_down, block_ref, grad_ref[0], grad_ref[height - 1], sums, width)

    return kernel


def tail_kernel(act_ref, weights_ref, pooled_ref, level_ref, out_ref, rows3, table, line_ref):
    height, width, chans = pooled_ref.shape
    build_table(table, weights_ref, False)
    put_row(rows3, 0, act_ref[0].astype(F32))
    put_row(rows3, height + 1, act_ref[height + 1].astype(F32))

    def emit(r, value, carry):
        two = pooled_ref[r] + value
        line_ref[pl.ds(0, width, stride=2)] = two
        line_ref[pl.ds(1, width, stride=2)] = two
        wide = line_ref[...]
        out_ref[2 * r] = level_ref[2 * r] + wide
        out_ref[2 * r + 1] = level_ref[2 * r + 1] + wide
        return carry

    conv_pairs(rows3, table, height, lambda r: put_row(rows3, r, act_ref[r].astype(F32)), emit, 0)


def back_conv(rows3, table, fill, x_ref, vec, grad_ref, to_up, to_down, block_ref):
    height, width, chans = x_ref.shape

    def emit(r, value, sums):
        grad_ref[r] = value
        gs, normed = act_grad(value, x_ref[r], vec)
        return sums[0] + fold8(gs), sums[1] + fold8(gs * normed)

    sums = conv_pairs(rows3, table, height, fill, emit, zeros2(chans))
    send_grad(to_up, to_down, block_ref, grad_ref[0], grad_ref[height - 1], sums, width)


def make_back_mid(count):
    def kernel(ga_ref, y_ref, yup_ref, ydown_ref, vec_ref, gup_ref, gdown_ref, opp_ref, own_ref,
               edge_ref, weights_ref, x_ref, xvec_ref,
               g_ref, out_ref, to_up, to_down, block_ref, rows3, table):
        height, width, chans = y_ref.shape
        vec = vec_ref[...]
        first, second = back_vectors(gup_ref, gdown_ref, opp_ref, own_ref, vec, width, count)
        above, below = halo_raw(yup_ref, ydown_ref, vec, width)
        g_above = norm_grad(gup_ref[0:width].astype(F32), above, vec, first, second)
        g_below = norm_grad(gdown_ref[0:width].astype(F32), below, vec, first, second)
        put_row(rows3, 0, g_above * edge_ref[0:1])
        put_row(rows3, height + 1, g_below * edge_ref[1:2])

        def fill(r):
            value = norm_grad(ga_ref[r - 1], y_ref[r - 1], vec, first, second)
            put_row(rows3, r, value)
            g_ref[r - 1] = value.astype(BF)

        build_table(table, weights_ref, True)
        back_conv(rows3, table, fill, x_ref, xvec_ref[...], out_ref, to_up, to_down, block_ref)

    return kernel


def make_back_join(count):
    def kernel(ga_ref, p_ref, pup_ref, pdown_ref, pvec_ref, gup_ref, gdown_ref, opp_ref, own_ref,
               edge_ref, pg_ref, og_ref, oup_ref, odown_ref, weights_ref, x_ref, xvec_ref,
               g_ref, out_ref, to_up, to_down, block_ref, rows3, table, line_ref):
        half_height, half, chans = p_ref.shape
        height, width, _ = og_ref.shape
        vec = pvec_ref[...]
        first, second = back_vectors(gup_ref, gdown_ref, opp_ref, own_ref, vec, half, count)

        def widened(value):
            line_ref[pl.ds(0, half, stride=2)] = value
            line_ref[pl.ds(1, half, stride=2)] = value
            return 0.25 * line_ref[...]

        above, below = halo_raw(pup_ref, pdown_ref, vec, half)
        g_above = norm_grad(gup_ref[0:half].astype(F32), above, vec, first, second)
        g_below = norm_grad(gdown_ref[0:half].astype(F32), below, vec, first, second)
        wide = widened(g_above + oup_ref[width : width + half].astype(F32))
        put_row(rows3, 0, (oup_ref[0:width].astype(F32) + wide) * edge_ref[0:1])
        wide = widened(g_below + odown_ref[width : width + half].astype(F32))
        put_row(rows3, height + 1, (odown_ref[0:width].astype(F32) + wide) * edge_ref[1:2])

        def widen_row(r, _):
            value = pg_ref[r] + norm_grad(ga_ref[r], p_ref[r], vec, first, second)
            wide = widened(value)
            for i in range(2):
                g_ref[2 * r + i] = (og_ref[2 * r + i] + wide).astype(BF)
            return 0

        def fill(r):
            put_row(rows3, r, g_ref[r - 1].astype(F32))

        build_table(table, weights_ref, True)
        lax.fori_loop(0, half_height, widen_row, 0, unroll=True)
        back_conv(rows3, table, fill, x_ref, xvec_ref[...], out_ref, to_up, to_down, block_ref)

    return kernel


def taps_of(g_ref, rows3, acc_ref, out_ref):
    height, width, chans = g_ref.shape
    acc_ref[...] = jnp.zeros(acc_ref.shape, F32)

    def step(r, _):
        rhs = jnp.concatenate([rows3[r + s] for s in range(3)], axis=1)
        acc_ref[...] += lax.dot_general(
            g_ref[r], rhs, (((0,), (0,)), ((), ())), preferred_element_type=F32
        )
        return 0

    lax.fori_loop(0, height, step, 0, unroll=True)
    for tap in range(9):
        part = acc_ref[:, tap * chans : (tap + 1) * chans]
        out_ref[tap * chans : (tap + 1) * chans] = part.astype(out_ref.dtype)


def taps_act_kernel(g_ref, act_ref, out_ref, rows3, acc_ref):
    def fill(r, _):
        put_row(rows3, r, act_ref[r].astype(F32))
        return 0

    lax.fori_loop(0, g_ref.shape[0] + 2, fill, 0, unroll=True)
    taps_of(g_ref, rows3, acc_ref, out_ref)


def taps_raw_kernel(g_ref, x_ref, up_ref, down_ref, vec_ref, edge_ref, out_ref, rows3, acc_ref):
    fill = norm_rows(x_ref, vec_ref[...], up_ref, down_ref, edge_ref, rows3, None)

    def one(r, _):
        fill(r + 1)
        return 0

    lax.fori_loop(0, g_ref.shape[0], one, 0, unroll=True)
    taps_of(g_ref, rows3, acc_ref, out_ref)


def params_kernel(taps_a, taps_b, taps_c, taps_d, lift_ref, own_a, own_b, own_c, own_d, out_ref):
    start = 0
    for taps in (taps_a, taps_b, taps_c, taps_d):
        out_ref[start : start + taps.shape[0]] = taps[...]
        start += taps.shape[0]
    lift = lift_ref[...]
    chans, lanes = lift.shape
    lift = (lift + pltpu.roll(lift, lanes // 2, 1)).T[: lanes // 2]
    gains = [stat_pair(own[...])[1] for own in (own_a, own_b, own_c, own_d)]
    rows = jnp.concatenate([lift] + gains + [jnp.zeros((12, chans), F32)], axis=0)
    out_ref[start : start + rows.shape[0]] = rows.astype(BF)
    start += rows.shape[0]
    out_ref[start:] = jnp.zeros((out_ref.shape[0] - start, chans), BF)


def make_last(count):
    def kernel(route_ref, ga_ref, x_ref, vec_ref, gup_ref, gdown_ref, opp_ref, own_ref, level_ref,
               lift_ref, cond_ref, out_ref, lift_out, line_ref):
        height, width, chans = x_ref.shape
        region = out_ref.shape[1]
        per_row = width // region
        vec = vec_ref[...]
        first, second = back_vectors(gup_ref, gdown_ref, opp_ref, own_ref, vec, 0, count)
        upper = lax.broadcasted_iota(jnp.int32, (region, chans), 1) >= chans // 2
        table = lift_ref[...]
        lift_out[...] = jnp.zeros(lift_out.shape, F32)

        def clear(d, _):
            out_ref[d] = jnp.zeros((region, chans), BF)
            return 0

        lax.fori_loop(0, out_ref.shape[0], clear, 0, unroll=8)

        def step(r, _):
            grad = norm_grad(ga_ref[r], x_ref[r], vec, first, second)
            grad = (level_ref[r].astype(F32) + grad).astype(BF)
            lift_out[...] += lax.dot_general(
                grad, cond_ref[r], (((0,), (0,)), ((), ())), preferred_element_type=F32
            )
            line_ref[...] = jnp.dot(grad, table, preferred_element_type=F32)
            for i in range(per_row):
                k = r * per_row + i
                d = route_ref[3, k]
                piece = line_ref[i * region : (i + 1) * region]
                keep = upper == (route_ref[4, k] > 0)
                out_ref[d] = jnp.where(keep, piece, out_ref[d].astype(F32)).astype(BF)
            return 0

        lax.fori_loop(0, height, step, 0, unroll=7)

    return kernel


def make_owner(interp_at):
    def kernel(route_ref, arrived_ref, coarse_ref, interp_ref, known_ref, grad_ref, params_ref,
               low_ref, high_ref, interp_out, tail_ref, sem):
        owner_sums(route_ref, arrived_ref, coarse_ref, interp_ref, grad_ref, low_ref, high_ref,
                   interp_out)
        rows = interp_out.shape[0]
        pad = jnp.zeros((8, interp_out.shape[1]), F32)
        tail_ref[...] = jnp.concatenate([interp_out[...], pad], axis=0).astype(BF)
        target = params_ref.at[pl.ds(interp_at, rows + 8)]
        copy = pltpu.make_async_copy(tail_ref, target, sem)
        copy.start()
        copy.wait()

    return kernel


def owner_sums(route_ref, arrived_ref, coarse_ref, interp_ref, grad_ref, low_ref, high_ref,
               interp_out):
    tiles, region, lanes = arrived_ref.shape
    half = lanes // 2
    blocks = coarse_ref.shape[0]
    upper = lax.broadcasted_iota(jnp.int32, (region, lanes), 1) >= half

    def clear(b, _):
        low_ref[b] = jnp.zeros((region, lanes), F32)
        high_ref[b] = jnp.zeros((region, lanes), F32)
        return 0

    lax.fori_loop(0, blocks, clear, 0, unroll=8)

    def gather(d, _):
        piece = arrived_ref[d].astype(F32)
        count = route_ref[2, d]
        first, second = route_ref[0, d], route_ref[1, d]
        keep = jnp.logical_not(upper) & (count > 0)
        low_ref[first] += jnp.where(keep, piece, 0.0)
        keep = upper & (count > 1)
        high_ref[second] += jnp.where(keep, piece, 0.0)
        return 0

    lax.fori_loop(0, tiles, gather, 0, unroll=8)
    table = interp_ref[...]
    interp_out[...] = jnp.zeros(interp_out.shape, F32)

    def finish(b, _):
        one = low_ref[2 * b] + high_ref[2 * b]
        two = low_ref[2 * b + 1] + high_ref[2 * b + 1]
        one, two = one + pltpu.roll(one, half, 1), two + pltpu.roll(two, half, 1)
        total = jnp.where(upper, two, one).astype(BF)
        wide = lax.dot_general(total, table, (((0,), (0,)), ((), ())), preferred_element_type=F32)
        grad_ref[pl.ds(2 * b, 2)] = wide.reshape(2, half, wide.shape[1])
        pair = coarse_ref[pl.ds(2 * b, 2)].reshape(lanes, coarse_ref.shape[2])
        interp_out[...] += jnp.dot(total, pair, preferred_element_type=F32)
        return 0

    lax.fori_loop(0, blocks // 2, finish, 0, unroll=8)


def make_sum(scale):
    def kernel(parts_ref, out_ref):
        devices, rows, lanes = parts_ref.shape

        def add(d, total):
            return total + parts_ref[d].astype(F32)

        total = lax.fori_loop(0, devices, add, jnp.zeros((rows, lanes), F32), unroll=8)
        total = (total * scale).astype(BF)

        def put(d, _):
            out_ref[d] = total
            return 0

        lax.fori_loop(0, devices, put, 0, unroll=8)

    return kernel


def finish_kernel(rows_ref, *outs):
    start = 0
    for out in outs:
        count = out.shape[0]
        span = -(-count // 8) * 8
        step = 128 if count % 128 == 0 else span

        def move(i, _, start=start, out=out, step=step, count=count):
            part = rows_ref[pl.ds(pl.multiple_of(start + i * step, 8), step)].astype(F32)
            out[pl.ds(i * step, min(step, count))] = part[: min(step, count)]
            return 0

        lax.fori_loop(0, span // step, move, 0)
        start += span


def ring(x, shift):
    count = lax.axis_size("lat")
    return lax.ppermute(x, "lat", [(i, (i + shift) % count) for i in range(count)])


def exchange(to_up, to_down, block):
    return ring(to_down, 1), ring(to_up, -1), ring(block, 2), block


def both(first, second):
    return lax.optimization_barrier((first, second))


def body(coarse, slot_owner, slot_block, interp, lift, conv_weights, gains, fine_noisy, out_grad):
    devices = lax.axis_size(BOTH)
    lat_count = lax.axis_size("lat")
    lat = lax.axis_index("lat")
    me = lax.axis_index(BOTH).astype(jnp.int32).reshape(1)
    noisy = jnp.transpose(fine_noisy[0], (1, 2, 0))
    grad = jnp.transpose(out_grad[0], (1, 2, 0))
    height, width, chans = noisy.shape
    half_height, half = height // 2, width // 2
    slots = slot_owner.shape[1]
    blocks, coarse_chans, cells = coarse.shape
    region = interp.shape[1]
    full_count = float(chans // GROUPS * height * width * lat_count)
    half_count = full_count / 4

    edge = jnp.stack([lat > 0, lat < lat_count - 1]).astype(F32)
    edge = jnp.broadcast_to(edge[:, None], (2, chans))
    turned = jnp.transpose(conv_weights, (0, 1, 3, 2))
    forward = [turned[i] for i in range(4)]
    backward = [conv_weights[i] for i in range(4)]
    lift_rows = jnp.concatenate([lift.T, lift.T], axis=0)
    lift_cols = jnp.concatenate([lift, lift], axis=1)
    gain_rows = [gains[i : i + 1] for i in range(4)]

    full = (height, width, chans)
    small = (half_height, half, chans)
    table = ((SPAN * 3 * chans, 2 * chans), BF)
    full3 = [((height + 2, width, 3 * chans), BF), table]
    small3 = [((half_height + 2, half, 3 * chans), BF), table]
    line = ((width, chans), F32)
    vec_shape = ((8, chans), F32)
    small_act = ((half_height + 2, half, chans), BF)
    full_msg = [((width + STAT_ROWS, chans), BF)] * 2 + [((STAT_ROWS, chans), BF)]
    small_msg = [((half + STAT_ROWS, chans), BF)] * 2 + [((STAT_ROWS, chans), BF)]

    (route,) = call(
        route_kernel,
        [((8, devices), jnp.int32)],
        [],
        [me],
        [slot_owner[:, :, 0].T, slot_block.T],
        "route",
    )
    piece_shape = (region, 2 * coarse_chans)
    (outgoing,) = call(
        send_kernel, [((devices,) + piece_shape, BF)], [((blocks,) + piece_shape, F32)] * 2, [route],
        [coarse, interp.T], "send",
    )
    arrived = lax.all_to_all(outgoing, BOTH, split_axis=0, concat_axis=0, tiled=True)
    edge_msg = ((width + half, chans), BF)
    pooled_grad, edge_up, edge_down = call(
        pool_kernel, [(small, F32), edge_msg, edge_msg], [line], [], [grad], "pool_grad"
    )
    grad_above, grad_below = ring(edge_down, 1), ring(edge_up, -1)
    arrived, (pooled_grad, turned) = both(arrived, (pooled_grad, turned))

    hidden, cond, *msg = call(
        hidden_kernel, [(full, F32), (full, BF)] + full_msg, [line], [route],
        [arrived, noisy, lift_rows], "hidden",
    )
    msg_h = exchange(*msg)
    (act_grad_d,) = call(
        head_back_kernel, [(small, F32)], small3, [],
        [pooled_grad, grad_above, grad_below, edge, backward[3]], "back_d",
    )
    msg_h, act_grad_d = both(msg_h, act_grad_d)
    conv_a, vec_a, *msg = call(
        make_first(full_count, False), [(full, F32), vec_shape] + full_msg, full3, [],
        [hidden, *msg_h, edge, gain_rows[0], forward[0]], "conv_a",
    )
    msg_a = exchange(*msg)
    level, pooled, vec_b, *msg = call(
        make_second(full_count), [(full, F32), (small, F32), vec_shape] + small_msg,
        full3 + [line], [], [conv_a, *msg_a, edge, gain_rows[1], forward[1], hidden], "conv_b",
    )
    msg_p = exchange(*msg)
    conv_c, act_c, vec_c, *msg = call(
        make_first(half_count, True), [(small, F32), small_act, vec_shape] + small_msg, small3, [],
        [pooled, *msg_p, edge, gain_rows[2], forward[2]], "conv_c",
    )
    msg_c = exchange(*msg)
    act_d, vec_d, *msg = call(
        make_turn(half_count), [small_act, vec_shape] + small_msg, [], [],
        [conv_c, *msg_c, edge, gain_rows[3], act_grad_d], "turn_d",
    )
    back_d = exchange(*msg)

    acc = ((chans, 9 * chans), F32)
    taps_shape = [((9 * chans, chans), BF)]

    def taps_grad(g, act, name):
        return call(taps_act_kernel, taps_shape, [small3[0], acc], [], [g, act], name)[0]

    def taps_again(g, x, msg, vec, name):
        args = [g, x, msg[0], msg[1], vec, edge]
        return call(taps_raw_kernel, taps_shape, [full3[0], acc], [], args, name)[0]

    taps_d = taps_grad(pooled_grad.astype(BF), act_d, "taps_d")
    back_d, taps_d = both(back_d, taps_d)
    g_c, act_grad_c, *msg = call(
        make_back_mid(half_count), [(small, BF), (small, F32)] + small_msg, small3, [],
        [act_grad_d, conv_c, msg_c[0], msg_c[1], vec_d, *back_d, edge, backward[2], pooled, vec_c],
        "back_c",
    )
    back_c = exchange(*msg)
    taps_c = taps_grad(g_c, act_c, "taps_c")
    back_c, taps_c = both(back_c, taps_c)
    g_b, act_grad_b, *msg = call(
        make_back_join(half_count), [(full, BF), (full, F32)] + full_msg,
        full3 + [line], [],
        [act_grad_c, pooled, msg_p[0], msg_p[1], vec_c, *back_c, edge, pooled_grad, grad,
         grad_above, grad_below, backward[1], conv_a, vec_b],
        "back_b",
    )
    back_b = exchange(*msg)
    g_a, act_grad_a, *msg = call(
        make_back_mid(full_count), [(full, BF), (full, F32)] + full_msg, full3, [],
        [act_grad_b, conv_a, msg_a[0], msg_a[1], vec_b, *back_b, edge, backward[0], hidden, vec_a],
        "back_a",
    )
    block = msg[2]
    back_a = (ring(block, 1), ring(block, -1), ring(block, 2), block)
    placed, lift_term = call(
        make_last(full_count),
        [((devices, region, 2 * coarse_chans), BF), ((chans, 2 * coarse_chans), F32)], [line],
        [route],
        [act_grad_a, hidden, vec_a, *back_a, g_b, lift_cols, cond], "grad_pieces",
    )

    placed, (g_a, g_b, act_d) = both(placed, (g_a, g_b, act_d))
    returned = lax.all_to_all(placed, BOTH, split_axis=0, concat_axis=0, tiled=True)
    taps_b = taps_again(g_b, conv_a, msg_a, vec_b, "taps_b")
    taps_a = taps_again(g_a, hidden, msg_h, vec_a, "taps_a")
    chunk = 40
    conv_rows = 36 * chans
    interp_at = conv_rows + coarse_chans + 16
    params_shape = ((devices * chunk, chans), BF)
    (params,) = call(
        params_kernel, [params_shape], [], [],
        [taps_a, taps_b, taps_c, taps_d, lift_term, back_a[3], back_b[3], back_c[3], back_d[3]],
        "params",
    )
    returned, params = both(returned, params)
    coarse_grad, params = call(
        make_owner(interp_at), [((blocks, coarse_chans, cells), F32), params_shape],
        [((blocks,) + piece_shape, F32)] * 2 + [((region, cells), F32), ((region + 8, cells), BF)],
        [route], [returned, coarse, interp.T, params], "owner", {4: 1}, 1,
    )
    params, act_d = both(params, act_d)
    params = lax.all_to_all(
        params.reshape(devices, chunk, chans), BOTH, split_axis=0, concat_axis=0, tiled=True
    )
    (denoised,) = call(
        tail_kernel, [(full, F32)], small3 + [line], [], [act_d, forward[3], pooled, level], "conv_d"
    )
    scale = 1.0 / math.sqrt(height * width * devices)
    (copies,) = call(make_sum(scale), [((devices, chunk, chans), BF)], [], [], [params], "sums")
    everything = lax.all_to_all(copies, BOTH, split_axis=0, concat_axis=0, tiled=True)
    everything, denoised = both(everything, denoised)
    conv_total, lift_total, gain_total, interp_total = call(
        finish_kernel,
        [((conv_rows, chans), F32), ((coarse_chans, chans), F32), ((16, chans), F32),
         ((region, cells), F32)],
        [], [], [everything.reshape(devices * chunk, chans)], "finish",
    )
    conv_total = conv_total.reshape(4, 9, chans, chans)
    lift_total = lift_total.T
    gain_total = gain_total[:4]
    interp_total = interp_total.T
    return (
        jnp.transpose(denoised, (2, 0, 1))[None],
        coarse_grad,
        interp_total,
        lift_total,
        conv_total,
        gain_total,
    )


def solution(mesh):
    placed = (
        P(BOTH, None, None),
        P(),
        P(),
        P(),
        P(),
        P(),
        P(),
        P("patch", None, "lat", None),
        P("patch", None, "lat", None),
    )
    return jax.shard_map(
        body,
        mesh=mesh,
        in_specs=placed,
        out_specs=(
            P("patch", None, "lat", None),
            P(BOTH, None, None),
            P(),
            P(),
            P(),
            P(),
        ),
        check_vma=False,
    )
```

```python
import math

import jax
import jax.numpy as jnp
from jax import lax
from jax.experimental import pallas as pl
from jax.experimental.pallas import tpu as pltpu
from jax.sharding import PartitionSpec as P

GROUPS = 32
EPSILON = 1e-05
BF = jnp.bfloat16
F32 = jnp.float32
BOTH = ("lat", "patch")
VMEM_BYTES = 15 * 1024 * 1024
STAT_ROWS = 16
SPAN = 4


def call(kernel, outs, scratch, scalars, args, name, aliases={}, copies=0):
    smem = pl.BlockSpec(memory_space=pltpu.SMEM)
    vmem = pl.BlockSpec(memory_space=pltpu.VMEM)
    stay = pl.BlockSpec(memory_space=pl.ANY)
    taken = [i + len(scalars) in aliases for i in range(len(args))]
    return pl.pallas_call(
        kernel,
        out_shape=[jax.ShapeDtypeStruct(s, d) for s, d in outs],
        in_specs=[smem] * len(scalars) + [stay if t else vmem for t in taken],
        out_specs=[stay if i in aliases.values() else vmem for i in range(len(outs))],
        scratch_shapes=[pltpu.VMEM(s, d) for s, d in scratch]
        + [pltpu.SemaphoreType.DMA] * copies,
        compiler_params=pltpu.CompilerParams(vmem_limit_bytes=VMEM_BYTES),
        name=name,
        input_output_aliases=aliases,
    )(*scalars, *args)


def fold8(x):
    return jnp.sum(x.reshape(x.shape[0] // 8, 8, x.shape[1]), axis=0)


def group_sum(v):
    lane = lax.broadcasted_iota(jnp.int32, v.shape, 1)
    n = v.shape[1]
    v = v + jnp.where(lane % 2 == 0, pltpu.roll(v, n - 1, 1), pltpu.roll(v, 1, 1))
    return v + jnp.where(lane % 4 < 2, pltpu.roll(v, n - 2, 1), pltpu.roll(v, 2, 1))


def split3(v):
    hi = v.astype(BF).astype(F32)
    mid = (v - hi).astype(BF).astype(F32)
    return hi, mid, v - hi - mid


def stat_block(first, second):
    row = lax.broadcasted_iota(jnp.int32, (STAT_ROWS, first.shape[1]), 0)
    block = jnp.zeros(row.shape, F32)
    for i, part in enumerate(split3(first) + split3(second)):
        block = jnp.where(row == i, part, block)
    return block.astype(BF)


def stat_pair(block):
    f = block.astype(F32)
    return f[0:1] + f[1:2] + f[2:3], f[3:4] + f[4:5] + f[5:6]


def total_pair(blocks):
    pairs = [stat_pair(b) for b in blocks]
    return sum(p[0] for p in pairs), sum(p[1] for p in pairs)


def put_row(dst, index, value):
    width, chans = value.shape
    cell = lax.broadcasted_iota(jnp.int32, value.shape, 0)
    left = jnp.where(cell == 0, 0.0, pltpu.roll(value, 1, 0))
    right = jnp.where(cell == width - 1, 0.0, pltpu.roll(value, width - 1, 0))
    dst[index, :, 0:chans] = left.astype(BF)
    dst[index, :, chans : 2 * chans] = value.astype(BF)
    dst[index, :, 2 * chans : 3 * chans] = right.astype(BF)


def build_table(table, weights, flipped):
    chans = weights.shape[2]
    span = 3 * chans
    blank = jnp.zeros((span, chans), BF)
    table[0:span, chans : 2 * chans] = blank
    table[3 * span : 4 * span, 0:chans] = blank
    for tap in range(9):
        value = weights[8 - tap if flipped else tap]
        table[tap * chans : (tap + 1) * chans, 0:chans] = value
        table[span + tap * chans : span + (tap + 1) * chans, chans : 2 * chans] = value


def conv_pairs(rows3, table, height, fill, emit, carry):
    chans = table.shape[1] // 2

    def pair(j):
        lhs = jnp.concatenate([rows3[2 * j + s] for s in range(SPAN)], axis=1)
        return jnp.dot(lhs, table[...], preferred_element_type=F32)

    def both(j, out, carry):
        carry = emit(2 * j, out[:, :chans], carry)
        return emit(2 * j + 1, out[:, chans:], carry)

    mixed = (height - 3) // 2
    for r in range(1, 4):
        fill(r)
    for r in range(4 + 2 * mixed, height + 1):
        fill(r)

    def step(j, carry):
        out = pair(j)
        fill(2 * j + 4)
        fill(2 * j + 5)
        return both(j, out, carry)

    carry = lax.fori_loop(0, mixed, step, carry, unroll=True)
    for j in range(mixed, height // 2):
        carry = both(j, pair(j), carry)
    if height % 2:
        lhs = jnp.concatenate([rows3[height - 1 + s] for s in range(3)], axis=1)
        out = jnp.dot(lhs, table[0 : lhs.shape[1], 0:chans], preferred_element_type=F32)
        carry = emit(height - 1, out, carry)
    return carry


def sigm(y):
    return 0.5 * jnp.tanh(0.5 * y) + 0.5


def act_of(x, vec):
    y = x * vec[2:3] + vec[3:4]
    return y * sigm(y)


def act_grad(grad, x, vec):
    y = x * vec[2:3] + vec[3:4]
    sg = sigm(y)
    return grad * sg * (1.0 + y * (1.0 - sg)), (x - vec[0:1]) * vec[1:2]


def norm_vectors(up, down, opposite, own, gain, width, height, count):
    up_stats, down_stats = up[width : width + STAT_ROWS], down[width : width + STAT_ROWS]
    first, second = total_pair([own[...], up_stats, down_stats, opposite[...]])
    first = group_sum(jnp.broadcast_to(first, (8, first.shape[1])))
    second = group_sum(jnp.broadcast_to(second, first.shape))
    mean = first / count
    inv = lax.rsqrt(second / count - mean * mean + EPSILON)
    gain8 = jnp.broadcast_to(gain[...], mean.shape)
    scale = inv * gain8
    row = lax.broadcasted_iota(jnp.int32, mean.shape, 0)
    local = 1.0 / (width * height)
    up_mean = stat_pair(up_stats)[0] * local
    down_mean = stat_pair(down_stats)[0] * local
    vec = jnp.where(row == 0, mean, inv)
    for i, part in enumerate([scale, -mean * scale, gain8, up_mean, down_mean]):
        vec = jnp.where(row == i + 2, part, vec)
    return vec


def back_vectors(up, down, opposite, own, vec, width, count):
    stats = [own[...], opposite[...]]
    stats += [up[width : width + STAT_ROWS], down[width : width + STAT_ROWS]]
    first, second = total_pair(stats)
    first = group_sum(jnp.broadcast_to(first * vec[4:5], (8, first.shape[1])))
    second = group_sum(jnp.broadcast_to(second * vec[4:5], first.shape))
    inv = vec[1:2]
    slope = inv * inv * (second[0:1] / count)
    return inv * (first[0:1] / count) - vec[0:1] * slope, slope


def norm_grad(grad, x, vec, offset, slope):
    y = x * vec[2:3] + vec[3:4]
    sg = sigm(y)
    gs = grad * sg * (1.0 + y * (1.0 - sg))
    return gs * vec[2:3] - (x * slope + offset)


def send_raw(to_up, to_down, block, top, bottom, sums, width, height):
    first = jnp.sum(sums[0], axis=0, keepdims=True)
    second = jnp.sum(sums[1], axis=0, keepdims=True)
    stats = stat_block(first, second)
    mean = stat_pair(stats)[0] * (1.0 / (width * height))
    to_up[0:width] = (top - mean).astype(BF)
    to_down[0:width] = (bottom - mean).astype(BF)
    to_up[width : width + STAT_ROWS] = stats
    to_down[width : width + STAT_ROWS] = stats
    block[...] = stats


def send_grad(to_up, to_down, block, top, bottom, sums, width):
    stats = stat_block(
        jnp.sum(sums[0], axis=0, keepdims=True), jnp.sum(sums[1], axis=0, keepdims=True)
    )
    to_up[0:width] = top.astype(BF)
    to_down[0:width] = bottom.astype(BF)
    to_up[width : width + STAT_ROWS] = stats
    to_down[width : width + STAT_ROWS] = stats
    block[...] = stats


def halo_raw(up, down, vec, width):
    above = up[0:width].astype(F32) + vec[5:6]
    below = down[0:width].astype(F32) + vec[6:7]
    return above, below


def zeros2(chans):
    return jnp.zeros((8, chans), F32), jnp.zeros((8, chans), F32)


def add_sums(sums, x):
    return sums[0] + fold8(x), sums[1] + fold8(x * x)


def route_kernel(me_ref, owners_ref, blocks_ref, out_ref):
    me = me_ref[0]
    slots, tiles = owners_ref.shape
    owners = owners_ref[...]
    mine = owners == me
    k = lax.broadcasted_iota(jnp.int32, (slots, slots), 0)
    j = lax.broadcasted_iota(jnp.int32, (slots, slots), 1)
    earlier = jnp.where(j < k, 1.0, 0.0).astype(BF)
    flags = jnp.where(mine, 1.0, 0.0)
    before = jnp.dot(earlier, flags.astype(BF), preferred_element_type=F32)
    blocks = blocks_ref[...].astype(F32)
    first = jnp.sum(jnp.where(mine & (before < 0.5), blocks, 0.0), axis=0, keepdims=True)
    second = jnp.sum(jnp.where(mine & (before > 0.5), blocks, 0.0), axis=0, keepdims=True)
    count = jnp.sum(flags, axis=0, keepdims=True)
    lane = lax.broadcasted_iota(jnp.int32, (slots, tiles), 1)
    slot = lax.broadcasted_iota(jnp.int32, (slots, tiles), 0)
    column = jnp.sum(jnp.where(lane == me, owners, 0).astype(F32), axis=1, keepdims=True)
    as_row = jnp.sum(jnp.where(lane == slot, column, 0.0), axis=0, keepdims=True)
    same = (column == as_row) & (slot < lane) & (lane < slots)
    position = jnp.sum(jnp.where(same, 1.0, 0.0), axis=0, keepdims=True)
    row = lax.broadcasted_iota(jnp.int32, (8, tiles), 0)
    out = jnp.where(row == 0, first, 0.0)
    for i, part in enumerate([second, count, as_row, position]):
        out = jnp.where(row == i + 1, part, out)
    out_ref[...] = out.astype(jnp.int32)


def send_kernel(route_ref, coarse_ref, interp_ref, out_ref, low_ref, high_ref):
    table = interp_ref[...]
    region = table.shape[0]
    blocks, chans, _ = coarse_ref.shape
    upper = lax.broadcasted_iota(jnp.int32, (region, 2 * chans), 1) >= chans

    def pieces(b, _):
        pair = coarse_ref[pl.ds(2 * b, 2)].reshape(2 * chans, coarse_ref.shape[2])
        piece = lax.dot_general(table, pair, (((1,), (1,)), ((), ())), preferred_element_type=F32)
        turned = pltpu.roll(piece, chans, 1)
        low_ref[2 * b] = piece
        high_ref[2 * b] = turned
        low_ref[2 * b + 1] = turned
        high_ref[2 * b + 1] = piece
        return 0

    lax.fori_loop(0, blocks // 2, pieces, 0, unroll=8)

    def step(d, _):
        first, second = low_ref[route_ref[0, d]], high_ref[route_ref[1, d]]
        out_ref[d] = jnp.where(upper, second, first).astype(BF)
        return 0

    lax.fori_loop(0, out_ref.shape[0], step, 0, unroll=8)


def pool_kernel(grad_ref, pooled_ref, up_ref, down_ref, rows_ref):
    height, width, chans = grad_ref.shape
    half = width // 2

    def step(r, _):
        rows_ref[...] = grad_ref[2 * r] + grad_ref[2 * r + 1]
        pooled_ref[r] = rows_ref[pl.ds(0, half, stride=2)] + rows_ref[pl.ds(1, half, stride=2)]
        return 0

    lax.fori_loop(0, height // 2, step, 0)
    up_ref[0:width] = grad_ref[0].astype(BF)
    up_ref[width : width + half] = pooled_ref[0].astype(BF)
    down_ref[0:width] = grad_ref[height - 1].astype(BF)
    down_ref[width : width + half] = pooled_ref[height // 2 - 1].astype(BF)


def head_back_kernel(pooled_ref, up_ref, down_ref, edge_ref, weights_ref, grad_ref, rows3, table):
    height, width, chans = pooled_ref.shape
    start = up_ref.shape[0] - width
    build_table(table, weights_ref, True)
    put_row(rows3, 0, up_ref[start:].astype(F32) * edge_ref[0:1])
    put_row(rows3, height + 1, down_ref[start:].astype(F32) * edge_ref[1:2])

    def emit(r, value, carry):
        grad_ref[r] = value
        return carry

    conv_pairs(rows3, table, height, lambda r: put_row(rows3, r, pooled_ref[r - 1]), emit, 0)


def hidden_kernel(route_ref, arrived_ref, noisy_ref, lift_ref, hid_ref, cond_ref, up_ref, down_ref,
                  block_ref, line_ref):
    height, width, chans = noisy_ref.shape
    region = arrived_ref.shape[1]
    per_row = width // region
    upper = lax.broadcasted_iota(jnp.int32, (region, chans), 1) >= chans // 2
    table = lift_ref[...]

    def step(r, sums):
        for i in range(per_row):
            k = r * per_row + i
            piece = arrived_ref[route_ref[3, k]].astype(F32)
            keep = upper == (route_ref[4, k] > 0)
            line_ref[i * region : (i + 1) * region] = jnp.where(keep, piece, 0.0)
        cond = line_ref[...].astype(BF)
        cond_ref[r] = cond
        hidden = noisy_ref[r].astype(F32) + jnp.dot(cond, table, preferred_element_type=F32)
        hid_ref[r] = hidden
        return add_sums(sums, hidden)

    sums = lax.fori_loop(0, height, step, zeros2(chans), unroll=7)
    send_raw(up_ref, down_ref, block_ref, hid_ref[0], hid_ref[height - 1], sums, width, height)


def norm_rows(x_ref, vec, up_ref, down_ref, edge_ref, rows3, act_ref):
    height, width, chans = x_ref.shape
    above, below = halo_raw(up_ref, down_ref, vec, width)
    above = act_of(above, vec) * edge_ref[0:1]
    below = act_of(below, vec) * edge_ref[1:2]
    put_row(rows3, 0, above)
    put_row(rows3, height + 1, below)
    if act_ref is not None:
        act_ref[0] = above.astype(BF)
        act_ref[height + 1] = below.astype(BF)

    def fill(r):
        value = act_of(x_ref[r - 1], vec)
        put_row(rows3, r, value)
        if act_ref is not None:
            act_ref[r] = value.astype(BF)

    return fill


def make_first(count, keep):
    def kernel(x_ref, up_ref, down_ref, opp_ref, own_ref, edge_ref, gain_ref, weights_ref,
               y_ref, *rest):
        act_ref = rest[0] if keep else None
        vec_ref, to_up, to_down, block_ref, rows3, table = rest[1:] if keep else rest
        height, width, chans = x_ref.shape
        vec = norm_vectors(up_ref, down_ref, opp_ref, own_ref, gain_ref, width, height, count)
        vec_ref[...] = vec
        build_table(table, weights_ref, False)
        fill = norm_rows(x_ref, vec, up_ref, down_ref, edge_ref, rows3, act_ref)

        def emit(r, value, sums):
            y_ref[r] = value
            return add_sums(sums, value)

        sums = conv_pairs(rows3, table, height, fill, emit, zeros2(chans))
        send_raw(to_up, to_down, block_ref, y_ref[0], y_ref[height - 1], sums, width, height)

    return kernel


def make_second(count):
    def kernel(y_ref, up_ref, down_ref, opp_ref, own_ref, edge_ref, gain_ref, weights_ref, hid_ref,
               level_ref, pooled_ref, vec_ref, to_up, to_down, block_ref, rows3, table,
               line_ref):
        height, width, chans = y_ref.shape
        half = width // 2
        vec = norm_vectors(up_ref, down_ref, opp_ref, own_ref, gain_ref, width, height, count)
        vec_ref[...] = vec
        build_table(table, weights_ref, False)
        fill = norm_rows(y_ref, vec, up_ref, down_ref, edge_ref, rows3, None)

        def emit(r, value, carry):
            one = hid_ref[r] + value
            level_ref[r] = one
            if carry[0] is None:
                return one, carry[1]
            line_ref[...] = carry[0] + one
            pooled = 0.25 * (line_ref[pl.ds(0, half, stride=2)] + line_ref[pl.ds(1, half, stride=2)])
            pooled_ref[r // 2] = pooled
            return None, add_sums(carry[1], pooled)

        sums = conv_pairs(rows3, table, height, fill, emit, (None, zeros2(chans)))[1]
        last = height // 2 - 1
        send_raw(to_up, to_down, block_ref, pooled_ref[0], pooled_ref[last], sums, half, height // 2)

    return kernel


def make_turn(count):
    def kernel(y_ref, up_ref, down_ref, opp_ref, own_ref, edge_ref, gain_ref, grad_ref,
               act_ref, vec_ref, to_up, to_down, block_ref):
        height, width, chans = y_ref.shape
        vec = norm_vectors(up_ref, down_ref, opp_ref, own_ref, gain_ref, width, height, count)
        vec_ref[...] = vec
        above, below = halo_raw(up_ref, down_ref, vec, width)
        act_ref[0] = (act_of(above, vec) * edge_ref[0:1]).astype(BF)
        act_ref[height + 1] = (act_of(below, vec) * edge_ref[1:2]).astype(BF)

        def fill(r, sums):
            x = y_ref[r]
            y = x * vec[2:3] + vec[3:4]
            sg = sigm(y)
            act_ref[r + 1] = (y * sg).astype(BF)
            gs = grad_ref[r] * sg * (1.0 + y * (1.0 - sg))
            return sums[0] + fold8(gs), sums[1] + fold8(gs * (x - vec[0:1]) * vec[1:2])

        sums = lax.fori_loop(0, height, fill, zeros2(chans))
        send_grad(to_up, to_down, block_ref, grad_ref[0], grad_ref[height - 1], sums, width)

    return kernel


def tail_kernel(act_ref, weights_ref, pooled_ref, level_ref, out_ref, rows3, table, line_ref):
    height, width, chans = pooled_ref.shape
    build_table(table, weights_ref, False)
    put_row(rows3, 0, act_ref[0].astype(F32))
    put_row(rows3, height + 1, act_ref[height + 1].astype(F32))

    def emit(r, value, carry):
        two = pooled_ref[r] + value
        line_ref[pl.ds(0, width, stride=2)] = two
        line_ref[pl.ds(1, width, stride=2)] = two
        wide = line_ref[...]
        out_ref[2 * r] = level_ref[2 * r] + wide
        out_ref[2 * r + 1] = level_ref[2 * r + 1] + wide
        return carry

    conv_pairs(rows3, table, height, lambda r: put_row(rows3, r, act_ref[r].astype(F32)), emit, 0)


def back_conv(rows3, table, fill, x_ref, vec, grad_ref, to_up, to_down, block_ref):
    height, width, chans = x_ref.shape

    def emit(r, value, sums):
        grad_ref[r] = value.astype(grad_ref.dtype)
        gs, normed = act_grad(value, x_ref[r], vec)
        return sums[0] + fold8(gs), sums[1] + fold8(gs * normed)

    sums = conv_pairs(rows3, table, height, fill, emit, zeros2(chans))
    send_grad(to_up, to_down, block_ref, grad_ref[0], grad_ref[height - 1], sums, width)


def make_back_mid(count):
    def kernel(ga_ref, y_ref, yup_ref, ydown_ref, vec_ref, gup_ref, gdown_ref, opp_ref, own_ref,
               edge_ref, weights_ref, x_ref, xvec_ref,
               g_ref, out_ref, to_up, to_down, block_ref, rows3, table):
        height, width, chans = y_ref.shape
        vec = vec_ref[...]
        first, second = back_vectors(gup_ref, gdown_ref, opp_ref, own_ref, vec, width, count)
        above, below = halo_raw(yup_ref, ydown_ref, vec, width)
        g_above = norm_grad(gup_ref[0:width].astype(F32), above, vec, first, second)
        g_below = norm_grad(gdown_ref[0:width].astype(F32), below, vec, first, second)
        put_row(rows3, 0, g_above * edge_ref[0:1])
        put_row(rows3, height + 1, g_below * edge_ref[1:2])

        def fill(r):
            value = norm_grad(ga_ref[r - 1].astype(F32), y_ref[r - 1], vec, first, second)
            put_row(rows3, r, value)
            g_ref[r - 1] = value.astype(BF)

        build_table(table, weights_ref, True)
        back_conv(rows3, table, fill, x_ref, xvec_ref[...], out_ref, to_up, to_down, block_ref)

    return kernel


def make_back_join(count):
    def kernel(ga_ref, p_ref, pup_ref, pdown_ref, pvec_ref, gup_ref, gdown_ref, opp_ref, own_ref,
               edge_ref, pg_ref, og_ref, oup_ref, odown_ref, weights_ref, x_ref, xvec_ref,
               g_ref, out_ref, to_up, to_down, block_ref, rows3, table, line_ref):
        half_height, half, chans = p_ref.shape
        height, width, _ = og_ref.shape
        vec = pvec_ref[...]
        first, second = back_vectors(gup_ref, gdown_ref, opp_ref, own_ref, vec, half, count)

        def widened(value):
            line_ref[pl.ds(0, half, stride=2)] = value
            line_ref[pl.ds(1, half, stride=2)] = value
            return 0.25 * line_ref[...]

        above, below = halo_raw(pup_ref, pdown_ref, vec, half)
        g_above = norm_grad(gup_ref[0:half].astype(F32), above, vec, first, second)
        g_below = norm_grad(gdown_ref[0:half].astype(F32), below, vec, first, second)
        wide = widened(g_above + oup_ref[width : width + half].astype(F32))
        put_row(rows3, 0, (oup_ref[0:width].astype(F32) + wide) * edge_ref[0:1])
        wide = widened(g_below + odown_ref[width : width + half].astype(F32))
        put_row(rows3, height + 1, (odown_ref[0:width].astype(F32) + wide) * edge_ref[1:2])

        def widen_row(r, _):
            value = pg_ref[r] + norm_grad(ga_ref[r], p_ref[r], vec, first, second)
            wide = widened(value)
            for i in range(2):
                g_ref[2 * r + i] = (og_ref[2 * r + i] + wide).astype(BF)
            return 0

        def fill(r):
            put_row(rows3, r, g_ref[r - 1].astype(F32))

        build_table(table, weights_ref, True)
        lax.fori_loop(0, half_height, widen_row, 0, unroll=True)
        back_conv(rows3, table, fill, x_ref, xvec_ref[...], out_ref, to_up, to_down, block_ref)

    return kernel


def taps_of(g_ref, rows3, acc_ref, out_ref):
    height, width, chans = g_ref.shape
    acc_ref[...] = jnp.zeros(acc_ref.shape, F32)

    def step(r, _):
        rhs = jnp.concatenate([rows3[r + s] for s in range(3)], axis=1)
        acc_ref[...] += lax.dot_general(
            g_ref[r], rhs, (((0,), (0,)), ((), ())), preferred_element_type=F32
        )
        return 0

    lax.fori_loop(0, height, step, 0, unroll=True)
    for tap in range(9):
        part = acc_ref[:, tap * chans : (tap + 1) * chans]
        out_ref[tap * chans : (tap + 1) * chans] = part.astype(out_ref.dtype)


def taps_act_kernel(g_ref, act_ref, out_ref, rows3, acc_ref):
    def fill(r, _):
        put_row(rows3, r, act_ref[r].astype(F32))
        return 0

    lax.fori_loop(0, g_ref.shape[0] + 2, fill, 0, unroll=True)
    taps_of(g_ref, rows3, acc_ref, out_ref)


def taps_raw_kernel(g_ref, x_ref, up_ref, down_ref, vec_ref, edge_ref, out_ref, rows3, acc_ref):
    fill = norm_rows(x_ref, vec_ref[...], up_ref, down_ref, edge_ref, rows3, None)

    def one(r, _):
        fill(r + 1)
        return 0

    lax.fori_loop(0, g_ref.shape[0], one, 0, unroll=True)
    taps_of(g_ref, rows3, acc_ref, out_ref)


def params_kernel(taps_a, taps_b, taps_c, taps_d, lift_ref, own_a, own_b, own_c, own_d, out_ref):
    start = 0
    for taps in (taps_a, taps_b, taps_c, taps_d):
        out_ref[start : start + taps.shape[0]] = taps[...]
        start += taps.shape[0]
    lift = lift_ref[...]
    chans, lanes = lift.shape
    lift = (lift + pltpu.roll(lift, lanes // 2, 1)).T[: lanes // 2]
    gains = [stat_pair(own[...])[1] for own in (own_a, own_b, own_c, own_d)]
    rows = jnp.concatenate([lift] + gains + [jnp.zeros((12, chans), F32)], axis=0)
    out_ref[start : start + rows.shape[0]] = rows.astype(BF)
    start += rows.shape[0]
    out_ref[start:] = jnp.zeros((out_ref.shape[0] - start, chans), BF)


def make_last(count):
    def kernel(route_ref, ga_ref, x_ref, vec_ref, gup_ref, gdown_ref, opp_ref, own_ref, level_ref,
               lift_ref, cond_ref, out_ref, lift_out, line_ref):
        height, width, chans = x_ref.shape
        region = out_ref.shape[1]
        per_row = width // region
        vec = vec_ref[...]
        first, second = back_vectors(gup_ref, gdown_ref, opp_ref, own_ref, vec, 0, count)
        upper = lax.broadcasted_iota(jnp.int32, (region, chans), 1) >= chans // 2
        table = lift_ref[...]
        lift_out[...] = jnp.zeros(lift_out.shape, F32)

        def clear(d, _):
            out_ref[d] = jnp.zeros((region, chans), BF)
            return 0

        lax.fori_loop(0, out_ref.shape[0], clear, 0, unroll=8)

        def step(r, _):
            grad = norm_grad(ga_ref[r].astype(F32), x_ref[r], vec, first, second)
            grad = (level_ref[r].astype(F32) + grad).astype(BF)
            lift_out[...] += lax.dot_general(
                grad, cond_ref[r], (((0,), (0,)), ((), ())), preferred_element_type=F32
            )
            line_ref[...] = jnp.dot(grad, table, preferred_element_type=F32)
            for i in range(per_row):
                k = r * per_row + i
                d = route_ref[3, k]
                piece = line_ref[i * region : (i + 1) * region]
                keep = upper == (route_ref[4, k] > 0)
                out_ref[d] = jnp.where(keep, piece, out_ref[d].astype(F32)).astype(BF)
            return 0

        lax.fori_loop(0, height, step, 0, unroll=7)

    return kernel


def make_owner(interp_at):
    def kernel(route_ref, arrived_ref, coarse_ref, interp_ref, known_ref, grad_ref, params_ref,
               low_ref, high_ref, interp_out, tail_ref, sem):
        owner_sums(route_ref, arrived_ref, coarse_ref, interp_ref, grad_ref, low_ref, high_ref,
                   interp_out)
        rows = interp_out.shape[0]
        pad = jnp.zeros((8, interp_out.shape[1]), F32)
        tail_ref[...] = jnp.concatenate([interp_out[...], pad], axis=0).astype(BF)
        target = params_ref.at[pl.ds(interp_at, rows + 8)]
        copy = pltpu.make_async_copy(tail_ref, target, sem)
        copy.start()
        copy.wait()

    return kernel


def owner_sums(route_ref, arrived_ref, coarse_ref, interp_ref, grad_ref, low_ref, high_ref,
               interp_out):
    tiles, region, lanes = arrived_ref.shape
    half = lanes // 2
    blocks = coarse_ref.shape[0]
    upper = lax.broadcasted_iota(jnp.int32, (region, lanes), 1) >= half

    def clear(b, _):
        low_ref[b] = jnp.zeros((region, lanes), F32)
        high_ref[b] = jnp.zeros((region, lanes), F32)
        return 0

    lax.fori_loop(0, blocks, clear, 0, unroll=8)

    def gather(d, _):
        piece = arrived_ref[d].astype(F32)
        count = route_ref[2, d]
        first, second = route_ref[0, d], route_ref[1, d]
        keep = jnp.logical_not(upper) & (count > 0)
        low_ref[first] += jnp.where(keep, piece, 0.0)
        keep = upper & (count > 1)
        high_ref[second] += jnp.where(keep, piece, 0.0)
        return 0

    lax.fori_loop(0, tiles, gather, 0, unroll=8)
    table = interp_ref[...]
    interp_out[...] = jnp.zeros(interp_out.shape, F32)

    def finish(b, _):
        one = low_ref[2 * b] + high_ref[2 * b]
        two = low_ref[2 * b + 1] + high_ref[2 * b + 1]
        one, two = one + pltpu.roll(one, half, 1), two + pltpu.roll(two, half, 1)
        total = jnp.where(upper, two, one).astype(BF)
        wide = lax.dot_general(total, table, (((0,), (0,)), ((), ())), preferred_element_type=F32)
        grad_ref[pl.ds(2 * b, 2)] = wide.reshape(2, half, wide.shape[1])
        pair = coarse_ref[pl.ds(2 * b, 2)].reshape(lanes, coarse_ref.shape[2])
        interp_out[...] += jnp.dot(total, pair, preferred_element_type=F32)
        return 0

    lax.fori_loop(0, blocks // 2, finish, 0, unroll=8)


def make_sum(scale):
    def kernel(parts_ref, out_ref):
        devices, rows, lanes = parts_ref.shape

        def add(d, total):
            return total + parts_ref[d].astype(F32)

        total = lax.fori_loop(0, devices, add, jnp.zeros((rows, lanes), F32), unroll=8)
        total = (total * scale).astype(BF)

        def put(d, _):
            out_ref[d] = total
            return 0

        lax.fori_loop(0, devices, put, 0, unroll=8)

    return kernel


def finish_kernel(rows_ref, *outs):
    start = 0
    for out in outs:
        count = out.shape[0]
        span = -(-count // 8) * 8
        step = 128 if count % 128 == 0 else span

        def move(i, _, start=start, out=out, step=step, count=count):
            part = rows_ref[pl.ds(pl.multiple_of(start + i * step, 8), step)].astype(F32)
            out[pl.ds(i * step, min(step, count))] = part[: min(step, count)]
            return 0

        lax.fori_loop(0, span // step, move, 0)
        start += span


def ring(x, shift):
    count = lax.axis_size("lat")
    return lax.ppermute(x, "lat", [(i, (i + shift) % count) for i in range(count)])


def exchange(to_up, to_down, block):
    return ring(to_down, 1), ring(to_up, -1), ring(block, 2), block


def both(first, second):
    return lax.optimization_barrier((first, second))


def body(coarse, slot_owner, slot_block, interp, lift, conv_weights, gains, fine_noisy, out_grad):
    devices = lax.axis_size(BOTH)
    lat_count = lax.axis_size("lat")
    lat = lax.axis_index("lat")
    me = lax.axis_index(BOTH).astype(jnp.int32).reshape(1)
    noisy = jnp.transpose(fine_noisy[0], (1, 2, 0))
    grad = jnp.transpose(out_grad[0], (1, 2, 0))
    height, width, chans = noisy.shape
    half_height, half = height // 2, width // 2
    slots = slot_owner.shape[1]
    blocks, coarse_chans, cells = coarse.shape
    region = interp.shape[1]
    full_count = float(chans // GROUPS * height * width * lat_count)
    half_count = full_count / 4

    edge = jnp.stack([lat > 0, lat < lat_count - 1]).astype(F32)
    edge = jnp.broadcast_to(edge[:, None], (2, chans))
    turned = jnp.transpose(conv_weights, (0, 1, 3, 2))
    forward = [turned[i] for i in range(4)]
    backward = [conv_weights[i] for i in range(4)]
    lift_rows = jnp.concatenate([lift.T, lift.T], axis=0)
    lift_cols = jnp.concatenate([lift, lift], axis=1)
    gain_rows = [gains[i : i + 1] for i in range(4)]

    full = (height, width, chans)
    small = (half_height, half, chans)
    table = ((SPAN * 3 * chans, 2 * chans), BF)
    full3 = [((height + 2, width, 3 * chans), BF), table]
    small3 = [((half_height + 2, half, 3 * chans), BF), table]
    line = ((width, chans), F32)
    vec_shape = ((8, chans), F32)
    small_act = ((half_height + 2, half, chans), BF)
    full_msg = [((width + STAT_ROWS, chans), BF)] * 2 + [((STAT_ROWS, chans), BF)]
    small_msg = [((half + STAT_ROWS, chans), BF)] * 2 + [((STAT_ROWS, chans), BF)]

    (route,) = call(
        route_kernel,
        [((8, devices), jnp.int32)],
        [],
        [me],
        [slot_owner[:, :, 0].T, slot_block.T],
        "route",
    )
    piece_shape = (region, 2 * coarse_chans)
    (outgoing,) = call(
        send_kernel, [((devices,) + piece_shape, BF)], [((blocks,) + piece_shape, F32)] * 2, [route],
        [coarse, interp.T], "send",
    )
    arrived = lax.all_to_all(outgoing, BOTH, split_axis=0, concat_axis=0, tiled=True)
    edge_msg = ((width + half, chans), BF)
    pooled_grad, edge_up, edge_down = call(
        pool_kernel, [(small, F32), edge_msg, edge_msg], [line], [], [grad], "pool_grad"
    )
    grad_above, grad_below = ring(edge_down, 1), ring(edge_up, -1)
    arrived, (pooled_grad, turned) = both(arrived, (pooled_grad, turned))

    hidden, cond, *msg = call(
        hidden_kernel, [(full, F32), (full, BF)] + full_msg, [line], [route],
        [arrived, noisy, lift_rows], "hidden",
    )
    msg_h = exchange(*msg)
    (act_grad_d,) = call(
        head_back_kernel, [(small, F32)], small3, [],
        [pooled_grad, grad_above, grad_below, edge, backward[3]], "back_d",
    )
    msg_h, act_grad_d = both(msg_h, act_grad_d)
    conv_a, vec_a, *msg = call(
        make_first(full_count, False), [(full, F32), vec_shape] + full_msg, full3, [],
        [hidden, *msg_h, edge, gain_rows[0], forward[0]], "conv_a",
    )
    msg_a = exchange(*msg)
    level, pooled, vec_b, *msg = call(
        make_second(full_count), [(full, F32), (small, F32), vec_shape] + small_msg,
        full3 + [line], [], [conv_a, *msg_a, edge, gain_rows[1], forward[1], hidden], "conv_b",
    )
    msg_p = exchange(*msg)
    conv_c, act_c, vec_c, *msg = call(
        make_first(half_count, True), [(small, F32), small_act, vec_shape] + small_msg, small3, [],
        [pooled, *msg_p, edge, gain_rows[2], forward[2]], "conv_c",
    )
    msg_c = exchange(*msg)
    act_d, vec_d, *msg = call(
        make_turn(half_count), [small_act, vec_shape] + small_msg, [], [],
        [conv_c, *msg_c, edge, gain_rows[3], act_grad_d], "turn_d",
    )
    back_d = exchange(*msg)

    acc = ((chans, 9 * chans), F32)
    taps_shape = [((9 * chans, chans), BF)]

    def taps_grad(g, act, name):
        return call(taps_act_kernel, taps_shape, [small3[0], acc], [], [g, act], name)[0]

    def taps_again(g, x, msg, vec, name):
        args = [g, x, msg[0], msg[1], vec, edge]
        return call(taps_raw_kernel, taps_shape, [full3[0], acc], [], args, name)[0]

    taps_d = taps_grad(pooled_grad.astype(BF), act_d, "taps_d")
    back_d, taps_d = both(back_d, taps_d)
    g_c, act_grad_c, *msg = call(
        make_back_mid(half_count), [(small, BF), (small, F32)] + small_msg, small3, [],
        [act_grad_d, conv_c, msg_c[0], msg_c[1], vec_d, *back_d, edge, backward[2], pooled, vec_c],
        "back_c",
    )
    back_c = exchange(*msg)
    taps_c = taps_grad(g_c, act_c, "taps_c")
    back_c, taps_c = both(back_c, taps_c)
    g_b, act_grad_b, *msg = call(
        make_back_join(half_count), [(full, BF), (full, BF)] + full_msg,
        full3 + [line], [],
        [act_grad_c, pooled, msg_p[0], msg_p[1], vec_c, *back_c, edge, pooled_grad, grad,
         grad_above, grad_below, backward[1], conv_a, vec_b],
        "back_b",
    )
    back_b = exchange(*msg)
    g_a, act_grad_a, *msg = call(
        make_back_mid(full_count), [(full, BF), (full, BF)] + full_msg, full3, [],
        [act_grad_b, conv_a, msg_a[0], msg_a[1], vec_b, *back_b, edge, backward[0], hidden, vec_a],
        "back_a",
    )
    block = msg[2]
    back_a = (ring(block, 1), ring(block, -1), ring(block, 2), block)
    placed, lift_term = call(
        make_last(full_count),
        [((devices, region, 2 * coarse_chans), BF), ((chans, 2 * coarse_chans), F32)], [line],
        [route],
        [act_grad_a, hidden, vec_a, *back_a, g_b, lift_cols, cond], "grad_pieces",
    )

    placed, (g_a, g_b, act_d) = both(placed, (g_a, g_b, act_d))
    returned = lax.all_to_all(placed, BOTH, split_axis=0, concat_axis=0, tiled=True)
    taps_b = taps_again(g_b, conv_a, msg_a, vec_b, "taps_b")
    taps_a = taps_again(g_a, hidden, msg_h, vec_a, "taps_a")
    chunk = 40
    conv_rows = 36 * chans
    interp_at = conv_rows + coarse_chans + 16
    params_shape = ((devices * chunk, chans), BF)
    (params,) = call(
        params_kernel, [params_shape], [], [],
        [taps_a, taps_b, taps_c, taps_d, lift_term, back_a[3], back_b[3], back_c[3], back_d[3]],
        "params",
    )
    returned, params = both(returned, params)
    coarse_grad, params = call(
        make_owner(interp_at), [((blocks, coarse_chans, cells), F32), params_shape],
        [((blocks,) + piece_shape, F32)] * 2 + [((region, cells), F32), ((region + 8, cells), BF)],
        [route], [returned, coarse, interp.T, params], "owner", {4: 1}, 1,
    )
    params, act_d = both(params, act_d)
    params = lax.all_to_all(
        params.reshape(devices, chunk, chans), BOTH, split_axis=0, concat_axis=0, tiled=True
    )
    (denoised,) = call(
        tail_kernel, [(full, F32)], small3 + [line], [], [act_d, forward[3], pooled, level], "conv_d"
    )
    scale = 1.0 / math.sqrt(height * width * devices)
    (copies,) = call(make_sum(scale), [((devices, chunk, chans), BF)], [], [], [params], "sums")
    everything = lax.all_to_all(copies, BOTH, split_axis=0, concat_axis=0, tiled=True)
    everything, denoised = both(everything, denoised)
    conv_total, lift_total, gain_total, interp_total = call(
        finish_kernel,
        [((conv_rows, chans), F32), ((coarse_chans, chans), F32), ((16, chans), F32),
         ((region, cells), F32)],
        [], [], [everything.reshape(devices * chunk, chans)], "finish",
    )
    conv_total = conv_total.reshape(4, 9, chans, chans)
    lift_total = lift_total.T
    gain_total = gain_total[:4]
    interp_total = interp_total.T
    return (
        jnp.transpose(denoised, (2, 0, 1))[None],
        coarse_grad,
        interp_total,
        lift_total,
        conv_total,
        gain_total,
    )


def solution(mesh):
    placed = (
        P(BOTH, None, None),
        P(),
        P(),
        P(),
        P(),
        P(),
        P(),
        P("patch", None, "lat", None),
        P("patch", None, "lat", None),
    )
    return jax.shard_map(
        body,
        mesh=mesh,
        in_specs=placed,
        out_specs=(
            P("patch", None, "lat", None),
            P(BOTH, None, None),
            P(),
            P(),
            P(),
            P(),
        ),
        check_vma=False,
    )
```
